32 devices in a mesh: dp: 2 (over y), expert: 16 (over z, x, core).
Axes of the slice: x: 2, y: 2, z: 4, core: 2. Of those that a mesh axis runs over, the one named last changes fastest.
Arguments:
- tokens: bfloat16 [3584, 1024], P(('dp', 'expert')), parts along dimension 0, may hold values from -6 to 6
- expert_ids: int32 [3584, 8], P(('dp', 'expert')), parts along dimension 0, may hold values from 0 to 15, all different within a row; in each aligned block of 112 rows (0 to 111, 112 to 223, ...) at most 112 rows name the same one
- gate_probs: float32 [3584, 8], P(('dp', 'expert')), parts along dimension 0, may hold values from 0.05 to 0.5
- w_gate: bfloat16 [16, 1024, 384], P('expert'), may hold values from -0.1875 to 0.1875
- w_up: bfloat16 [16, 1024, 384], P('expert'), may hold values from -0.1875 to 0.1875
- w_down: bfloat16 [16, 384, 1024], P('expert'), may hold values from -0.3125 to 0.3125
- placement: int32 [16], replicated, may hold values from 0 to 15, each once
- swap_flags: int32 [16], replicated, may hold values from 0 to 1, as said below
Outputs:
- mixed: bfloat16 [3584, 1024], P(('dp', 'expert')), parts along dimension 0
- stored_gate: bfloat16 [32, 1024, 384], P(('dp', 'expert')), parts along dimension 0
- stored_up: bfloat16 [32, 1024, 384], P(('dp', 'expert')), parts along dimension 0
- stored_down: bfloat16 [32, 384, 1024], P(('dp', 'expert')), parts along dimension 0
The draws below stay inside these ranges and needn't reach their ends.
There are 2 independent parts, one for each index of `dp`. The reference program is written for one: setup_inputs(seed, part) draws one part's arguments, and reference() takes and returns one part's arrays. A program takes and returns all parts, laid end to end along the dimension named above; an argument that names none is the same for every part. Nothing has to cross between parts.
Inputs may be any that keep to these rules, and one draw needn't show every extreme that they name: `expert_ids`: each row names 8 different experts; the 112 rows of one device name one expert at most 112 times, a bound that some block reaches. `placement`: each expert is stored on exactly one device. swap_flags[d] equals swap_flags[d XOR (8)]; the number of devices is a power of two. The first and last pairs always trade, the second pair never does.
All inputs are finite; a program needn't handle non-finite values.
Results may differ from the reference program's by a relative error of at most 0.0057.
Values may be sent and summed in bfloat16 or wider, within the bound.
No kernel may reach another device: no remote copies, remote signals or barrier semaphores. Data moves between devices by JAX's collectives and lax.ppermute only.
A program may use at most 64 MiB of HBM per device.

```python
import math
import jax
import jax.numpy as jnp
import numpy as np
from jax import lax

D = 1024
FF = 384
TOP = 8
TOK_DEV = 112
EXPERTS = 16
CAP = 112
TOKENS = 1792


def draw_swap_flags(key, part):
    halves = jax.random.randint(jax.random.fold_in(key, 7), (EXPERTS // 2,), 0, 2).astype(jnp.int32)
    halves = halves.at[0].set(1).at[1].set(0).at[EXPERTS // 2 - 1].set(1)
    return jnp.concatenate([halves, halves], axis=0)


def block_scale(key, dims, shards, low, high):
    factor_of = 1.0
    for dim, shards_of in shards:
        steps = jax.random.uniform(jax.random.fold_in(jax.random.fold_in(key, 6), dim), (shards_of,), jnp.float32, low / len(shards), high / len(shards))
        factor_of = factor_of * jnp.repeat(jnp.exp(steps), dims[dim] // shards_of).reshape((-1,) + (1,) * (len(dims) - 1 - dim))
    return factor_of


def routed_block(key, own, number, rows, count, top, bound, lean):
    sequence = jax.random.permutation(key, count)
    crowded, ordinary = shares(count, rows * top, bound, lean, True), shares(count, rows * top, bound, lean, False)
    places = jnp.arange(count)

    def named(tallies, rotation):
        used = int((tallies > 0).sum())
        fixed = max(1, used // 4)
        shifted = fixed + (places - fixed + rotation * (used - fixed)) % max(1, count - fixed)
        return jnp.zeros((count,), jnp.int32).at[sequence[jnp.where(places < fixed, places, shifted)]].set(jnp.asarray(tallies, jnp.int32))

    tallies = jnp.where(number % 4 == 0, named(crowded, number // 4), named(ordinary, number - number // 4 - 1))
    mixed = jax.random.permutation(jax.random.fold_in(own, 3), count)
    source_of, taker = mixed[0:count // 2 * 2:2], mixed[1:count // 2 * 2:2]
    room = jnp.minimum(tallies[source_of] - 1, bound - tallies[taker]) // 2
    room = jnp.where((source_of == sequence[0]) | (taker == sequence[0]) | (tallies[taker] == 0), 0, jnp.maximum(room, 0))
    shifted = jax.random.randint(jax.random.fold_in(own, 4), (count // 2,), 0, 1 << 20) % (room + 1)
    tallies = tallies.at[source_of].add(-shifted).at[taker].add(shifted)
    members = jnp.searchsorted(jnp.cumsum(tallies), jnp.arange(rows * top), side="right").astype(jnp.int32)
    listing = members.reshape(top, rows).T
    listing = listing[jax.random.permutation(jax.random.fold_in(own, 1), rows)]
    rotation = jax.random.randint(jax.random.fold_in(own, 2), (rows, 1), 0, top)
    return jnp.take_along_axis(listing, (jnp.arange(top)[None, :] + rotation) % top, axis=1)


def shares(amount, total, reach, slope, full):
    loads = [(1 << 20) // math.isqrt(standing ** slope) + 1 for standing in range(1, amount + 1)]
    largest = reach if full else min(reach, max(-(-total // amount), total * loads[0] // sum(loads)))
    least = 1 if total - largest >= amount - 1 else 0
    holding, surplus = [largest] + [least] * (amount - 1), total - largest - least * (amount - 1)
    while surplus > 0:
        candidates = [i for i in range(1, amount) if holding[i] < largest] or [i for i in range(1, amount) if holding[i] < reach]
        mass, remaining = sum([loads[i] for i in candidates]), surplus
        for i in candidates:
            addition = min(reach - holding[i], max(1, remaining * loads[i] // mass), surplus)
            holding[i] = holding[i] + addition
            surplus = surplus - addition
    return np.array(holding)


def centred(own_key, extent, width, limit, cuts=(), kind=jnp.bfloat16):
    entries = jax.random.normal(own_key, extent, jnp.float32) * width
    if len(cuts) > 0:
        entries = block_scale(own_key, extent, cuts, -0.22, 0.18) * entries
    return jnp.clip(entries, min=-limit, max=limit).astype(kind)


def setup_inputs(seed: int = 0, part: int = 0) -> dict:
    key_list = jax.random.split(jax.random.key(seed), 9)
    part_keys = jax.random.split(jax.random.fold_in(key_list[8], part), 9)
    tokens = centred(part_keys[0], (TOKENS, D), 1.0, 6.0, ((0, 16),))
    expert_ids_keys = jax.random.split(jax.random.fold_in(part_keys[1], 1), TOKENS // TOK_DEV)
    expert_ids_turns = jax.random.permutation(jax.random.fold_in(part_keys[1], 3), TOKENS // TOK_DEV)
    expert_ids = jax.vmap(lambda own, number: routed_block(jax.random.fold_in(part_keys[1], 2), own, number, TOK_DEV, EXPERTS, TOP, CAP, 2))(expert_ids_keys, expert_ids_turns).reshape((TOKENS, TOP))
    gate_probs = jnp.clip(jnp.exp(math.log(0.5) - 2.3025851 * jax.random.uniform(part_keys[2], (TOKENS, TOP), jnp.float32) ** block_scale(part_keys[2], (TOKENS, TOP), ((0, 16),), -0.2, 0.2)), 0.05, 0.5)
    w_gate = centred(key_list[3], (EXPERTS, D, FF), D ** -0.5, 0.1875, ((0, 16),))
    w_up = centred(key_list[4], (EXPERTS, D, FF), D ** -0.5, 0.1875, ((0, 16),))
    w_down = centred(key_list[5], (EXPERTS, FF, D), FF ** -0.5, 0.3125, ((0, 16),))
    placement = jax.random.permutation(key_list[6], EXPERTS).astype(jnp.int32)
    swap_flags = draw_swap_flags(jax.random.fold_in(key_list[8], 71), part)
    return dict(tokens=tokens, expert_ids=expert_ids, gate_probs=gate_probs, w_gate=w_gate, w_up=w_up, w_down=w_down, placement=placement, swap_flags=swap_flags)


def expert_apply(rows, gate_w, up_w, down_w):
    gate = jnp.dot(rows, gate_w, preferred_element_type=jnp.float32)
    upward = jnp.dot(rows, up_w, preferred_element_type=jnp.float32)
    hidden = (jax.nn.silu(gate) * upward).astype(jnp.bfloat16)
    return jnp.dot(hidden, down_w, preferred_element_type=jnp.float32).astype(jnp.bfloat16)


def reference(tokens, expert_ids, gate_probs, w_gate, w_up, w_down, placement, swap_flags):
    most_rows = EXPERTS * CAP

    def one_store(carry, stored):
        gate_w, up_w, down_w, expert = stored
        chosen = expert_ids == expert
        picked = jnp.any(chosen, axis=1)
        weight_row = jnp.sum(jnp.where(chosen, gate_probs, jnp.zeros_like(gate_probs)), axis=1)
        count = jnp.sum(picked.astype(jnp.int32))
        (row_index,) = jnp.nonzero(picked, size=most_rows, fill_value=0)
        row_index = row_index.astype(jnp.int32)
        live = jnp.arange(most_rows, dtype=jnp.int32) < count
        outputs = expert_apply(tokens[row_index], gate_w, up_w, down_w)
        outputs = jnp.where(live[:, None], outputs, jnp.zeros_like(outputs))
        values = outputs.astype(jnp.float32)
        carry = carry.at[row_index].add(weight_row[row_index][:, None] * values)
        return carry, None

    mixed, unused = lax.scan(one_store, jnp.zeros((TOKENS, D), jnp.float32), (w_gate, w_up, w_down, placement))
    devices = jnp.arange(EXPERTS, dtype=jnp.int32)
    partners = (devices + EXPERTS // 2) % EXPERTS
    source = jnp.where(swap_flags == 1, partners, devices).astype(jnp.int32)
    return mixed.astype(jnp.bfloat16), w_gate[source], w_up[source], w_down[source]
```

```python
import jax
import jax.numpy as jnp
from jax import lax
from jax.sharding import PartitionSpec as P


def expert_apply(rows, gate_w, up_w, down_w):
    gate = jnp.dot(rows, gate_w, preferred_element_type=jnp.float32)
    upward = jnp.dot(rows, up_w, preferred_element_type=jnp.float32)
    hidden = (jax.nn.silu(gate) * upward).astype(jnp.bfloat16)
    return jnp.dot(hidden, down_w, preferred_element_type=jnp.float32).astype(jnp.bfloat16)


def per_device(tokens, expert_ids, gate_probs, w_gate, w_up, w_down, placement, swap_flags):
    count_dev = lax.axis_size("expert")
    own_index = lax.axis_index("expert")
    half_axis = count_dev // 2
    pairs = [(d, d ^ half_axis) for d in range(count_dev) if d % half_axis != 1]
    taken = swap_flags[own_index] == 1
    moved = [lax.ppermute(w, "expert", pairs) for w in (w_gate, w_up, w_down)]

    experts = jnp.arange(count_dev, dtype=jnp.int32)
    chosen = expert_ids[None, :, :] == experts[:, None, None]
    weights = jnp.sum(jnp.where(chosen, gate_probs[None], 0.0), axis=2)
    all_tokens = lax.all_gather(tokens, "expert", axis=0, tiled=True)
    all_weights = lax.all_gather(weights, "expert", axis=0)
    mine = placement[own_index]
    own_weights = jnp.sum(
        jnp.where((experts == mine)[None, :, None], all_weights, 0.0), axis=1
    ).reshape(-1)
    outputs = expert_apply(all_tokens, w_gate[0], w_up[0], w_down[0])
    partial = (outputs.astype(jnp.float32) * own_weights[:, None]).astype(jnp.bfloat16)
    mixed = lax.psum_scatter(partial, "expert", scatter_dimension=0, tiled=True)

    stored = [jnp.where(taken, m, w) for m, w in zip(moved, (w_gate, w_up, w_down))]
    return (mixed.astype(jnp.bfloat16), *stored)


def solution(mesh):
    in_specs = (
        P(("dp", "expert"), None),
        P(("dp", "expert"), None),
        P(("dp", "expert"), None),
        P("expert", None, None),
        P("expert", None, None),
        P("expert", None, None),
        P(),
        P(),
    )
    out_specs = (
        P(("dp", "expert"), None),
        P(("dp", "expert"), None, None),
        P(("dp", "expert"), None, None),
        P(("dp", "expert"), None, None),
    )
    return jax.shard_map(
        per_device, mesh=mesh, in_specs=in_specs, out_specs=out_specs, check_vma=False
    )
```

```python
import jax
import jax.numpy as jnp
from jax import lax
from jax.sharding import PartitionSpec as P

LANES = 128


def split_parts(values):
    parts = []
    for _ in range(3):
        part = lax.reduce_precision(values, exponent_bits=8, mantissa_bits=7)
        parts.append(part.astype(jnp.bfloat16))
        values = values - part
    return parts


def expert_apply(rows, gate_w, up_w, down_w):
    gate = jnp.dot(rows, gate_w, preferred_element_type=jnp.float32)
    upward = jnp.dot(rows, up_w, preferred_element_type=jnp.float32)
    hidden = (jax.nn.silu(gate) * upward).astype(jnp.bfloat16)
    return jnp.dot(hidden, down_w, preferred_element_type=jnp.float32).astype(jnp.bfloat16)


def per_device(tokens, expert_ids, gate_probs, w_gate, w_up, w_down, placement, swap_flags):
    count_dev = lax.axis_size("expert")
    own_index = lax.axis_index("expert")
    replica = lax.axis_index("dp")
    half_axis = count_dev // 2
    width = tokens.shape[1]
    taken = swap_flags[own_index] == 1
    own = (w_gate, w_up, w_down)

    couple = replica % 2
    replicas = lax.axis_size("dp")
    trades = [(d, d ^ 1) for d in range(replicas)]
    pairs = [(d, d ^ half_axis) for d in range(count_dev) if d % half_axis != 1]
    stored = []
    for w in own:
        rows = w.shape[1] // 2
        half = lax.dynamic_slice_in_dim(w, couple * rows, rows, axis=1)
        came = lax.ppermute(half, "expert", pairs)
        other = lax.ppermute(came, "dp", trades)
        first = jnp.where(couple == 0, came, other)
        second = jnp.where(couple == 0, other, came)
        stored.append(jnp.where(taken, jnp.concatenate([first, second], axis=1), w))

    siblings = [(d, d ^ 1) for d in range(count_dev)]
    near = [lax.ppermute(w, "expert", siblings) for w in own]
    same_core = [list(range(core, count_dev, 2)) for core in range(2)]

    experts = jnp.arange(count_dev, dtype=jnp.int32)
    chosen = expert_ids[:, None, :] == experts[None, :, None]
    weights = jnp.sum(jnp.where(chosen, gate_probs[:, None, :], 0.0), axis=2)
    parts = jnp.concatenate(split_parts(weights), axis=1)
    parts = jnp.pad(parts, ((0, 0), (0, LANES - parts.shape[1])))
    packed = jnp.concatenate([tokens, parts], axis=1)
    gathered = lax.all_gather(
        packed, "expert", axis=0, axis_index_groups=same_core, tiled=True
    )
    rows = gathered[:, :width]
    dense = gathered[:, width : width + 3 * count_dev].astype(jnp.float32)
    dense = dense.reshape(-1, 3, count_dev)
    total = 0.0
    for block, device in ((own, own_index), (near, own_index ^ 1)):
        expert = placement[device]
        weight = jnp.sum(jnp.where(experts == expert, dense, 0.0), axis=(1, 2))
        outputs = expert_apply(rows, *(w[0] for w in block))
        total = total + outputs.astype(jnp.float32) * weight[:, None]
    mixed = lax.psum_scatter(
        total.astype(jnp.bfloat16),
        "expert",
        scatter_dimension=0,
        axis_index_groups=same_core,
        tiled=True,
    )
    return (mixed, *stored)


def solution(mesh):
    in_specs = (
        P(("dp", "expert"), None),
        P(("dp", "expert"), None),
        P(("dp", "expert"), None),
        P("expert", None, None),
        P("expert", None, None),
        P("expert", None, None),
        P(),
        P(),
    )
    out_specs = (
        P(("dp", "expert"), None),
        P(("dp", "expert"), None, None),
        P(("dp", "expert"), None, None),
        P(("dp", "expert"), None, None),
    )
    return jax.shard_map(
        per_device, mesh=mesh, in_specs=in_specs, out_specs=out_specs, check_vma=False
    )
```

```python
import functools

import jax
import jax.numpy as jnp
from jax import lax
from jax.experimental import pallas as pl
from jax.experimental.pallas import tpu as pltpu
from jax.sharding import PartitionSpec as P

LANES = 128
VMEM_LIMIT = 48 * 2**20


def split_parts(values):
    parts = []
    for _ in range(3):
        part = lax.reduce_precision(values, exponent_bits=8, mantissa_bits=7)
        parts.append(part.astype(jnp.bfloat16))
        values = values - part
    return parts


def pack_gates(tokens, expert_ids, gate_probs, count):
    experts = jnp.arange(count, dtype=jnp.int32)
    chosen = expert_ids[:, None, :] == experts[None, :, None]
    weights = jnp.sum(jnp.where(chosen, gate_probs[:, None, :], 0.0), axis=2)
    parts = jnp.concatenate(split_parts(weights), axis=1)
    parts = jnp.pad(parts, ((0, 0), (0, -parts.shape[1] % LANES)))
    return jnp.concatenate([tokens, parts], axis=1)


def dot(a, b):
    return jnp.dot(a, b, preferred_element_type=jnp.float32)


def experts_kernel(count, blocks, halved, based, *refs):
    info, refs = refs[0], refs[1:]
    rows, refs = refs[:blocks], refs[blocks:]
    each = 6 if halved else 3
    weights, refs = [refs[:each], refs[each : 2 * each]], refs[2 * each :]
    base, refs = (refs[0], refs[1:]) if based else (None, refs)
    out, x = refs
    height, width = rows[0].shape[0], x.shape[1]
    group = 2
    for first in range(0, blocks, group):
        for i in range(group):
            x[i * height : (i + 1) * height, :] = rows[first + i][:, :width]
        tail = jnp.concatenate(
            [rows[first + i][:, width:].astype(jnp.float32) for i in range(group)], axis=0
        )
        lane = lax.broadcasted_iota(jnp.int32, tail.shape, 1)
        span = pl.ds(first * height, group * height)
        for slot, mats in enumerate(weights):
            mine = (lane % count == info[slot]) & (lane < 3 * count)
            weight = jnp.sum(jnp.where(mine, tail, 0.0), axis=1, keepdims=True)
            if halved:
                ga, gb, ua, ub, da, db = mats
                depth = ga.shape[0]
                at = pl.multiple_of(info[2] * depth, depth)
                off = pl.multiple_of(depth - at, depth)
                xa, xb = x[:, pl.ds(at, depth)], x[:, pl.ds(off, depth)]
                gate = dot(xa, ga[...]) + dot(xb, gb[...])
                up = dot(xa, ua[...]) + dot(xb, ub[...])
                part = da.shape[1]
                at = pl.multiple_of(info[2] * part, part)
                off = pl.multiple_of(part - at, part)
                downs = [(pl.ds(at, part), da), (pl.ds(off, part), db)]
            else:
                g, u, d = mats
                gate, up = dot(x[...], g[...]), dot(x[...], u[...])
                downs = [(slice(None), d)]
            hidden = (gate / (1.0 + jnp.exp(-gate)) * up).astype(jnp.bfloat16)
            for columns, d in downs:
                value = dot(hidden, d[...]).astype(jnp.bfloat16).astype(jnp.float32) * weight
                if slot > 0:
                    value = value + out[span, columns]
                elif based:
                    value = value + base[span, columns]
                out[span, columns] = value


def run_experts(info, rows, weights, count, width, base=None):
    halved = len(weights[0]) == 6
    height = rows[0].shape[0]
    vmem = pl.BlockSpec(memory_space=pltpu.VMEM)
    flat = [m for mats in weights for m in mats]
    extra = [] if base is None else [base]
    shape = (len(rows) * height, width)
    flops = 6 * shape[0] * sum(m.size for m in flat) // 3
    return pl.pallas_call(
        functools.partial(experts_kernel, count, len(rows), halved, base is not None),
        out_shape=jax.ShapeDtypeStruct(shape, jnp.float32),
        in_specs=[pl.BlockSpec(memory_space=pltpu.SMEM)]
        + [vmem] * (len(rows) + len(flat) + len(extra)),
        out_specs=vmem,
        scratch_shapes=[pltpu.VMEM((2 * height, width), jnp.bfloat16)],
        compiler_params=pltpu.CompilerParams(vmem_limit_bytes=VMEM_LIMIT),
        cost_estimate=pl.CostEstimate(
            flops=flops, bytes_accessed=4 * shape[0] * width, transcendentals=0
        ),
    )(info, *rows, *flat, *extra)


def per_device(tokens, expert_ids, gate_probs, w_gate, w_up, w_down, placement, swap_flags):
    count = lax.axis_size("expert")
    me = lax.axis_index("expert")
    couple = lax.axis_index("dp") % 2
    half_axis = count // 2
    height, width = tokens.shape
    own = (w_gate[0], w_up[0], w_down[0])
    axes = (0, 0, 1)
    trades = [(d, d ^ 1) for d in range(lax.axis_size("dp"))]
    pairs = [(d, d ^ half_axis) for d in range(count) if d % half_axis != 1]

    def send(value, bit):
        return lax.ppermute(value, "expert", [(d, d ^ bit) for d in range(count)])

    bits = []
    bit = half_axis
    while bit > 2:
        bits.append(bit)
        bit //= 2
    blocks = {0: pack_gates(tokens, expert_ids, gate_probs, count)}
    for stage, bit in enumerate(bits):
        for i in sorted(blocks, reverse=True):
            blocks[i | 1 << stage] = send(blocks[i], bit)
    rows = [blocks[i] for i in range(len(blocks))]

    halves = []
    for w, axis in zip(own, axes):
        size = w.shape[axis] // 2
        halves.append(lax.dynamic_slice_in_dim(w, couple * size, size, axis=axis))

    near = [send(w, 1) for w in own]
    far = [[], []]
    for half in halves:
        came = send(half, 2)
        other = lax.ppermute(came, "dp", trades)
        far[0] += [came, other]
        far[1] += [send(came, 1), send(other, 1)]

    def info(a, b):
        return jnp.stack([placement[me ^ a], placement[me ^ b], couple]).astype(jnp.int32)

    base = run_experts(info(0, 1), rows, [own, near], count, width)
    total = run_experts(info(2, 3), rows, far, count, width, base)
    parts = [total[i * height : (i + 1) * height] for i in range(len(rows))]
    for stage in reversed(range(len(bits))):
        for i in reversed(range(1 << stage)):
            came = send(parts[i | 1 << stage].astype(jnp.bfloat16), bits[stage])
            parts[i] = parts[i] + came.astype(jnp.float32)
    mixed = parts[0].astype(jnp.bfloat16)

    taken = swap_flags[me] == 1
    stored = []
    for w, half, axis in zip(own, halves, axes):
        came = lax.ppermute(half, "expert", pairs)
        other = lax.ppermute(came, "dp", trades)
        first = jnp.where(couple == 0, came, other)
        second = jnp.where(couple == 0, other, came)
        stored.append(jnp.where(taken, jnp.concatenate([first, second], axis=axis), w)[None])
    return (mixed, *stored)


def solution(mesh):
    in_specs = (
        P(("dp", "expert"), None),
        P(("dp", "expert"), None),
        P(("dp", "expert"), None),
        P("expert", None, None),
        P("expert", None, None),
        P("expert", None, None),
        P(),
        P(),
    )
    out_specs = (
        P(("dp", "expert"), None),
        P(("dp", "expert"), None, None),
        P(("dp", "expert"), None, None),
        P(("dp", "expert"), None, None),
    )
    return jax.shard_map(
        per_device, mesh=mesh, in_specs=in_specs, out_specs=out_specs, check_vma=False
    )
```

```python
import functools

import jax
import jax.numpy as jnp
from jax import lax
from jax.experimental import pallas as pl
from jax.experimental.pallas import tpu as pltpu
from jax.sharding import PartitionSpec as P

LANES = 128
VMEM_LIMIT = 48 * 2**20


def split_parts(values):
    parts = []
    for _ in range(3):
        part = lax.reduce_precision(values, exponent_bits=8, mantissa_bits=7)
        parts.append(part.astype(jnp.bfloat16))
        values = values - part
    return parts


def pack_gates(tokens, expert_ids, gate_probs, count):
    experts = jnp.arange(count, dtype=jnp.int32)
    chosen = expert_ids[:, None, :] == experts[None, :, None]
    weights = jnp.sum(jnp.where(chosen, gate_probs[:, None, :], 0.0), axis=2)
    parts = jnp.concatenate(split_parts(weights), axis=1)
    parts = jnp.pad(parts, ((0, 0), (0, -parts.shape[1] % LANES)))
    return jnp.concatenate([tokens, parts], axis=1)


def dot(a, b):
    return jnp.dot(a, b, preferred_element_type=jnp.float32)


def experts_kernel(count, halved, based, sent, *refs):
    info, refs = refs[0], refs[1:]
    rows, refs = refs[:2], refs[2:]
    each = 4 if halved else 3
    weights, refs = [refs[:each], refs[each : 2 * each]], refs[2 * each :]
    base, refs = (refs[:2], refs[2:]) if based else (None, refs)
    outs, x, total = refs[:2], refs[2], refs[3]
    height, width = rows[0].shape[0], x.shape[1]
    for i in range(2):
        x[i * height : (i + 1) * height, :] = rows[i][:, :width]
    tail = jnp.concatenate([r[:, width:].astype(jnp.float32) for r in rows], axis=0)
    lane = lax.broadcasted_iota(jnp.int32, tail.shape, 1)
    for slot, mats in enumerate(weights):
        mine = (lane % count == info[slot]) & (lane < 3 * count)
        weight = jnp.sum(jnp.where(mine, tail, 0.0), axis=1, keepdims=True)
        if halved:
            first, down_first, second, down_second = mats
            depth = first.shape[0] // 2
            at = pl.multiple_of(info[2] * depth, depth)
            off = pl.multiple_of(depth - at, depth)
            xa, xb = x[:, pl.ds(at, depth)], x[:, pl.ds(off, depth)]
            gate = dot(xa, first[:depth, :]) + dot(xb, second[:depth, :])
            up = dot(xa, first[depth:, :]) + dot(xb, second[depth:, :])
            part = down_first.shape[1]
            at = pl.multiple_of(info[2] * part, part)
            off = pl.multiple_of(part - at, part)
            downs = [(pl.ds(at, part), down_first), (pl.ds(off, part), down_second)]
        else:
            g, u, d = mats
            gate, up = dot(x[...], g[...]), dot(x[...], u[...])
            downs = [(slice(None), d)]
        hidden = (gate / (1.0 + jnp.exp(-gate)) * up).astype(jnp.bfloat16)
        for columns, d in downs:
            value = dot(hidden, d[...]).astype(jnp.bfloat16).astype(jnp.float32) * weight
            if slot > 0:
                value = value + total[:, columns]
            total[:, columns] = value
    for i in range(2):
        value = total[i * height : (i + 1) * height, :]
        if based:
            value = value + base[i][...]
        outs[i][...] = value.astype(outs[i].dtype)


def run_experts(info, rows, weights, count, width, base=(), sent=False):
    halved = len(weights[0]) == 4
    height = rows[0].shape[0]
    vmem = pl.BlockSpec(memory_space=pltpu.VMEM)
    flat = [m for mats in weights for m in mats]
    dtype = jnp.bfloat16 if sent else jnp.float32
    flops = 2 * 2 * height * sum(m.size for m in flat)
    return pl.pallas_call(
        functools.partial(experts_kernel, count, halved, len(base) > 0, sent),
        out_shape=[jax.ShapeDtypeStruct((height, width), dtype)] * 2,
        in_specs=[pl.BlockSpec(memory_space=pltpu.SMEM)]
        + [vmem] * (2 + len(flat) + len(base)),
        out_specs=[vmem] * 2,
        scratch_shapes=[
            pltpu.VMEM((2 * height, width), jnp.bfloat16),
            pltpu.VMEM((2 * height, width), jnp.float32),
        ],
        compiler_params=pltpu.CompilerParams(vmem_limit_bytes=VMEM_LIMIT),
        cost_estimate=pl.CostEstimate(
            flops=flops, bytes_accessed=16 * height * width, transcendentals=0
        ),
    )(info, *rows, *flat, *base)


def halves_kernel(info, gate, up, down, upper, lower, sems):
    depth, part = upper.shape[0] // 2, lower.shape[1]
    at = pl.ds(pl.multiple_of(info[0] * depth, depth), depth)
    columns = pl.ds(pl.multiple_of(info[0] * part, part), part)
    copies = [
        pltpu.make_async_copy(gate.at[at, :], upper.at[pl.ds(0, depth), :], sems.at[0]),
        pltpu.make_async_copy(up.at[at, :], upper.at[pl.ds(depth, depth), :], sems.at[1]),
        pltpu.make_async_copy(down.at[:, columns], lower, sems.at[2]),
    ]
    for copy in copies:
        copy.start()
    for copy in copies:
        copy.wait()


def take_halves(couple, gate, up, down):
    hbm = pl.BlockSpec(memory_space=pl.ANY)
    return pl.pallas_call(
        halves_kernel,
        out_shape=[
            jax.ShapeDtypeStruct(gate.shape, gate.dtype),
            jax.ShapeDtypeStruct((down.shape[0], down.shape[1] // 2), down.dtype),
        ],
        in_specs=[pl.BlockSpec(memory_space=pltpu.SMEM)] + [hbm] * 3,
        out_specs=[hbm] * 2,
        scratch_shapes=[pltpu.SemaphoreType.DMA((3,))],
        cost_estimate=pl.CostEstimate(
            flops=0, bytes_accessed=4 * (gate.size + down.size // 2), transcendentals=0
        ),
    )(couple[None], gate, up, down)


def store_kernel(info, gate, up, down, upper, lower, other_upper, other_lower, *refs):
    out_gate, out_up, out_down, sems = refs
    depth, part = upper.shape[0] // 2, lower.shape[1]

    def run(copies):
        copies = [pltpu.make_async_copy(a, b, sems.at[i]) for i, (a, b) in enumerate(copies)]
        for copy in copies:
            copy.start()
        for copy in copies:
            copy.wait()

    @pl.when(info[1] == 1)
    def _():
        copies = []
        for flip, a, b in ((0, upper, lower), (1, other_upper, other_lower)):
            half = jnp.bitwise_xor(info[0], flip)
            at = pl.ds(pl.multiple_of(half * depth, depth), depth)
            columns = pl.ds(pl.multiple_of(half * part, part), part)
            copies.append((a.at[pl.ds(0, depth), :], out_gate.at[at, :]))
            copies.append((a.at[pl.ds(depth, depth), :], out_up.at[at, :]))
            copies.append((b, out_down.at[:, columns]))
        run(copies)

    @pl.when(info[1] != 1)
    def _():
        run([(gate, out_gate), (up, out_up), (down, out_down)])


def store_expert(info, own, came):
    hbm = pl.BlockSpec(memory_space=pl.ANY)
    size = sum(w.size for w in own)
    return pl.pallas_call(
        store_kernel,
        out_shape=[jax.ShapeDtypeStruct(w.shape, w.dtype) for w in own],
        in_specs=[pl.BlockSpec(memory_space=pltpu.SMEM)] + [hbm] * 7,
        out_specs=[hbm] * 3,
        scratch_shapes=[pltpu.SemaphoreType.DMA((6,))],
        cost_estimate=pl.CostEstimate(flops=0, bytes_accessed=4 * size, transcendentals=0),
    )(info, *own, *came)


def after(value, *others):
    return lax.optimization_barrier((value, *others))[0]


def per_device(tokens, expert_ids, gate_probs, w_gate, w_up, w_down, placement, swap_flags):
    count = lax.axis_size("expert")
    me = lax.axis_index("expert")
    couple = (lax.axis_index("dp") % 2).astype(jnp.int32)
    half_axis = count // 2
    width = tokens.shape[1]
    own = (w_gate[0], w_up[0], w_down[0])
    trades = [(d, d ^ 1) for d in range(lax.axis_size("dp"))]
    pairs = [(d, d ^ half_axis) for d in range(count) if d % half_axis != 1]

    def send(value, bit, name):
        with jax.named_scope(name):
            return lax.ppermute(value, "expert", [(d, d ^ bit) for d in range(count)])

    def swap(value):
        with jax.named_scope("swap"):
            return lax.ppermute(value, "expert", pairs)

    def trade(value, name):
        with jax.named_scope(name):
            return lax.ppermute(value, "dp", trades)

    upper, lower = take_halves(couple, *own)
    x_upper, x_lower = send(upper, 2, "x_upper"), send(lower, 2, "x_lower")

    bits = []
    bit = half_axis
    while bit > 2:
        bits.append(bit)
        bit //= 2
    blocks = {0: pack_gates(tokens, expert_ids, gate_probs, count)}
    for stage, bit in enumerate(bits):
        for i in sorted(blocks):
            blocks[i | 1 << stage] = send(blocks[i], bit, "tokens")
    near = [send(w, 1, "near") for w in own]

    z_upper = swap(after(upper, blocks[1]))
    z_lower = swap(after(lower, x_lower))

    y_upper = trade(x_upper, "x_trade")
    y_lower = trade(x_lower, "x_trade")
    far = [x_upper, x_lower, y_upper, y_lower]
    across = [send(part, 1, "x_near") for part in far]

    def info(a, b):
        return jnp.stack([placement[me ^ a], placement[me ^ b], couple]).astype(jnp.int32)

    parts = {}
    for first in reversed(range(0, len(blocks), 2)):
        rows = [blocks[first], blocks[first + 1]]
        base = run_experts(info(0, 1), rows, [own, near], count, width)
        sent = first >= len(blocks) // 2
        parts[first], parts[first + 1] = run_experts(
            info(2, 3), rows, [far, across], count, width, base, sent
        )
    for stage in reversed(range(len(bits))):
        for i in reversed(range(1 << stage)):
            came = send(parts[i | 1 << stage].astype(jnp.bfloat16), bits[stage], "sums")
            parts[i] = parts[i] + came.astype(jnp.float32)
    mixed = parts[0].astype(jnp.bfloat16)

    w_upper = trade(after(z_upper, y_lower), "swap_trade")
    w_lower = trade(after(z_lower, y_lower), "swap_trade")
    settings = jnp.stack([couple, swap_flags[me]])
    stored = store_expert(settings, own, (z_upper, z_lower, w_upper, w_lower))
    return (mixed, *(w[None] for w in stored))


def solution(mesh):
    in_specs = (
        P(("dp", "expert"), None),
        P(("dp", "expert"), None),
        P(("dp", "expert"), None),
        P("expert", None, None),
        P("expert", None, None),
        P("expert", None, None),
        P(),
        P(),
    )
    out_specs = (
        P(("dp", "expert"), None),
        P(("dp", "expert"), None, None),
        P(("dp", "expert"), None, None),
        P(("dp", "expert"), None, None),
    )
    return jax.shard_map(
        per_device, mesh=mesh, in_specs=in_specs, out_specs=out_specs, check_vma=False
    )
```

```python
import functools

import jax
import jax.numpy as jnp
from jax import lax
from jax.experimental import pallas as pl
from jax.experimental.pallas import tpu as pltpu
from jax.sharding import PartitionSpec as P

LANES = 128
VMEM_LIMIT = 20 * 2**20


def split_parts(values):
    parts = []
    for _ in range(3):
        part = lax.reduce_precision(values, exponent_bits=8, mantissa_bits=7)
        parts.append(part.astype(jnp.bfloat16))
        values = values - part
    return parts


def pack_gates(tokens, expert_ids, gate_probs, count):
    experts = jnp.arange(count, dtype=jnp.int32)
    chosen = expert_ids[:, None, :] == experts[None, :, None]
    weights = jnp.sum(jnp.where(chosen, gate_probs[:, None, :], 0.0), axis=2)
    parts = jnp.concatenate(split_parts(weights), axis=1)
    parts = jnp.pad(parts, ((0, 0), (0, -parts.shape[1] % LANES)))
    return jnp.concatenate([tokens, parts], axis=1)


def dot(a, b):
    return jnp.dot(a, b, preferred_element_type=jnp.float32)


def experts_kernel(count, halved, based, sent, *refs):
    info, refs = refs[0], refs[1:]
    rows, refs = refs[:2], refs[2:]
    each = 4 if halved else 3
    weights, refs = [refs[:each], refs[each : 2 * each]], refs[2 * each :]
    base, refs = (refs[:2], refs[2:]) if based else (None, refs)
    outs, x, total = refs[:2], refs[2], refs[3]
    height, width = rows[0].shape[0], x.shape[1]
    for i in range(2):
        x[i * height : (i + 1) * height, :] = rows[i][:, :width]
    tail = jnp.concatenate([r[:, width:].astype(jnp.float32) for r in rows], axis=0)
    lane = lax.broadcasted_iota(jnp.int32, tail.shape, 1)
    for slot, mats in enumerate(weights):
        mine = (lane % count == info[slot]) & (lane < 3 * count)
        weight = jnp.sum(jnp.where(mine, tail, 0.0), axis=1, keepdims=True)
        if halved:
            first, down_first, second, down_second = mats
            depth = first.shape[0] // 2
            at = pl.multiple_of(info[2] * depth, depth)
            off = pl.multiple_of(depth - at, depth)
            xa, xb = x[:, pl.ds(at, depth)], x[:, pl.ds(off, depth)]
            gate = dot(xa, first[:depth, :]) + dot(xb, second[:depth, :])
            up = dot(xa, first[depth:, :]) + dot(xb, second[depth:, :])
            part = down_first.shape[1]
            at = pl.multiple_of(info[2] * part, part)
            off = pl.multiple_of(part - at, part)
            downs = [(pl.ds(at, part), down_first), (pl.ds(off, part), down_second)]
        else:
            g, u, d = mats
            gate, up = dot(x[...], g[...]), dot(x[...], u[...])
            downs = [(slice(None), d)]
        hidden = (gate / (1.0 + jnp.exp(-gate)) * up).astype(jnp.bfloat16)
        for columns, d in downs:
            value = dot(hidden, d[...]).astype(jnp.bfloat16).astype(jnp.float32) * weight
            if slot > 0:
                value = value + total[:, columns]
            total[:, columns] = value
    for i in range(2):
        value = total[i * height : (i + 1) * height, :]
        if based:
            value = value + base[i][...]
        outs[i][...] = value.astype(outs[i].dtype)


def run_experts(info, rows, weights, count, width, base=(), sent=False):
    halved = len(weights[0]) == 4
    height = rows[0].shape[0]
    vmem = pl.BlockSpec(memory_space=pltpu.VMEM)
    flat = [m for mats in weights for m in mats]
    dtype = jnp.bfloat16 if sent else jnp.float32
    flops = 2 * 2 * height * sum(m.size for m in flat)
    return pl.pallas_call(
        functools.partial(experts_kernel, count, halved, len(base) > 0, sent),
        out_shape=[jax.ShapeDtypeStruct((height, width), dtype)] * 2,
        in_specs=[pl.BlockSpec(memory_space=pltpu.SMEM)]
        + [vmem] * (2 + len(flat) + len(base)),
        out_specs=[vmem] * 2,
        scratch_shapes=[
            pltpu.VMEM((2 * height, width), jnp.bfloat16),
            pltpu.VMEM((2 * height, width), jnp.float32),
        ],
        compiler_params=pltpu.CompilerParams(vmem_limit_bytes=VMEM_LIMIT),
        cost_estimate=pl.CostEstimate(
            flops=flops, bytes_accessed=16 * height * width, transcendentals=0
        ),
    )(info, *rows, *flat, *base)


def halves_kernel(info, gate, up, down, upper, lower, sems):
    depth, part = upper.shape[0] // 2, lower.shape[1]
    at = pl.ds(pl.multiple_of(info[0] * depth, depth), depth)
    columns = pl.ds(pl.multiple_of(info[0] * part, part), part)
    copies = [
        pltpu.make_async_copy(gate.at[at, :], upper.at[pl.ds(0, depth), :], sems.at[0]),
        pltpu.make_async_copy(up.at[at, :], upper.at[pl.ds(depth, depth), :], sems.at[1]),
        pltpu.make_async_copy(down.at[:, columns], lower, sems.at[2]),
    ]
    for copy in copies:
        copy.start()
    for copy in copies:
        copy.wait()


def take_halves(couple, gate, up, down):
    hbm = pl.BlockSpec(memory_space=pl.ANY)
    return pl.pallas_call(
        halves_kernel,
        out_shape=[
            jax.ShapeDtypeStruct(gate.shape, gate.dtype),
            jax.ShapeDtypeStruct((down.shape[0], down.shape[1] // 2), down.dtype),
        ],
        in_specs=[pl.BlockSpec(memory_space=pltpu.SMEM)] + [hbm] * 3,
        out_specs=[pl.BlockSpec(memory_space=pltpu.VMEM)] * 2,
        scratch_shapes=[pltpu.SemaphoreType.DMA((3,))],
        compiler_params=pltpu.CompilerParams(vmem_limit_bytes=8 * 2**20),
        cost_estimate=pl.CostEstimate(
            flops=0, bytes_accessed=4 * (gate.size + down.size // 2), transcendentals=0
        ),
    )(couple[None], gate, up, down)


def store_kernel(info, gate, up, down, upper, lower, other_upper, other_lower, *refs):
    out_gate, out_up, out_down, sems = refs
    depth, part = upper.shape[0] // 2, lower.shape[1]

    def run(copies):
        copies = [pltpu.make_async_copy(a, b, sems.at[i]) for i, (a, b) in enumerate(copies)]
        for copy in copies:
            copy.start()
        for copy in copies:
            copy.wait()

    @pl.when(info[1] == 1)
    def _():
        copies = []
        for flip, a, b in ((0, upper, lower), (1, other_upper, other_lower)):
            half = jnp.bitwise_xor(info[0], flip)
            at = pl.ds(pl.multiple_of(half * depth, depth), depth)
            columns = pl.ds(pl.multiple_of(half * part, part), part)
            copies.append((a.at[pl.ds(0, depth), :], out_gate.at[at, :]))
            copies.append((a.at[pl.ds(depth, depth), :], out_up.at[at, :]))
            copies.append((b, out_down.at[:, columns]))
        run(copies)

    @pl.when(info[1] != 1)
    def _():
        run([(gate, out_gate), (up, out_up), (down, out_down)])


def store_expert(info, own, came):
    hbm = pl.BlockSpec(memory_space=pl.ANY)
    size = sum(w.size for w in own)
    return pl.pallas_call(
        store_kernel,
        out_shape=[jax.ShapeDtypeStruct(w.shape, w.dtype) for w in own],
        in_specs=[pl.BlockSpec(memory_space=pltpu.SMEM)]
        + [pl.BlockSpec(memory_space=pltpu.VMEM)] * 7,
        out_specs=[hbm] * 3,
        scratch_shapes=[pltpu.SemaphoreType.DMA((6,))],
        compiler_params=pltpu.CompilerParams(vmem_limit_bytes=12 * 2**20),
        cost_estimate=pl.CostEstimate(flops=0, bytes_accessed=4 * size, transcendentals=0),
    )(info, *own, *came)


def after(value, *others):
    return lax.optimization_barrier((value, *others))[0]


def per_device(tokens, expert_ids, gate_probs, w_gate, w_up, w_down, placement, swap_flags):
    count = lax.axis_size("expert")
    me = lax.axis_index("expert")
    couple = (lax.axis_index("dp") % 2).astype(jnp.int32)
    half_axis = count // 2
    width = tokens.shape[1]
    own = (w_gate[0], w_up[0], w_down[0])
    trades = [(d, d ^ 1) for d in range(lax.axis_size("dp"))]
    pairs = [(d, d ^ half_axis) for d in range(count) if d % half_axis != 1]

    def send(value, bit, name):
        with jax.named_scope(name):
            return lax.ppermute(value, "expert", [(d, d ^ bit) for d in range(count)])

    def swap(value):
        with jax.named_scope("swap"):
            return lax.ppermute(value, "expert", pairs)

    def trade(value, name):
        with jax.named_scope(name):
            return lax.ppermute(value, "dp", trades)

    upper, lower = take_halves(couple, *own)
    x_upper = send(upper, 2, "x_upper")

    bits = []
    bit = half_axis
    while bit > 2:
        bits.append(bit)
        bit //= 2
    near = [send(w, 1, "near") for w in own]
    blocks = {0: after(pack_gates(tokens, expert_ids, gate_probs, count), *near)}
    for stage, bit in enumerate(bits):
        for i in sorted(blocks):
            blocks[i | 1 << stage] = send(blocks[i], bit, "tokens")
    rows = [blocks[i] for i in range(len(blocks))]
    x_lower = send(after(lower, blocks[2]), 2, "x_lower")

    z_upper = swap(upper)
    y_upper = trade(after(x_upper, blocks[1]), "x_trade")
    across = [send(x_upper, 1, "x_near"), send(after(x_lower, x_upper), 1, "x_near")]
    y_lower = trade(after(x_lower, z_upper, *across, *rows), "x_trade")
    z_lower = swap(after(lower, z_upper))
    across.append(send(y_upper, 1, "x_near"))

    def info(a, b):
        return jnp.stack([placement[me ^ a], placement[me ^ b], couple]).astype(jnp.int32)

    firsts = list(reversed(range(0, len(rows), 2)))
    bases = {}
    for first in firsts:
        bases[first] = run_experts(info(0, 1), rows[first : first + 2], [own, near], count, width)
    across.append(send(after(y_lower, [bases[i] for i in firsts]), 1, "x_near"))
    far = [x_upper, x_lower, y_upper, y_lower]
    parts = {}
    for first in firsts:
        sent = first >= len(rows) // 2
        late = [] if sent else [z_lower]
        parts[first], parts[first + 1] = run_experts(
            after(info(2, 3), *late),
            rows[first : first + 2],
            [far, across],
            count,
            width,
            bases[first],
            sent,
        )
    for stage in reversed(range(len(bits))):
        for i in reversed(range(1 << stage)):
            came = send(parts[i | 1 << stage].astype(jnp.bfloat16), bits[stage], "sums")
            parts[i] = parts[i] + came.astype(jnp.float32)
    mixed = parts[0].astype(jnp.bfloat16)

    w_upper = trade(after(z_upper, y_lower), "swap_trade")
    w_lower = trade(after(z_lower, y_lower), "swap_trade")
    settings = jnp.stack([couple, swap_flags[me]])
    stored = store_expert(settings, own, (z_upper, z_lower, w_upper, w_lower))
    return (mixed, *(w[None] for w in stored))


def solution(mesh):
    in_specs = (
        P(("dp", "expert"), None),
        P(("dp", "expert"), None),
        P(("dp", "expert"), None),
        P("expert", None, None),
        P("expert", None, None),
        P("expert", None, None),
        P(),
        P(),
    )
    out_specs = (
        P(("dp", "expert"), None),
        P(("dp", "expert"), None, None),
        P(("dp", "expert"), None, None),
        P(("dp", "expert"), None, None),
    )
    return jax.shard_map(
        per_device, mesh=mesh, in_specs=in_specs, out_specs=out_specs, check_vma=False
    )
```

```python
import functools

import jax
import jax.numpy as jnp
from jax import lax
from jax.experimental import pallas as pl
from jax.experimental.pallas import tpu as pltpu
from jax.sharding import PartitionSpec as P

LANES = 128
VMEM_LIMIT = 20 * 2**20


def split_parts(values):
    parts = []
    for _ in range(3):
        part = lax.reduce_precision(values, exponent_bits=8, mantissa_bits=7)
        parts.append(part.astype(jnp.bfloat16))
        values = values - part
    return parts


def pack_gates(tokens, expert_ids, gate_probs, count):
    experts = jnp.arange(count, dtype=jnp.int32)
    chosen = expert_ids[:, None, :] == experts[None, :, None]
    weights = jnp.sum(jnp.where(chosen, gate_probs[:, None, :], 0.0), axis=2)
    parts = jnp.concatenate(split_parts(weights), axis=1)
    parts = jnp.pad(parts, ((0, 0), (0, -parts.shape[1] % LANES)))
    return jnp.concatenate([tokens, parts], axis=1)


def dot(a, b):
    return jnp.dot(a, b, preferred_element_type=jnp.float32)


def experts_kernel(count, flips, halved, based, *refs):
    placement, refs = refs[0], refs[1:]
    rows, refs = refs[:2], refs[2:]
    each = 6 if halved else 3
    weights, refs = [refs[:each], refs[each : 2 * each]], refs[2 * each :]
    base, refs = (refs[:2], refs[2:]) if based else (None, refs)
    outs, x, total = refs[:2], refs[2], refs[3]
    height, width = rows[0].shape[0], x.shape[1]
    me = lax.axis_index("expert")
    half = lax.axis_index("dp") % 2
    for i in range(2):
        x[i * height : (i + 1) * height, :] = rows[i][:, :width]
    tail = jnp.concatenate([r[:, width:].astype(jnp.float32) for r in rows], axis=0)
    lane = lax.broadcasted_iota(jnp.int32, tail.shape, 1)
    for slot, mats in enumerate(weights):
        expert = placement[me ^ flips[slot]]
        mine = (lane % count == expert) & (lane < 3 * count)
        weight = jnp.sum(jnp.where(mine, tail, 0.0), axis=1, keepdims=True)
        if halved:
            ga, ua, da, gb, ub, db = mats
            depth = ga.shape[0]
            at = pl.multiple_of(half * depth, depth)
            off = pl.multiple_of(depth - at, depth)
            xa, xb = x[:, pl.ds(at, depth)], x[:, pl.ds(off, depth)]
            gate = dot(xa, ga[...]) + dot(xb, gb[...])
            up = dot(xa, ua[...]) + dot(xb, ub[...])
            part = da.shape[1]
            at = pl.multiple_of(half * part, part)
            off = pl.multiple_of(part - at, part)
            downs = [(pl.ds(at, part), da), (pl.ds(off, part), db)]
        else:
            g, u, d = mats
            gate, up = dot(x[...], g[...]), dot(x[...], u[...])
            downs = [(slice(None), d)]
        hidden = (gate / (1.0 + jnp.exp(-gate)) * up).astype(jnp.bfloat16)
        for columns, d in downs:
            value = dot(hidden, d[...]).astype(jnp.bfloat16).astype(jnp.float32) * weight
            if slot > 0:
                value = value + total[:, columns]
            total[:, columns] = value
    for i in range(2):
        value = total[i * height : (i + 1) * height, :]
        if based:
            value = value + base[i][...]
        outs[i][...] = value.astype(outs[i].dtype)


def run_experts(placement, flips, rows, weights, count, width, base=(), sent=False):
    halved = len(weights[0]) == 6
    height = rows[0].shape[0]
    vmem = pl.BlockSpec(memory_space=pltpu.VMEM)
    flat = [m for mats in weights for m in mats]
    dtype = jnp.bfloat16 if sent else jnp.float32
    flops = 2 * 2 * height * sum(m.size for m in flat)
    return pl.pallas_call(
        functools.partial(experts_kernel, count, flips, halved, len(base) > 0),
        out_shape=[jax.ShapeDtypeStruct((height, width), dtype)] * 2,
        in_specs=[pl.BlockSpec(memory_space=pltpu.SMEM)]
        + [vmem] * (2 + len(flat) + len(base)),
        out_specs=[vmem] * 2,
        scratch_shapes=[
            pltpu.VMEM((2 * height, width), jnp.bfloat16),
            pltpu.VMEM((2 * height, width), jnp.float32),
        ],
        compiler_params=pltpu.CompilerParams(vmem_limit_bytes=VMEM_LIMIT),
        cost_estimate=pl.CostEstimate(
            flops=flops, bytes_accessed=16 * height * width, transcendentals=0
        ),
    )(placement, *rows, *flat, *base)


def run_copies(copies, sems):
    copies = [pltpu.make_async_copy(a, b, sems.at[i]) for i, (a, b) in enumerate(copies)]
    for copy in copies:
        copy.start()
    for copy in copies:
        copy.wait()


def part_of(ref, axis, half, size):
    span = pl.ds(pl.multiple_of(half * size, size), size)
    return ref.at[span, :] if axis == 0 else ref.at[:, span]


def halves_kernel(axes, *refs):
    sources, outs, sems = refs[:3], refs[3:6], refs[6]
    half = lax.axis_index("dp") % 2
    run_copies(
        [
            (part_of(source, axis, half, out.shape[axis]), out)
            for source, out, axis in zip(sources, outs, axes)
        ],
        sems,
    )


def take_halves(own, axes):
    shapes = []
    for w, axis in zip(own, axes):
        shape = list(w.shape)
        shape[axis] //= 2
        shapes.append(jax.ShapeDtypeStruct(tuple(shape), w.dtype))
    return pl.pallas_call(
        functools.partial(halves_kernel, axes),
        out_shape=shapes,
        in_specs=[pl.BlockSpec(memory_space=pltpu.HBM)] * 3,
        out_specs=[pl.BlockSpec(memory_space=pltpu.VMEM)] * 3,
        scratch_shapes=[pltpu.SemaphoreType.DMA((3,))],
        compiler_params=pltpu.CompilerParams(vmem_limit_bytes=8 * 2**20),
        cost_estimate=pl.CostEstimate(
            flops=0, bytes_accessed=2 * sum(w.size for w in own), transcendentals=0
        ),
    )(*own)


def store_kernel(axis, flags, own, came, other, out, sems):
    half = lax.axis_index("dp") % 2
    size = came.shape[axis]
    taken = flags[lax.axis_index("expert")] == 1

    @pl.when(taken)
    def _():
        run_copies(
            [
                (came, part_of(out, axis, half, size)),
                (other, part_of(out, axis, 1 - half, size)),
            ],
            sems,
        )

    @pl.when(jnp.logical_not(taken))
    def _():
        run_copies([(own, out)], sems)


def store(axis, flags, own, came, other):
    vmem = pl.BlockSpec(memory_space=pltpu.VMEM)
    return pl.pallas_call(
        functools.partial(store_kernel, axis),
        out_shape=jax.ShapeDtypeStruct(own.shape, own.dtype),
        in_specs=[pl.BlockSpec(memory_space=pltpu.SMEM)] + [vmem] * 3,
        out_specs=pl.BlockSpec(memory_space=pl.ANY),
        scratch_shapes=[pltpu.SemaphoreType.DMA((2,))],
        compiler_params=pltpu.CompilerParams(vmem_limit_bytes=8 * 2**20),
        cost_estimate=pl.CostEstimate(flops=0, bytes_accessed=4 * own.size, transcendentals=0),
    )(flags, own, came, other)


def after(value, *others):
    return lax.optimization_barrier((value, *others))[0]


def per_device(tokens, expert_ids, gate_probs, w_gate, w_up, w_down, placement, swap_flags):
    count = lax.axis_size("expert")
    half_axis = count // 2
    width = tokens.shape[1]
    own = (w_gate[0], w_up[0], w_down[0])
    trades = [(d, d ^ 1) for d in range(lax.axis_size("dp"))]
    pairs = [(d, d ^ half_axis) for d in range(count) if d % half_axis != 1]

    def send(value, bit, name):
        with jax.named_scope(name):
            return lax.ppermute(value, "expert", [(d, d ^ bit) for d in range(count)])

    def swap(value):
        with jax.named_scope("swap"):
            return lax.ppermute(value, "expert", pairs)

    def trade(value, name):
        with jax.named_scope(name):
            return lax.ppermute(value, "dp", trades)

    axes = (0, 0, 1)
    halves = take_halves(own, axes)
    near = [send(w, 1, "near") for w in own]
    x = [send(half, 2, "x_half") for half in halves[:2]]

    bits = []
    bit = half_axis
    while bit > 2:
        bits.append(bit)
        bit //= 2
    blocks = {0: after(pack_gates(tokens, expert_ids, gate_probs, count), *near)}
    for stage, bit in enumerate(bits):
        for i in sorted(blocks):
            blocks[i | 1 << stage] = send(blocks[i], bit, "tokens")
    rows = [blocks[i] for i in range(len(blocks))]
    x.append(send(after(halves[2], x[0], rows[2]), 2, "x_half"))

    z = [swap(halves[0])]
    z.append(swap(after(halves[1], z[0])))
    z.append(swap(after(halves[2], z[1])))
    y = [trade(x[0], "x_trade"), trade(x[1], "x_trade")]
    y.append(trade(after(x[2], z[0], rows[1]), "x_trade"))
    x_near = [send(part, 1, "x_near") for part in x]
    y_near = [send(part, 1, "x_near") for part in y[:2]]

    moved = [trade(after(z[0], y[2]), "swap_trade")]
    moved.append(trade(after(z[1], moved[0]), "swap_trade"))

    firsts = list(reversed(range(0, len(rows), 2)))
    bases = {}
    for first in firsts:
        bases[first] = run_experts(
            placement, (0, 1), rows[first : first + 2], [own, near], count, width
        )
    y_near.append(send(after(y[2], [bases[i] for i in firsts]), 1, "x_near"))
    parts = {}
    for first in firsts:
        sent = first >= len(rows) // 2
        parts[first], parts[first + 1] = run_experts(
            after(placement, z[1]) if sent else after(placement, moved[0]),
            (2, 3),
            rows[first : first + 2],
            [x + y, x_near + y_near],
            count,
            width,
            bases[first],
            sent,
        )
    for stage in reversed(range(len(bits))):
        for i in reversed(range(1 << stage)):
            part = parts[i | 1 << stage].astype(jnp.bfloat16)
            if stage == 0:
                part = after(part, moved[1])
            parts[i] = parts[i] + send(part, bits[stage], "sums").astype(jnp.float32)
    mixed = parts[0].astype(jnp.bfloat16)

    moved.append(trade(after(z[2], part), "swap_trade"))
    stored = [store(axis, swap_flags, *parts) for axis, *parts in zip(axes, own, z, moved)]
    stored = [w[None] for w in stored]
    return (mixed, *stored)


def solution(mesh):
    in_specs = (
        P(("dp", "expert"), None),
        P(("dp", "expert"), None),
        P(("dp", "expert"), None),
        P("expert", None, None),
        P("expert", None, None),
        P("expert", None, None),
        P(),
        P(),
    )
    out_specs = (
        P(("dp", "expert"), None),
        P(("dp", "expert"), None, None),
        P(("dp", "expert"), None, None),
        P(("dp", "expert"), None, None),
    )
    return jax.shard_map(
        per_device, mesh=mesh, in_specs=in_specs, out_specs=out_specs, check_vma=False
    )
```

```python
import functools

import jax
import jax.numpy as jnp
from jax import lax
from jax.experimental import pallas as pl
from jax.experimental.pallas import tpu as pltpu
from jax.sharding import PartitionSpec as P

LANES = 128
VMEM_LIMIT = 20 * 2**20


def split_parts(values):
    parts = []
    for _ in range(3):
        part = lax.reduce_precision(values, exponent_bits=8, mantissa_bits=7)
        parts.append(part.astype(jnp.bfloat16))
        values = values - part
    return parts


def pack_gates(tokens, expert_ids, gate_probs, count):
    experts = jnp.arange(count, dtype=jnp.int32)
    chosen = expert_ids[:, None, :] == experts[None, :, None]
    weights = jnp.sum(jnp.where(chosen, gate_probs[:, None, :], 0.0), axis=2)
    parts = jnp.concatenate(split_parts(weights), axis=1)
    parts = jnp.pad(parts, ((0, 0), (0, -parts.shape[1] % LANES)))
    return jnp.concatenate([tokens, parts], axis=1)


def dot(a, b):
    return jnp.dot(a, b, preferred_element_type=jnp.float32)


def token_weight(tail, expert, count):
    lane = lax.broadcasted_iota(jnp.int32, tail.shape, 1)
    mine = (lane % count == expert) & (lane < 3 * count)
    return jnp.sum(jnp.where(mine, tail.astype(jnp.float32), 0.0), axis=1, keepdims=True)


def activate(gate, up):
    return (gate / (1.0 + jnp.exp(-gate)) * up).astype(jnp.bfloat16)


def rounded(value):
    return value.astype(jnp.bfloat16).astype(jnp.float32)


def near_kernel(count, placement, *refs):
    rows, weights, outs, x = refs[:2], (refs[2:5], refs[5:8]), refs[8:10], refs[10]
    height, width = rows[0].shape[0], x.shape[1]
    me = lax.axis_index("expert")
    for i in range(2):
        x[i * height : (i + 1) * height, :] = rows[i][:, :width]
    totals = [0.0, 0.0]
    for flip, (g, u, d) in enumerate(weights):
        hidden = activate(dot(x[...], g[...]), dot(x[...], u[...]))
        value = rounded(dot(hidden, d[...]))
        for i in range(2):
            weight = token_weight(rows[i][:, width:], placement[me ^ flip], count)
            totals[i] = totals[i] + value[i * height : (i + 1) * height, :] * weight
    for i in range(2):
        outs[i][...] = totals[i]


def hidden_kernel(blocks, width, *refs):
    rows, weights, out, x = refs[:blocks], refs[blocks : blocks + 8], refs[blocks + 8], refs[blocks + 9]
    height = rows[0].shape[0]
    half = lax.axis_index("dp") % 2
    for first in range(0, blocks, 2):
        for i in range(2):
            x[i * height : (i + 1) * height, :] = rows[first + i][:, :width]
        for slot in range(2):
            ga, ua, gb, ub = weights[4 * slot : 4 * slot + 4]
            depth, ff = ga.shape
            at = pl.multiple_of(half * depth, depth)
            off = pl.multiple_of(depth - at, depth)
            xa, xb = x[:, pl.ds(at, depth)], x[:, pl.ds(off, depth)]
            gate = dot(xa, ga[...]) + dot(xb, gb[...])
            up = dot(xa, ua[...]) + dot(xb, ub[...])
            span = slice(first * height, (first + 2) * height)
            out[span, slot * ff : (slot + 1) * ff] = activate(gate, up)


def down_kernel(count, first, placement, *refs):
    rows, hidden, downs, base, outs = refs[:2], refs[2], refs[3:7], refs[7:9], refs[9:11]
    height, width = base[0].shape
    me = lax.axis_index("expert")
    far = lax.axis_size("expert") // 2
    half = lax.axis_index("dp") % 2
    weights = [
        [token_weight(r[:, width:], placement[me ^ far ^ slot], count) for slot in range(2)]
        for r in rows
    ]
    part, ff = downs[0].shape[1], downs[0].shape[0]
    at = pl.multiple_of(half * part, part)
    off = pl.multiple_of(part - at, part)
    for which, start in ((0, at), (1, off)):
        columns = pl.ds(start, part)
        totals = [base[i][:, columns] for i in range(2)]
        for slot in range(2):
            span = slice(first * height, (first + 2) * height)
            units = hidden[span, slot * ff : (slot + 1) * ff]
            value = rounded(dot(units, downs[2 * slot + which][...]))
            for i in range(2):
                totals[i] = totals[i] + value[i * height : (i + 1) * height, :] * weights[i][slot]
        for i in range(2):
            outs[i][:, columns] = totals[i].astype(outs[i].dtype)


def call(kernel, out_shape, args, scratch=(), scalars=0):
    vmem = pl.BlockSpec(memory_space=pltpu.VMEM)
    smem = pl.BlockSpec(memory_space=pltpu.SMEM)
    return pl.pallas_call(
        kernel,
        out_shape=out_shape,
        in_specs=[smem] * scalars + [vmem] * (len(args) - scalars),
        out_specs=jax.tree.map(lambda _: vmem, out_shape),
        scratch_shapes=list(scratch),
        compiler_params=pltpu.CompilerParams(vmem_limit_bytes=VMEM_LIMIT),
        cost_estimate=pl.CostEstimate(flops=0, bytes_accessed=2**20, transcendentals=0),
    )(*args)


def run_copies(copies, sems):
    copies = [pltpu.make_async_copy(a, b, sems.at[i]) for i, (a, b) in enumerate(copies)]
    for copy in copies:
        copy.start()
    for copy in copies:
        copy.wait()


def part_of(ref, axis, half, size):
    span = pl.ds(pl.multiple_of(half * size, size), size)
    return ref.at[span, :] if axis == 0 else ref.at[:, span]


def store_kernel(axis, flags, own, came, other, out, sems):
    half = lax.axis_index("dp") % 2
    size = came.shape[axis]
    taken = flags[lax.axis_index("expert")] == 1

    @pl.when(taken)
    def _():
        run_copies(
            [
                (came, part_of(out, axis, half, size)),
                (other, part_of(out, axis, 1 - half, size)),
            ],
            sems,
        )

    @pl.when(jnp.logical_not(taken))
    def _():
        run_copies([(own, out)], sems)


def store(axis, flags, own, came, other):
    vmem = pl.BlockSpec(memory_space=pltpu.VMEM)
    return pl.pallas_call(
        functools.partial(store_kernel, axis),
        out_shape=jax.ShapeDtypeStruct(own.shape, own.dtype),
        in_specs=[pl.BlockSpec(memory_space=pltpu.SMEM)] + [vmem] * 3,
        out_specs=pl.BlockSpec(memory_space=pl.ANY),
        scratch_shapes=[pltpu.SemaphoreType.DMA((2,))],
        compiler_params=pltpu.CompilerParams(vmem_limit_bytes=8 * 2**20),
        cost_estimate=pl.CostEstimate(flops=0, bytes_accessed=4 * own.size, transcendentals=0),
    )(flags, own, came, other)


def after(value, *others):
    return lax.optimization_barrier((value, *others))[0]


def per_device(tokens, expert_ids, gate_probs, w_gate, w_up, w_down, placement, swap_flags):
    count = lax.axis_size("expert")
    couple = lax.axis_index("dp") % 2
    half_axis = count // 2
    height, width = tokens.shape
    own = (w_gate[0], w_up[0], w_down[0])
    trades = [(d, d ^ 1) for d in range(lax.axis_size("dp"))]

    def send(value, bit, name):
        with jax.named_scope(name):
            return lax.ppermute(value, "expert", [(d, d ^ bit) for d in range(count)])

    def trade(value):
        with jax.named_scope("trade"):
            return lax.ppermute(value, "dp", trades)

    axes = (0, 0, 1)
    halves = []
    for w, axis in zip(own, axes):
        size = w.shape[axis] // 2
        halves.append(lax.dynamic_slice_in_dim(w, couple * size, size, axis=axis))
    z = [send(half, half_axis, "swap") for half in halves]
    near = [send(after(w, z[0], halves[2]), 1, "near") for w in own]

    bits = []
    bit = half_axis // 2
    while bit > 1:
        bits.append(bit)
        bit //= 2
    blocks = {0: pack_gates(tokens, expert_ids, gate_probs, count)}
    for stage, bit in enumerate(bits):
        for i in sorted(blocks):
            last = (i | 1 << stage) + 1 == 1 << len(bits)
            block = after(blocks[i], z[1]) if last else blocks[i]
            blocks[i | 1 << stage] = send(block, bit, "tokens")
    rows = [blocks[i] for i in range(len(blocks))]

    y = [trade(after(z[0], z[1], *rows[1:3])), trade(z[1])]
    z_near = [send(part, 1, "z_near") for part in z[:2]]

    scratch = [pltpu.VMEM((2 * height, width), jnp.bfloat16)]
    firsts = list(reversed(range(0, len(rows), 2)))
    base = {}
    for first in firsts:
        base[first] = call(
            functools.partial(near_kernel, count),
            [jax.ShapeDtypeStruct((height, width), jnp.float32)] * 2,
            [placement, *rows[first : first + 2], *own, *near],
            scratch,
            scalars=1,
        )
    lower = after(z[2], base)
    y.append(trade(lower))
    z_near.append(send(lower, 1, "z_near"))
    y_near = [send(after(part, lower), 1, "y_near") for part in y[:2]]
    ff = own[0].shape[1]
    hidden = call(
        functools.partial(hidden_kernel, len(rows), width),
        jax.ShapeDtypeStruct((len(rows) * height, 2 * ff), jnp.bfloat16),
        [*rows, *z[:2], *y[:2], *z_near[:2], *y_near[:2]],
        scratch,
    )
    y_near.append(send(after(y[2], hidden), 1, "y_near"))
    parts = {}
    for first in firsts:
        dtype = jnp.bfloat16 if first >= len(rows) // 2 else jnp.float32
        parts[first], parts[first + 1] = call(
            functools.partial(down_kernel, count, first),
            [jax.ShapeDtypeStruct((height, width), dtype)] * 2,
            [
                placement,
                *rows[first : first + 2],
                hidden,
                *(z[2], y[2], z_near[2], y_near[2]),
                *base[first],
            ],
            scalars=1,
        )
    for stage in reversed(range(len(bits))):
        for i in reversed(range(1 << stage)):
            part = parts[i | 1 << stage].astype(jnp.bfloat16)
            parts[i] = parts[i] + send(part, bits[stage], "sums").astype(jnp.float32)
    mixed = parts[0].astype(jnp.bfloat16)

    stored = [store(axis, swap_flags, *parts) for axis, *parts in zip(axes, own, z, y)]
    return (mixed, *(w[None] for w in stored))


def solution(mesh):
    in_specs = (
        P(("dp", "expert"), None),
        P(("dp", "expert"), None),
        P(("dp", "expert"), None),
        P("expert", None, None),
        P("expert", None, None),
        P("expert", None, None),
        P(),
        P(),
    )
    out_specs = (
        P(("dp", "expert"), None),
        P(("dp", "expert"), None, None),
        P(("dp", "expert"), None, None),
        P(("dp", "expert"), None, None),
    )
    return jax.shard_map(
        per_device, mesh=mesh, in_specs=in_specs, out_specs=out_specs, check_vma=False
    )
```

```python
import functools

import jax
import jax.numpy as jnp
from jax import lax
from jax.experimental import pallas as pl
from jax.experimental.pallas import tpu as pltpu
from jax.sharding import PartitionSpec as P

LANES = 128
VMEM_LIMIT = 20 * 2**20


def split_parts(values):
    parts = []
    for _ in range(3):
        part = lax.reduce_precision(values, exponent_bits=8, mantissa_bits=7)
        parts.append(part.astype(jnp.bfloat16))
        values = values - part
    return parts


def pack_gates(tokens, expert_ids, gate_probs, count):
    experts = jnp.arange(count, dtype=jnp.int32)
    chosen = expert_ids[:, None, :] == experts[None, :, None]
    weights = jnp.sum(jnp.where(chosen, gate_probs[:, None, :], 0.0), axis=2)
    parts = jnp.concatenate(split_parts(weights), axis=1)
    parts = jnp.pad(parts, ((0, 0), (0, -parts.shape[1] % LANES)))
    return jnp.concatenate([tokens, parts], axis=1)


def dot(a, b):
    return jnp.dot(a, b, preferred_element_type=jnp.float32)


def token_weight(tail, expert, count):
    lane = lax.broadcasted_iota(jnp.int32, tail.shape, 1)
    mine = (lane % count == expert) & (lane < 3 * count)
    return jnp.sum(jnp.where(mine, tail.astype(jnp.float32), 0.0), axis=1, keepdims=True)


def activate(gate, up):
    return (gate / (1.0 + jnp.exp(-gate)) * up).astype(jnp.bfloat16)


def rounded(value):
    return value.astype(jnp.bfloat16).astype(jnp.float32)


def near_kernel(count, placement, *refs):
    rows, weights, outs, x = refs[:2], (refs[2:5], refs[5:8]), refs[8:10], refs[10]
    height, width = rows[0].shape[0], x.shape[1]
    me = lax.axis_index("expert")
    for i in range(2):
        x[i * height : (i + 1) * height, :] = rows[i][:, :width]
    totals = [0.0, 0.0]
    for flip, (g, u, d) in enumerate(weights):
        hidden = activate(dot(x[...], g[...]), dot(x[...], u[...]))
        value = rounded(dot(hidden, d[...]))
        for i in range(2):
            weight = token_weight(rows[i][:, width:], placement[me ^ flip], count)
            totals[i] = totals[i] + value[i * height : (i + 1) * height, :] * weight
    for i in range(2):
        outs[i][...] = totals[i]


def hidden_kernel(blocks, width, *refs):
    rows, weights, out, x = refs[:blocks], refs[blocks : blocks + 8], refs[blocks + 8], refs[blocks + 9]
    height = rows[0].shape[0]
    half = lax.axis_index("dp") % 2
    for first in range(0, blocks, 2):
        for i in range(2):
            x[i * height : (i + 1) * height, :] = rows[first + i][:, :width]
        for slot in range(2):
            ga, ua, gb, ub = weights[4 * slot : 4 * slot + 4]
            depth, ff = ga.shape
            at = pl.multiple_of(half * depth, depth)
            off = pl.multiple_of(depth - at, depth)
            xa, xb = x[:, pl.ds(at, depth)], x[:, pl.ds(off, depth)]
            gate = dot(xa, ga[...]) + dot(xb, gb[...])
            up = dot(xa, ua[...]) + dot(xb, ub[...])
            span = slice(first * height, (first + 2) * height)
            out[span, slot * ff : (slot + 1) * ff] = activate(gate, up)


def down_kernel(count, first, placement, *refs):
    rows, hidden, downs, base, outs = refs[:2], refs[2], refs[3:7], refs[7:9], refs[9:11]
    height, width = base[0].shape
    me = lax.axis_index("expert")
    far = lax.axis_size("expert") // 2
    half = lax.axis_index("dp") % 2
    weights = [
        [token_weight(r[:, width:], placement[me ^ far ^ slot], count) for slot in range(2)]
        for r in rows
    ]
    part, ff = downs[0].shape[1], downs[0].shape[0]
    at = pl.multiple_of(half * part, part)
    off = pl.multiple_of(part - at, part)
    for which, start in ((0, at), (1, off)):
        columns = pl.ds(start, part)
        totals = [base[i][:, columns] for i in range(2)]
        for slot in range(2):
            span = slice(first * height, (first + 2) * height)
            units = hidden[span, slot * ff : (slot + 1) * ff]
            value = rounded(dot(units, downs[2 * slot + which][...]))
            for i in range(2):
                totals[i] = totals[i] + value[i * height : (i + 1) * height, :] * weights[i][slot]
        for i in range(2):
            outs[i][:, columns] = totals[i].astype(outs[i].dtype)


def call(kernel, out_shape, args, scratch=(), scalars=0):
    vmem = pl.BlockSpec(memory_space=pltpu.VMEM)
    smem = pl.BlockSpec(memory_space=pltpu.SMEM)
    return pl.pallas_call(
        kernel,
        out_shape=out_shape,
        in_specs=[smem] * scalars + [vmem] * (len(args) - scalars),
        out_specs=jax.tree.map(lambda _: vmem, out_shape),
        scratch_shapes=list(scratch),
        compiler_params=pltpu.CompilerParams(vmem_limit_bytes=VMEM_LIMIT),
        cost_estimate=pl.CostEstimate(flops=0, bytes_accessed=2**20, transcendentals=0),
    )(*args)


def run_copies(copies, sems):
    copies = [pltpu.make_async_copy(a, b, sems.at[i]) for i, (a, b) in enumerate(copies)]
    for copy in copies:
        copy.start()
    for copy in copies:
        copy.wait()


def part_of(ref, axis, half, size):
    span = pl.ds(pl.multiple_of(half * size, size), size)
    return ref.at[span, :] if axis == 0 else ref.at[:, span]


def store_kernel(axis, flags, own, came, other, out, sems):
    half = lax.axis_index("dp") % 2
    size = came.shape[axis]
    taken = flags[lax.axis_index("expert")] == 1

    @pl.when(taken)
    def _():
        run_copies(
            [
                (came, part_of(out, axis, half, size)),
                (other, part_of(out, axis, 1 - half, size)),
            ],
            sems,
        )

    @pl.when(jnp.logical_not(taken))
    def _():
        run_copies([(own, out)], sems)


def store(axis, flags, own, came, other):
    vmem = pl.BlockSpec(memory_space=pltpu.VMEM)
    return pl.pallas_call(
        functools.partial(store_kernel, axis),
        out_shape=jax.ShapeDtypeStruct(own.shape, own.dtype),
        in_specs=[pl.BlockSpec(memory_space=pltpu.SMEM)] + [vmem] * 3,
        out_specs=pl.BlockSpec(memory_space=pl.ANY),
        scratch_shapes=[pltpu.SemaphoreType.DMA((2,))],
        compiler_params=pltpu.CompilerParams(vmem_limit_bytes=8 * 2**20),
        cost_estimate=pl.CostEstimate(flops=0, bytes_accessed=4 * own.size, transcendentals=0),
    )(flags, own, came, other)


def after(value, *others):
    return lax.optimization_barrier((value, *others))[0]


def per_device(tokens, expert_ids, gate_probs, w_gate, w_up, w_down, placement, swap_flags):
    count = lax.axis_size("expert")
    couple = lax.axis_index("dp") % 2
    half_axis = count // 2
    height, width = tokens.shape
    own = (w_gate[0], w_up[0], w_down[0])
    trades = [(d, d ^ 1) for d in range(lax.axis_size("dp"))]

    def send(value, bit, name):
        with jax.named_scope(name):
            return lax.ppermute(value, "expert", [(d, d ^ bit) for d in range(count)])

    def trade(value):
        with jax.named_scope("trade"):
            return lax.ppermute(value, "dp", trades)

    axes = (0, 0, 1)
    halves = []
    for w, axis in zip(own, axes):
        size = w.shape[axis] // 2
        halves.append(lax.dynamic_slice_in_dim(w, couple * size, size, axis=axis))
    z = [send(half, half_axis, "swap") for half in halves]
    near = [send(w, 1, "near") for w in own]

    bits = []
    bit = half_axis // 2
    while bit > 1:
        bits.append(bit)
        bit //= 2
    blocks = {0: after(pack_gates(tokens, expert_ids, gate_probs, count), *near)}
    for stage, bit in enumerate(bits):
        for i in sorted(blocks):
            blocks[i | 1 << stage] = send(blocks[i], bit, "tokens")
    rows = [blocks[i] for i in range(len(blocks))]

    y = [trade(after(z[0], z[1])), trade(z[1])]
    z_near = [send(part, 1, "z_near") for part in z[:2]]

    scratch = [pltpu.VMEM((2 * height, width), jnp.bfloat16)]
    firsts = list(reversed(range(0, len(rows), 2)))
    base = {}
    for first in firsts:
        base[first] = call(
            functools.partial(near_kernel, count),
            [jax.ShapeDtypeStruct((height, width), jnp.float32)] * 2,
            [placement, *rows[first : first + 2], *own, *near],
            scratch,
            scalars=1,
        )
    lower = after(z[2], base)
    y.append(trade(lower))
    z_near.append(send(lower, 1, "z_near"))
    y_near = [send(after(part, z[2], base), 1, "y_near") for part in y[:2]]
    ff = own[0].shape[1]
    hidden = call(
        functools.partial(hidden_kernel, len(rows), width),
        jax.ShapeDtypeStruct((len(rows) * height, 2 * ff), jnp.bfloat16),
        [*rows, *z[:2], *y[:2], *z_near[:2], *y_near[:2]],
        scratch,
    )
    y_near.append(send(after(y[2], hidden), 1, "y_near"))
    parts = {}
    for first in firsts:
        dtype = jnp.bfloat16 if first >= len(rows) // 2 else jnp.float32
        parts[first], parts[first + 1] = call(
            functools.partial(down_kernel, count, first),
            [jax.ShapeDtypeStruct((height, width), dtype)] * 2,
            [
                placement,
                *rows[first : first + 2],
                hidden,
                *(z[2], y[2], z_near[2], y_near[2]),
                *base[first],
            ],
            scalars=1,
        )
    for stage in reversed(range(len(bits))):
        for i in reversed(range(1 << stage)):
            part = parts[i | 1 << stage].astype(jnp.bfloat16)
            parts[i] = parts[i] + send(part, bits[stage], "sums").astype(jnp.float32)
    mixed = parts[0].astype(jnp.bfloat16)

    stored = [store(axis, swap_flags, *parts) for axis, *parts in zip(axes, own, z, y)]
    return (mixed, *(w[None] for w in stored))


def solution(mesh):
    in_specs = (
        P(("dp", "expert"), None),
        P(("dp", "expert"), None),
        P(("dp", "expert"), None),
        P("expert", None, None),
        P("expert", None, None),
        P("expert", None, None),
        P(),
        P(),
    )
    out_specs = (
        P(("dp", "expert"), None),
        P(("dp", "expert"), None, None),
        P(("dp", "expert"), None, None),
        P(("dp", "expert"), None, None),
    )
    return jax.shard_map(
        per_device, mesh=mesh, in_specs=in_specs, out_specs=out_specs, check_vma=False
    )
```

```python
import functools

import jax
import jax.numpy as jnp
from jax import lax
from jax.experimental import pallas as pl
from jax.experimental.pallas import tpu as pltpu
from jax.sharding import PartitionSpec as P

LANES = 128
VMEM_LIMIT = 20 * 2**20


def split_parts(values):
    parts = []
    for _ in range(3):
        part = lax.reduce_precision(values, exponent_bits=8, mantissa_bits=7)
        parts.append(part.astype(jnp.bfloat16))
        values = values - part
    return parts


def pack_gates(tokens, expert_ids, gate_probs, count):
    experts = jnp.arange(count, dtype=jnp.int32)
    chosen = expert_ids[:, None, :] == experts[None, :, None]
    weights = jnp.sum(jnp.where(chosen, gate_probs[:, None, :], 0.0), axis=2)
    parts = jnp.concatenate(split_parts(weights), axis=1)
    parts = jnp.pad(parts, ((0, 0), (0, -parts.shape[1] % LANES)))
    return jnp.concatenate([tokens, parts], axis=1)


def dot(a, b):
    return jnp.dot(a, b, preferred_element_type=jnp.float32)


def token_weight(tail, expert, count):
    lane = lax.broadcasted_iota(jnp.int32, tail.shape, 1)
    mine = (lane % count == expert) & (lane < 3 * count)
    return jnp.sum(jnp.where(mine, tail.astype(jnp.float32), 0.0), axis=1, keepdims=True)


def activate(gate, up):
    return (gate / (1.0 + jnp.exp(-gate)) * up).astype(jnp.bfloat16)


def rounded(value):
    return value.astype(jnp.bfloat16).astype(jnp.float32)


def near_kernel(count, placement, *refs):
    rows, weights, outs, x = refs[:2], (refs[2:5], refs[5:8]), refs[8:10], refs[10]
    height, width = rows[0].shape[0], x.shape[1]
    me = lax.axis_index("expert")
    for i in range(2):
        x[i * height : (i + 1) * height, :] = rows[i][:, :width]
    totals = [0.0, 0.0]
    for flip, (g, u, d) in enumerate(weights):
        hidden = activate(dot(x[...], g[...]), dot(x[...], u[...]))
        value = rounded(dot(hidden, d[...]))
        for i in range(2):
            weight = token_weight(rows[i][:, width:], placement[me ^ flip], count)
            totals[i] = totals[i] + value[i * height : (i + 1) * height, :] * weight
    for i in range(2):
        outs[i][...] = totals[i]


def hidden_kernel(blocks, width, *refs):
    rows, weights, out, x = refs[:blocks], refs[blocks : blocks + 8], refs[blocks + 8], refs[blocks + 9]
    height = rows[0].shape[0]
    half = lax.axis_index("dp") % 2
    for first in range(0, blocks, 2):
        for i in range(2):
            x[i * height : (i + 1) * height, :] = rows[first + i][:, :width]
        for slot in range(2):
            ga, ua, gb, ub = weights[4 * slot : 4 * slot + 4]
            depth, ff = ga.shape
            at = pl.multiple_of(half * depth, depth)
            off = pl.multiple_of(depth - at, depth)
            xa, xb = x[:, pl.ds(at, depth)], x[:, pl.ds(off, depth)]
            gate = dot(xa, ga[...]) + dot(xb, gb[...])
            up = dot(xa, ua[...]) + dot(xb, ub[...])
            span = slice(first * height, (first + 2) * height)
            out[span, slot * ff : (slot + 1) * ff] = activate(gate, up)


def down_kernel(count, first, placement, *refs):
    rows, hidden, downs, base, outs = refs[:2], refs[2], refs[3:7], refs[7:9], refs[9:11]
    height, width = base[0].shape
    me = lax.axis_index("expert")
    far = lax.axis_size("expert") // 2
    half = lax.axis_index("dp") % 2
    weights = [
        [token_weight(r[:, width:], placement[me ^ far ^ slot], count) for slot in range(2)]
        for r in rows
    ]
    part, ff = downs[0].shape[1], downs[0].shape[0]
    at = pl.multiple_of(half * part, part)
    off = pl.multiple_of(part - at, part)
    for which, start in ((0, at), (1, off)):
        columns = pl.ds(start, part)
        totals = [base[i][:, columns] for i in range(2)]
        for slot in range(2):
            span = slice(first * height, (first + 2) * height)
            units = hidden[span, slot * ff : (slot + 1) * ff]
            value = rounded(dot(units, downs[2 * slot + which][...]))
            for i in range(2):
                totals[i] = totals[i] + value[i * height : (i + 1) * height, :] * weights[i][slot]
        for i in range(2):
            outs[i][:, columns] = totals[i].astype(outs[i].dtype)


def call(kernel, out_shape, args, scratch=(), scalars=0):
    vmem = pl.BlockSpec(memory_space=pltpu.VMEM)
    smem = pl.BlockSpec(memory_space=pltpu.SMEM)
    return pl.pallas_call(
        kernel,
        out_shape=out_shape,
        in_specs=[smem] * scalars + [vmem] * (len(args) - scalars),
        out_specs=jax.tree.map(lambda _: vmem, out_shape),
        scratch_shapes=list(scratch),
        compiler_params=pltpu.CompilerParams(vmem_limit_bytes=VMEM_LIMIT),
        cost_estimate=pl.CostEstimate(flops=0, bytes_accessed=2**20, transcendentals=0),
    )(*args)


def run_copies(copies, sems):
    copies = [pltpu.make_async_copy(a, b, sems.at[i]) for i, (a, b) in enumerate(copies)]
    for copy in copies:
        copy.start()
    for copy in copies:
        copy.wait()


def part_of(ref, axis, half, size):
    span = pl.ds(pl.multiple_of(half * size, size), size)
    return ref.at[span, :] if axis == 0 else ref.at[:, span]


def store_kernel(axis, flags, own, came, other, out, sems):
    half = lax.axis_index("dp") % 2
    size = came.shape[axis]
    taken = flags[lax.axis_index("expert")] == 1

    @pl.when(taken)
    def _():
        run_copies(
            [
                (came, part_of(out, axis, half, size)),
                (other, part_of(out, axis, 1 - half, size)),
            ],
            sems,
        )

    @pl.when(jnp.logical_not(taken))
    def _():
        run_copies([(own, out)], sems)


def store(axis, flags, own, came, other):
    vmem = pl.BlockSpec(memory_space=pltpu.VMEM)
    return pl.pallas_call(
        functools.partial(store_kernel, axis),
        out_shape=jax.ShapeDtypeStruct(own.shape, own.dtype),
        in_specs=[pl.BlockSpec(memory_space=pltpu.SMEM)] + [vmem] * 3,
        out_specs=pl.BlockSpec(memory_space=pl.ANY),
        scratch_shapes=[pltpu.SemaphoreType.DMA((2,))],
        compiler_params=pltpu.CompilerParams(vmem_limit_bytes=8 * 2**20),
        cost_estimate=pl.CostEstimate(flops=0, bytes_accessed=4 * own.size, transcendentals=0),
    )(flags, own, came, other)


def after(value, *others):
    return lax.optimization_barrier((value, *others))[0]


def per_device(tokens, expert_ids, gate_probs, w_gate, w_up, w_down, placement, swap_flags):
    count = lax.axis_size("expert")
    couple = lax.axis_index("dp") % 2
    half_axis = count // 2
    height, width = tokens.shape
    own = (w_gate[0], w_up[0], w_down[0])
    trades = [(d, d ^ 1) for d in range(lax.axis_size("dp"))]

    def send(value, bit, name):
        with jax.named_scope(name):
            return lax.ppermute(value, "expert", [(d, d ^ bit) for d in range(count)])

    def trade(value):
        with jax.named_scope("trade"):
            return lax.ppermute(value, "dp", trades)

    axes = (0, 0, 1)
    halves = []
    for w, axis in zip(own, axes):
        size = w.shape[axis] // 2
        halves.append(lax.dynamic_slice_in_dim(w, couple * size, size, axis=axis))
    z = [send(halves[0], half_axis, "swap")]
    bits = []
    bit = half_axis // 2
    while bit > 1:
        bits.append(bit)
        bit //= 2
    blocks = {0: pack_gates(tokens, expert_ids, gate_probs, count)}
    for stage, bit in enumerate(bits):
        for i in sorted(blocks):
            blocks[i | 1 << stage] = send(blocks[i], bit, "tokens")
    rows = [blocks[i] for i in range(len(blocks))]

    z.append(send(after(halves[1], z[0], halves[2], *rows[1:-1]), half_axis, "swap"))
    y = [trade(z[0])]
    z.append(send(after(halves[2], z[1], y[0], *rows), half_axis, "swap"))
    y.append(trade(z[1]))
    near = [send(after(w, z[0]), 1, "near") for w in own]
    z_near = [send(part, 1, "z_near") for part in z[:2]]
    y_near = [send(y[0], 1, "y_near")]

    scratch = [pltpu.VMEM((2 * height, width), jnp.bfloat16)]
    firsts = list(reversed(range(0, len(rows), 2)))
    base = {}
    for first in firsts:
        base[first] = call(
            functools.partial(near_kernel, count),
            [jax.ShapeDtypeStruct((height, width), jnp.float32)] * 2,
            [placement, *rows[first : first + 2], *own, *near],
            scratch,
            scalars=1,
        )
    lower = after(z[2], base)
    y.append(trade(lower))
    z_near.append(send(lower, 1, "z_near"))
    y_near.append(send(after(y[1], lower), 1, "y_near"))
    ff = own[0].shape[1]
    hidden = call(
        functools.partial(hidden_kernel, len(rows), width),
        jax.ShapeDtypeStruct((len(rows) * height, 2 * ff), jnp.bfloat16),
        [*rows, *z[:2], *y[:2], *z_near[:2], *y_near[:2]],
        scratch,
    )
    y_near.append(send(after(y[2], hidden), 1, "y_near"))
    parts = {}
    for first in firsts:
        dtype = jnp.bfloat16 if first >= len(rows) // 2 else jnp.float32
        parts[first], parts[first + 1] = call(
            functools.partial(down_kernel, count, first),
            [jax.ShapeDtypeStruct((height, width), dtype)] * 2,
            [
                placement,
                *rows[first : first + 2],
                hidden,
                *(z[2], y[2], z_near[2], y_near[2]),
                *base[first],
            ],
            scalars=1,
        )
    for stage in reversed(range(len(bits))):
        for i in reversed(range(1 << stage)):
            part = parts[i | 1 << stage].astype(jnp.bfloat16)
            parts[i] = parts[i] + send(part, bits[stage], "sums").astype(jnp.float32)
    mixed = parts[0].astype(jnp.bfloat16)

    stored = [store(axis, swap_flags, *parts) for axis, *parts in zip(axes, own, z, y)]
    return (mixed, *(w[None] for w in stored))


def solution(mesh):
    in_specs = (
        P(("dp", "expert"), None),
        P(("dp", "expert"), None),
        P(("dp", "expert"), None),
        P("expert", None, None),
        P("expert", None, None),
        P("expert", None, None),
        P(),
        P(),
    )
    out_specs = (
        P(("dp", "expert"), None),
        P(("dp", "expert"), None, None),
        P(("dp", "expert"), None, None),
        P(("dp", "expert"), None, None),
    )
    return jax.shard_map(
        per_device, mesh=mesh, in_specs=in_specs, out_specs=out_specs, check_vma=False
    )
```

```python
import functools

import jax
import jax.numpy as jnp
from jax import lax
from jax.experimental import pallas as pl
from jax.experimental.pallas import tpu as pltpu
from jax.sharding import PartitionSpec as P

LANES = 128
VMEM_LIMIT = 20 * 2**20


def split_parts(values):
    parts = []
    for _ in range(3):
        part = lax.reduce_precision(values, exponent_bits=8, mantissa_bits=7)
        parts.append(part.astype(jnp.bfloat16))
        values = values - part
    return parts


def pack_gates(tokens, expert_ids, gate_probs, count):
    experts = jnp.arange(count, dtype=jnp.int32)
    chosen = expert_ids[:, None, :] == experts[None, :, None]
    weights = jnp.sum(jnp.where(chosen, gate_probs[:, None, :], 0.0), axis=2)
    parts = jnp.concatenate(split_parts(weights), axis=1)
    parts = jnp.pad(parts, ((0, 0), (0, -parts.shape[1] % LANES)))
    return jnp.concatenate([tokens, parts], axis=1)


def dot(a, b):
    return jnp.dot(a, b, preferred_element_type=jnp.float32)


def token_weight(tail, expert, count):
    lane = lax.broadcasted_iota(jnp.int32, tail.shape, 1)
    mine = (lane % count == expert) & (lane < 3 * count)
    return jnp.sum(jnp.where(mine, tail.astype(jnp.float32), 0.0), axis=1, keepdims=True)


def activate(gate, up):
    return (gate / (1.0 + jnp.exp(-gate)) * up).astype(jnp.bfloat16)


def rounded(value):
    return value.astype(jnp.bfloat16).astype(jnp.float32)


def near_kernel(count, placement, *refs):
    rows, weights, outs, x = refs[:2], (refs[2:5], refs[5:8]), refs[8:10], refs[10]
    height, width = rows[0].shape[0], x.shape[1]
    me = lax.axis_index("expert")
    for i in range(2):
        x[i * height : (i + 1) * height, :] = rows[i][:, :width]
    totals = [0.0, 0.0]
    for flip, (g, u, d) in enumerate(weights):
        hidden = activate(dot(x[...], g[...]), dot(x[...], u[...]))
        value = rounded(dot(hidden, d[...]))
        for i in range(2):
            weight = token_weight(rows[i][:, width:], placement[me ^ flip], count)
            totals[i] = totals[i] + value[i * height : (i + 1) * height, :] * weight
    for i in range(2):
        outs[i][...] = totals[i]


def hidden_kernel(blocks, width, *refs):
    rows, weights, out, x = refs[:blocks], refs[blocks : blocks + 4], refs[blocks + 4], refs[blocks + 5]
    height = rows[0].shape[0]
    half = lax.axis_index("dp") % 2
    for first in range(0, blocks, 2):
        for i in range(2):
            x[i * height : (i + 1) * height, :] = rows[first + i][:, :width]
        for slot in range(2):
            own, other = weights[2 * slot : 2 * slot + 2]
            depth, ff = own.shape[0] // 2, own.shape[1]
            at = pl.multiple_of(half * depth, depth)
            off = pl.multiple_of(depth - at, depth)
            xa, xb = x[:, pl.ds(at, depth)], x[:, pl.ds(off, depth)]
            gate = dot(xa, own[:depth, :]) + dot(xb, other[:depth, :])
            up = dot(xa, own[depth:, :]) + dot(xb, other[depth:, :])
            span = slice(first * height, (first + 2) * height)
            out[span, slot * ff : (slot + 1) * ff] = activate(gate, up)


def down_kernel(count, first, flip, placement, *refs):
    rows, hidden, downs, base, outs = refs[:2], refs[2], refs[3:5], refs[5:7], refs[7:9]
    height, part = outs[0].shape
    ff = downs[0].shape[0]
    me = lax.axis_index("expert")
    far = lax.axis_size("expert") // 2
    half = (lax.axis_index("dp") + flip) % 2
    columns = pl.ds(pl.multiple_of(half * part, part), part)
    totals = [base[i][:, columns] for i in range(2)]
    for slot, down in enumerate(downs):
        span = slice(first * height, (first + 2) * height)
        value = rounded(dot(hidden[span, slot * ff : (slot + 1) * ff], down[...]))
        for i in range(2):
            weight = token_weight(rows[i][:, base[0].shape[1]:], placement[me ^ far ^ slot], count)
            totals[i] = totals[i] + value[i * height : (i + 1) * height, :] * weight
    for i in range(2):
        outs[i][...] = totals[i].astype(outs[i].dtype)


def call(kernel, out_shape, args, scratch=(), scalars=0):
    vmem = pl.BlockSpec(memory_space=pltpu.VMEM)
    smem = pl.BlockSpec(memory_space=pltpu.SMEM)
    return pl.pallas_call(
        kernel,
        out_shape=out_shape,
        in_specs=[smem] * scalars + [vmem] * (len(args) - scalars),
        out_specs=jax.tree.map(lambda _: vmem, out_shape),
        scratch_shapes=list(scratch),
        compiler_params=pltpu.CompilerParams(vmem_limit_bytes=VMEM_LIMIT),
        cost_estimate=pl.CostEstimate(flops=0, bytes_accessed=0, transcendentals=0),
    )(*args)


def run_copies(copies, sems):
    copies = [pltpu.make_async_copy(a, b, sems.at[i]) for i, (a, b) in enumerate(copies)]
    for copy in copies:
        copy.start()
    for copy in copies:
        copy.wait()


def part_of(ref, axis, half, size):
    span = pl.ds(pl.multiple_of(half * size, size), size)
    return ref.at[span, :] if axis == 0 else ref.at[:, span]


def store_kernel(axis, first, flags, own, came, other, out, sems):
    half = lax.axis_index("dp") % 2
    size = out.shape[axis] // 2
    taken = flags[lax.axis_index("expert")] == 1

    @pl.when(taken)
    def _():
        if axis == 0:
            parts = [ref.at[pl.ds(first, size), :] for ref in (came, other)]
        else:
            parts = [came, other]
        run_copies(
            [
                (parts[0], part_of(out, axis, half, size)),
                (parts[1], part_of(out, axis, 1 - half, size)),
            ],
            sems,
        )

    @pl.when(jnp.logical_not(taken))
    def _():
        run_copies([(own, out)], sems)


def store(axis, first, flags, own, came, other):
    vmem = pl.BlockSpec(memory_space=pltpu.VMEM)
    return pl.pallas_call(
        functools.partial(store_kernel, axis, first),
        out_shape=jax.ShapeDtypeStruct(own.shape, own.dtype),
        in_specs=[pl.BlockSpec(memory_space=pltpu.SMEM)] + [vmem] * 3,
        out_specs=pl.BlockSpec(memory_space=pl.ANY),
        scratch_shapes=[pltpu.SemaphoreType.DMA((2,))],
        compiler_params=pltpu.CompilerParams(vmem_limit_bytes=8 * 2**20),
        cost_estimate=pl.CostEstimate(flops=0, bytes_accessed=0, transcendentals=0),
    )(flags, own, came, other)


def after(value, *others):
    return lax.optimization_barrier((value, *others))[0]


def per_device(tokens, expert_ids, gate_probs, w_gate, w_up, w_down, placement, swap_flags):
    count = lax.axis_size("expert")
    couple = lax.axis_index("dp") % 2
    half_axis = count // 2
    height, width = tokens.shape
    own = (w_gate[0], w_up[0], w_down[0])
    ff = own[0].shape[1]
    trades = [(d, d ^ 1) for d in range(lax.axis_size("dp"))]

    def send(value, bit, name):
        with jax.named_scope(name):
            return lax.ppermute(value, "expert", [(d, d ^ bit) for d in range(count)])

    def trade(value):
        with jax.named_scope("trade"):
            return lax.ppermute(value, "dp", trades)

    depth, part = own[0].shape[0] // 2, width // 2

    def half_of(first, second):
        return jnp.where(couple == 0, first, second)

    upper = half_of(
        jnp.concatenate([own[0][:depth], own[1][:depth]], axis=0),
        jnp.concatenate([own[0][depth:], own[1][depth:]], axis=0),
    )
    lower = half_of(own[2][:, :part], own[2][:, part:])

    bits = []
    bit = half_axis // 2
    while bit > 1:
        bits.append(bit)
        bit //= 2
    blocks = {0: pack_gates(tokens, expert_ids, gate_probs, count)}
    for stage, bit in enumerate(bits):
        for i in sorted(blocks):
            blocks[i | 1 << stage] = send(blocks[i], bit, "tokens")
    rows = [blocks[i] for i in range(len(blocks))]

    z_upper = send(upper, half_axis, "swap")
    z_lower = send(after(lower, z_upper, *rows), half_axis, "swap")
    y_upper = trade(after(z_upper, *rows))
    near = [send(after(w, lower), 1, "near") for w in own]

    firsts = list(reversed(range(0, len(rows), 2)))
    scratch = [pltpu.VMEM((2 * height, width), jnp.bfloat16)]
    base = {}
    for first in firsts:
        base[first] = call(
            functools.partial(near_kernel, count),
            [jax.ShapeDtypeStruct((height, width), jnp.float32)] * 2,
            [placement, *rows[first : first + 2], *own, *near],
            scratch,
            scalars=1,
        )

    arrived = after(z_lower, base)
    y_lower = trade(arrived)
    z_near = [send(z_upper, 1, "z_near"), send(arrived, 1, "z_near")]
    y_near = [send(after(y_upper, arrived), 1, "y_near")]
    hidden = call(
        functools.partial(hidden_kernel, len(rows), width),
        jax.ShapeDtypeStruct((len(rows) * height, 2 * ff), jnp.bfloat16),
        [*rows, z_upper, y_upper, z_near[0], y_near[0]],
        scratch,
    )

    def far_sums(flip, downs):
        parts = {}
        for first in firsts:
            dtype = jnp.bfloat16 if first >= len(rows) // 2 else jnp.float32
            parts[first], parts[first + 1] = call(
                functools.partial(down_kernel, count, first, flip),
                [jax.ShapeDtypeStruct((height, downs[0].shape[1]), dtype)] * 2,
                [placement, *rows[first : first + 2], hidden, *downs, *base[first]],
                scalars=1,
            )
        return parts

    def collect(parts, stages, *others):
        for stage in stages:
            for i in reversed(range(1 << stage)):
                part = parts[i | 1 << stage].astype(jnp.bfloat16)
                came = after(send(part, bits[stage], "sums"), *others)
                parts[i] = parts[i] + came.astype(jnp.float32)
        return parts[0].astype(jnp.bfloat16)

    stages = list(reversed(range(len(bits))))
    parts = far_sums(0, [arrived, z_near[1]])
    flags = after(swap_flags, parts)
    stored = [
        store(0, 0, flags, own[0], z_upper, y_upper),
        store(0, depth, flags, own[1], z_upper, y_upper),
    ]
    landed = after(y_lower, stored)
    collect(parts, stages[:1], landed)
    y_near.append(send(after(landed, parts), 1, "y_near"))
    last_parts = far_sums(1, [landed, y_near[1]])
    stored.append(store(1, 0, after(swap_flags, last_parts), own[2], z_lower, y_lower))
    parts = after(parts, last_parts[firsts[0]])
    mixed = [collect(parts, stages[1:]), collect(last_parts, stages)]
    mixed = half_of(jnp.concatenate(mixed, axis=1), jnp.concatenate(mixed[::-1], axis=1))
    return (mixed, *(w[None] for w in stored))


def solution(mesh):
    in_specs = (
        P(("dp", "expert"), None),
        P(("dp", "expert"), None),
        P(("dp", "expert"), None),
        P("expert", None, None),
        P("expert", None, None),
        P("expert", None, None),
        P(),
        P(),
    )
    out_specs = (
        P(("dp", "expert"), None),
        P(("dp", "expert"), None, None),
        P(("dp", "expert"), None, None),
        P(("dp", "expert"), None, None),
    )
    return jax.shard_map(
        per_device, mesh=mesh, in_specs=in_specs, out_specs=out_specs, check_vma=False
    )
```

```python
import functools

import jax
import jax.numpy as jnp
from jax import lax
from jax.experimental import pallas as pl
from jax.experimental.pallas import tpu as pltpu
from jax.sharding import PartitionSpec as P

LANES = 128
VMEM_LIMIT = 20 * 2**20


def split_parts(values):
    parts = []
    for _ in range(3):
        part = lax.reduce_precision(values, exponent_bits=8, mantissa_bits=7)
        parts.append(part.astype(jnp.bfloat16))
        values = values - part
    return parts


def pack_gates(tokens, expert_ids, gate_probs, count):
    experts = jnp.arange(count, dtype=jnp.int32)
    chosen = expert_ids[:, None, :] == experts[None, :, None]
    weights = jnp.sum(jnp.where(chosen, gate_probs[:, None, :], 0.0), axis=2)
    parts = jnp.concatenate(split_parts(weights), axis=1)
    parts = jnp.pad(parts, ((0, 0), (0, -parts.shape[1] % LANES)))
    return jnp.concatenate([tokens, parts], axis=1)


def dot(a, b):
    return jnp.dot(a, b, preferred_element_type=jnp.float32)


def token_weight(tail, expert, count):
    lane = lax.broadcasted_iota(jnp.int32, tail.shape, 1)
    mine = (lane % count == expert) & (lane < 3 * count)
    return jnp.sum(jnp.where(mine, tail.astype(jnp.float32), 0.0), axis=1, keepdims=True)


def activate(gate, up):
    return (gate / (1.0 + jnp.exp(-gate)) * up).astype(jnp.bfloat16)


def rounded(value):
    return value.astype(jnp.bfloat16).astype(jnp.float32)


def near_kernel(count, placement, *refs):
    rows, weights, outs, x = refs[:2], (refs[2:5], refs[5:8]), refs[8:10], refs[10]
    height, width = rows[0].shape[0], x.shape[1]
    me = lax.axis_index("expert")
    for i in range(2):
        x[i * height : (i + 1) * height, :] = rows[i][:, :width]
    totals = [0.0, 0.0]
    for flip, (g, u, d) in enumerate(weights):
        hidden = activate(dot(x[...], g[...]), dot(x[...], u[...]))
        value = rounded(dot(hidden, d[...]))
        for i in range(2):
            weight = token_weight(rows[i][:, width:], placement[me ^ flip], count)
            totals[i] = totals[i] + value[i * height : (i + 1) * height, :] * weight
    for i in range(2):
        outs[i][...] = totals[i]


def hidden_kernel(blocks, width, *refs):
    rows, weights, out, x = refs[:blocks], refs[blocks : blocks + 4], refs[blocks + 4], refs[blocks + 5]
    height = rows[0].shape[0]
    half = lax.axis_index("dp") % 2
    for first in range(0, blocks, 2):
        for i in range(2):
            x[i * height : (i + 1) * height, :] = rows[first + i][:, :width]
        for slot in range(2):
            own, other = weights[2 * slot : 2 * slot + 2]
            depth, ff = own.shape[0] // 2, own.shape[1]
            at = pl.multiple_of(half * depth, depth)
            off = pl.multiple_of(depth - at, depth)
            xa, xb = x[:, pl.ds(at, depth)], x[:, pl.ds(off, depth)]
            gate = dot(xa, own[:depth, :]) + dot(xb, other[:depth, :])
            up = dot(xa, own[depth:, :]) + dot(xb, other[depth:, :])
            span = slice(first * height, (first + 2) * height)
            out[span, slot * ff : (slot + 1) * ff] = activate(gate, up)


def down_kernel(count, first, flip, placement, *refs):
    rows, hidden, downs, base, outs = refs[:2], refs[2], refs[3:5], refs[5:7], refs[7:9]
    height, part = outs[0].shape
    ff = downs[0].shape[0]
    me = lax.axis_index("expert")
    far = lax.axis_size("expert") // 2
    half = (lax.axis_index("dp") + flip) % 2
    columns = pl.ds(pl.multiple_of(half * part, part), part)
    totals = [base[i][:, columns] for i in range(2)]
    for slot, down in enumerate(downs):
        span = slice(first * height, (first + 2) * height)
        value = rounded(dot(hidden[span, slot * ff : (slot + 1) * ff], down[...]))
        for i in range(2):
            weight = token_weight(rows[i][:, base[0].shape[1]:], placement[me ^ far ^ slot], count)
            totals[i] = totals[i] + value[i * height : (i + 1) * height, :] * weight
    for i in range(2):
        outs[i][...] = totals[i].astype(outs[i].dtype)


def finish_kernel(ours, *refs):
    out = refs[-1]
    for flip, parts in ((0, refs[:ours]), (1, refs[ours:-1])):
        width = parts[0].shape[1]
        half = (lax.axis_index("dp") + flip) % 2
        total = parts[0][...]
        for part in parts[1:]:
            total = total + part[...].astype(jnp.float32)
        out[:, pl.ds(pl.multiple_of(half * width, width), width)] = total.astype(out.dtype)


def call(kernel, out_shape, args, scratch=(), scalars=0):
    vmem = pl.BlockSpec(memory_space=pltpu.VMEM)
    smem = pl.BlockSpec(memory_space=pltpu.SMEM)
    return pl.pallas_call(
        kernel,
        out_shape=out_shape,
        in_specs=[smem] * scalars + [vmem] * (len(args) - scalars),
        out_specs=jax.tree.map(lambda _: vmem, out_shape),
        scratch_shapes=list(scratch),
        compiler_params=pltpu.CompilerParams(vmem_limit_bytes=VMEM_LIMIT),
        cost_estimate=pl.CostEstimate(flops=0, bytes_accessed=0, transcendentals=0),
    )(*args)


def run_copies(copies, sems):
    copies = [pltpu.make_async_copy(a, b, sems.at[i]) for i, (a, b) in enumerate(copies)]
    for copy in copies:
        copy.start()
    for copy in copies:
        copy.wait()


def part_of(ref, axis, half, size):
    span = pl.ds(pl.multiple_of(half * size, size), size)
    return ref.at[span, :] if axis == 0 else ref.at[:, span]


def store_kernel(axis, first, flags, own, came, other, out, sems):
    half = lax.axis_index("dp") % 2
    size = out.shape[axis] // 2
    taken = flags[lax.axis_index("expert")] == 1

    @pl.when(taken)
    def _():
        if axis == 0:
            parts = [ref.at[pl.ds(first, size), :] for ref in (came, other)]
        else:
            parts = [came, other]
        run_copies(
            [
                (parts[0], part_of(out, axis, half, size)),
                (parts[1], part_of(out, axis, 1 - half, size)),
            ],
            sems,
        )

    @pl.when(jnp.logical_not(taken))
    def _():
        run_copies([(own, out)], sems)


def store(axis, first, flags, own, came, other):
    vmem = pl.BlockSpec(memory_space=pltpu.VMEM)
    return pl.pallas_call(
        functools.partial(store_kernel, axis, first),
        out_shape=jax.ShapeDtypeStruct(own.shape, own.dtype),
        in_specs=[pl.BlockSpec(memory_space=pltpu.SMEM)] + [vmem] * 3,
        out_specs=pl.BlockSpec(memory_space=pl.ANY),
        scratch_shapes=[pltpu.SemaphoreType.DMA((2,))],
        compiler_params=pltpu.CompilerParams(vmem_limit_bytes=8 * 2**20),
        cost_estimate=pl.CostEstimate(flops=0, bytes_accessed=0, transcendentals=0),
    )(flags, own, came, other)


def after(value, *others):
    return lax.optimization_barrier((value, *others))[0]


def per_device(tokens, expert_ids, gate_probs, w_gate, w_up, w_down, placement, swap_flags):
    count = lax.axis_size("expert")
    couple = lax.axis_index("dp") % 2
    half_axis = count // 2
    height, width = tokens.shape
    own = (w_gate[0], w_up[0], w_down[0])
    ff = own[0].shape[1]
    trades = [(d, d ^ 1) for d in range(lax.axis_size("dp"))]

    def send(value, bit, name):
        with jax.named_scope(name):
            return lax.ppermute(value, "expert", [(d, d ^ bit) for d in range(count)])

    def trade(value):
        with jax.named_scope("trade"):
            return lax.ppermute(value, "dp", trades)

    depth, part = own[0].shape[0] // 2, width // 2

    def half_of(first, second):
        return jnp.where(couple == 0, first, second)

    upper = half_of(
        jnp.concatenate([own[0][:depth], own[1][:depth]], axis=0),
        jnp.concatenate([own[0][depth:], own[1][depth:]], axis=0),
    )
    lower = half_of(own[2][:, :part], own[2][:, part:])

    bits = []
    bit = half_axis // 2
    while bit > 1:
        bits.append(bit)
        bit //= 2
    blocks = {0: pack_gates(tokens, expert_ids, gate_probs, count)}
    masks = {0: 0}
    for stage, bit in enumerate(bits):
        for i in sorted(blocks):
            blocks[i | 1 << stage] = send(blocks[i], bit, "tokens")
            masks[i | 1 << stage] = masks[i] ^ bit
    rows = [blocks[i] for i in range(len(blocks))]

    z_upper = send(upper, half_axis, "swap")
    z_lower = send(after(lower, z_upper, *rows), half_axis, "swap")
    y_upper = trade(after(z_upper, *rows))
    near = [send(after(w, lower), 1, "near") for w in own]

    firsts = list(reversed(range(0, len(rows), 2)))
    scratch = [pltpu.VMEM((2 * height, width), jnp.bfloat16)]
    base = {}
    for first in firsts:
        base[first] = call(
            functools.partial(near_kernel, count),
            [jax.ShapeDtypeStruct((height, width), jnp.float32)] * 2,
            [placement, *rows[first : first + 2], *own, *near],
            scratch,
            scalars=1,
        )

    arrived = after(z_lower, base)
    y_lower = trade(arrived)
    z_near = [send(z_upper, 1, "z_near"), send(arrived, 1, "z_near")]
    y_near = [send(after(y_upper, arrived), 1, "y_near")]
    hidden = call(
        functools.partial(hidden_kernel, len(rows), width),
        jax.ShapeDtypeStruct((len(rows) * height, 2 * ff), jnp.bfloat16),
        [*rows, z_upper, y_upper, z_near[0], y_near[0]],
        scratch,
    )

    def far_sums(flip, downs):
        parts = {}
        for first in firsts:
            for i in (0, 1):
                parts[first + i] = jnp.bfloat16 if first + i > 0 else jnp.float32
            shape = (height, downs[0].shape[1])
            parts[first], parts[first + 1] = call(
                functools.partial(down_kernel, count, first, flip),
                [jax.ShapeDtypeStruct(shape, parts[first + i]) for i in (0, 1)],
                [placement, *rows[first : first + 2], hidden, *downs, *base[first]],
                scalars=1,
            )
        return parts

    def collect(parts):
        return [parts[0]] + [send(parts[i], masks[i], "sums") for i in reversed(range(1, len(parts)))]

    parts = far_sums(0, [arrived, z_near[1]])
    flags = after(swap_flags, parts)
    stored = [
        store(0, 0, flags, own[0], z_upper, y_upper),
        store(0, depth, flags, own[1], z_upper, y_upper),
    ]
    ours = collect(parts)
    landed = after(y_lower, stored, ours[1:-1])
    y_near.append(send(landed, 1, "y_near"))
    last_parts = far_sums(1, [landed, y_near[1]])
    stored.append(store(1, 0, after(swap_flags, last_parts), own[2], z_lower, y_lower))
    others = collect(last_parts)
    mixed = call(
        functools.partial(finish_kernel, len(ours)),
        jax.ShapeDtypeStruct((height, width), tokens.dtype),
        [*ours, *others],
    )
    return (mixed, *(w[None] for w in stored))


def solution(mesh):
    in_specs = (
        P(("dp", "expert"), None),
        P(("dp", "expert"), None),
        P(("dp", "expert"), None),
        P("expert", None, None),
        P("expert", None, None),
        P("expert", None, None),
        P(),
        P(),
    )
    out_specs = (
        P(("dp", "expert"), None),
        P(("dp", "expert"), None, None),
        P(("dp", "expert"), None, None),
        P(("dp", "expert"), None, None),
    )
    return jax.shard_map(
        per_device, mesh=mesh, in_specs=in_specs, out_specs=out_specs, check_vma=False
    )
```

```python
import functools

import jax
import jax.numpy as jnp
from jax import lax
from jax.experimental import pallas as pl
from jax.experimental.pallas import tpu as pltpu
from jax.sharding import PartitionSpec as P

LANES = 128
VMEM_LIMIT = 20 * 2**20


def split_parts(values):
    parts = []
    for _ in range(3):
        part = lax.reduce_precision(values, exponent_bits=8, mantissa_bits=7)
        parts.append(part.astype(jnp.bfloat16))
        values = values - part
    return parts


def pack_gates(tokens, expert_ids, gate_probs, count):
    experts = jnp.arange(count, dtype=jnp.int32)
    chosen = expert_ids[:, None, :] == experts[None, :, None]
    weights = jnp.sum(jnp.where(chosen, gate_probs[:, None, :], 0.0), axis=2)
    parts = jnp.concatenate(split_parts(weights), axis=1)
    parts = jnp.pad(parts, ((0, 0), (0, -parts.shape[1] % LANES)))
    return jnp.concatenate([tokens, parts], axis=1)


def dot(a, b):
    return jnp.dot(a, b, preferred_element_type=jnp.float32)


def token_weight(tail, expert, count):
    lane = lax.broadcasted_iota(jnp.int32, tail.shape, 1)
    mine = (lane % count == expert) & (lane < 3 * count)
    return jnp.sum(jnp.where(mine, tail.astype(jnp.float32), 0.0), axis=1, keepdims=True)


def activate(gate, up):
    return (gate / (1.0 + jnp.exp(-gate)) * up).astype(jnp.bfloat16)


def rounded(value):
    return value.astype(jnp.bfloat16).astype(jnp.float32)


def near_kernel(count, placement, *refs):
    rows, weights, outs, x = refs[:2], (refs[2:5], refs[5:8]), refs[8:10], refs[10]
    height, width = rows[0].shape[0], x.shape[1]
    me = lax.axis_index("expert")
    for i in range(2):
        x[i * height : (i + 1) * height, :] = rows[i][:, :width]
    totals = [0.0, 0.0]
    for flip, (g, u, d) in enumerate(weights):
        hidden = activate(dot(x[...], g[...]), dot(x[...], u[...]))
        value = rounded(dot(hidden, d[...]))
        for i in range(2):
            weight = token_weight(rows[i][:, width:], placement[me ^ flip], count)
            totals[i] = totals[i] + value[i * height : (i + 1) * height, :] * weight
    for i in range(2):
        outs[i][...] = totals[i]


def hidden_kernel(blocks, width, *refs):
    rows, weights, out, x = refs[:blocks], refs[blocks : blocks + 4], refs[blocks + 4], refs[blocks + 5]
    height = rows[0].shape[0]
    half = lax.axis_index("dp") % 2
    for first in range(0, blocks, 2):
        for i in range(2):
            x[i * height : (i + 1) * height, :] = rows[first + i][:, :width]
        for slot in range(2):
            own, other = weights[2 * slot : 2 * slot + 2]
            depth, ff = own.shape[0] // 2, own.shape[1]
            at = pl.multiple_of(half * depth, depth)
            off = pl.multiple_of(depth - at, depth)
            xa, xb = x[:, pl.ds(at, depth)], x[:, pl.ds(off, depth)]
            gate = dot(xa, own[:depth, :]) + dot(xb, other[:depth, :])
            up = dot(xa, own[depth:, :]) + dot(xb, other[depth:, :])
            span = slice(first * height, (first + 2) * height)
            out[span, slot * ff : (slot + 1) * ff] = activate(gate, up)


def down_kernel(count, first, flip, placement, *refs):
    rows, hidden, downs, base, outs = refs[:2], refs[2], refs[3:5], refs[5:7], refs[7:9]
    height, part = outs[0].shape
    ff = downs[0].shape[0]
    me = lax.axis_index("expert")
    far = lax.axis_size("expert") // 2
    half = (lax.axis_index("dp") + flip) % 2
    columns = pl.ds(pl.multiple_of(half * part, part), part)
    totals = [base[i][:, columns] for i in range(2)]
    for slot, down in enumerate(downs):
        span = slice(first * height, (first + 2) * height)
        value = rounded(dot(hidden[span, slot * ff : (slot + 1) * ff], down[...]))
        for i in range(2):
            weight = token_weight(rows[i][:, base[0].shape[1]:], placement[me ^ far ^ slot], count)
            totals[i] = totals[i] + value[i * height : (i + 1) * height, :] * weight
    for i in range(2):
        outs[i][...] = totals[i].astype(outs[i].dtype)


def finish_kernel(ours, *refs):
    out = refs[-1]
    for flip, parts in ((0, refs[:ours]), (1, refs[ours:-1])):
        width = parts[0].shape[1]
        half = (lax.axis_index("dp") + flip) % 2
        total = parts[0][...]
        for part in parts[1:]:
            total = total + part[...].astype(jnp.float32)
        out[:, pl.ds(pl.multiple_of(half * width, width), width)] = total.astype(out.dtype)


def call(kernel, out_shape, args, scratch=(), scalars=0):
    vmem = pl.BlockSpec(memory_space=pltpu.VMEM)
    smem = pl.BlockSpec(memory_space=pltpu.SMEM)
    return pl.pallas_call(
        kernel,
        out_shape=out_shape,
        in_specs=[smem] * scalars + [vmem] * (len(args) - scalars),
        out_specs=jax.tree.map(lambda _: vmem, out_shape),
        scratch_shapes=list(scratch),
        compiler_params=pltpu.CompilerParams(vmem_limit_bytes=VMEM_LIMIT),
        cost_estimate=pl.CostEstimate(flops=0, bytes_accessed=0, transcendentals=0),
    )(*args)


def run_copies(copies, sems):
    copies = [pltpu.make_async_copy(a, b, sems.at[i]) for i, (a, b) in enumerate(copies)]
    for copy in copies:
        copy.start()
    for copy in copies:
        copy.wait()


def part_of(ref, axis, half, size):
    span = pl.ds(pl.multiple_of(half * size, size), size)
    return ref.at[span, :] if axis == 0 else ref.at[:, span]


def store_kernel(axis, first, flags, own, came, other, out, sems):
    half = lax.axis_index("dp") % 2
    size = out.shape[axis] // 2
    taken = flags[lax.axis_index("expert")] == 1

    @pl.when(taken)
    def _():
        if axis == 0:
            parts = [ref.at[pl.ds(first, size), :] for ref in (came, other)]
        else:
            parts = [came, other]
        run_copies(
            [
                (parts[0], part_of(out, axis, half, size)),
                (parts[1], part_of(out, axis, 1 - half, size)),
            ],
            sems,
        )

    @pl.when(jnp.logical_not(taken))
    def _():
        run_copies([(own, out)], sems)


def store(axis, first, flags, own, came, other):
    vmem = pl.BlockSpec(memory_space=pltpu.VMEM)
    return pl.pallas_call(
        functools.partial(store_kernel, axis, first),
        out_shape=jax.ShapeDtypeStruct(own.shape, own.dtype),
        in_specs=[pl.BlockSpec(memory_space=pltpu.SMEM)] + [vmem] * 3,
        out_specs=pl.BlockSpec(memory_space=pl.ANY),
        scratch_shapes=[pltpu.SemaphoreType.DMA((2,))],
        compiler_params=pltpu.CompilerParams(vmem_limit_bytes=8 * 2**20),
        cost_estimate=pl.CostEstimate(flops=0, bytes_accessed=0, transcendentals=0),
    )(flags, own, came, other)


def after(value, *others):
    return lax.optimization_barrier((value, *others))[0]


def per_device(tokens, expert_ids, gate_probs, w_gate, w_up, w_down, placement, swap_flags):
    count = lax.axis_size("expert")
    couple = lax.axis_index("dp") % 2
    half_axis = count // 2
    height, width = tokens.shape
    own = (w_gate[0], w_up[0], w_down[0])
    ff = own[0].shape[1]
    trades = [(d, d ^ 1) for d in range(lax.axis_size("dp"))]

    def send(value, bit, name):
        with jax.named_scope(name):
            return lax.ppermute(value, "expert", [(d, d ^ bit) for d in range(count)])

    def trade(value):
        with jax.named_scope("trade"):
            return lax.ppermute(value, "dp", trades)

    depth, part = own[0].shape[0] // 2, width // 2

    def half_of(first, second):
        return jnp.where(couple == 0, first, second)

    upper = half_of(
        jnp.concatenate([own[0][:depth], own[1][:depth]], axis=0),
        jnp.concatenate([own[0][depth:], own[1][depth:]], axis=0),
    )
    lower = half_of(own[2][:, :part], own[2][:, part:])

    bits = []
    bit = half_axis // 2
    while bit > 1:
        bits.append(bit)
        bit //= 2
    blocks = {0: pack_gates(tokens, expert_ids, gate_probs, count)}
    masks = {0: 0}
    for stage, bit in enumerate(bits):
        for i in sorted(blocks):
            blocks[i | 1 << stage] = send(blocks[i], bit, "tokens")
            masks[i | 1 << stage] = masks[i] ^ bit
    rows = [blocks[i] for i in range(len(blocks))]

    z_upper = send(upper, half_axis, "swap")
    z_lower = send(after(lower, z_upper, *rows), half_axis, "swap")
    y_upper = trade(after(z_upper, *rows))
    near = [send(after(w, lower), 1, "near") for w in own]

    firsts = list(reversed(range(0, len(rows), 2)))
    scratch = [pltpu.VMEM((2 * height, width), jnp.bfloat16)]
    base = {}
    for first in firsts:
        base[first] = call(
            functools.partial(near_kernel, count),
            [jax.ShapeDtypeStruct((height, width), jnp.float32)] * 2,
            [placement, *rows[first : first + 2], *own, *near],
            scratch,
            scalars=1,
        )

    arrived = after(z_lower, base)
    y_lower = trade(arrived)
    z_near = [send(z_upper, 1, "z_near"), send(arrived, 1, "z_near")]
    y_near = [send(after(y_upper, arrived), 1, "y_near")]
    hidden = call(
        functools.partial(hidden_kernel, len(rows), width),
        jax.ShapeDtypeStruct((len(rows) * height, 2 * ff), jnp.bfloat16),
        [*rows, z_upper, y_upper, z_near[0], y_near[0]],
        scratch,
    )

    def far_sums(flip, downs):
        parts = {}
        for first in firsts:
            for i in (0, 1):
                parts[first + i] = jnp.bfloat16 if first + i > 0 else jnp.float32
            shape = (height, downs[0].shape[1])
            parts[first], parts[first + 1] = call(
                functools.partial(down_kernel, count, first, flip),
                [jax.ShapeDtypeStruct(shape, parts[first + i]) for i in (0, 1)],
                [placement, *rows[first : first + 2], hidden, *downs, *base[first]],
                scalars=1,
            )
        return parts

    def collect(parts):
        return [parts[0]] + [send(parts[i], masks[i], "sums") for i in range(1, len(parts))]

    parts = far_sums(0, [arrived, z_near[1]])
    flags = after(swap_flags, parts)
    stored = [
        store(0, 0, flags, own[0], z_upper, y_upper),
        store(0, depth, flags, own[1], z_upper, y_upper),
    ]
    ours = collect(parts)
    landed = after(y_lower, stored, ours[1::2])
    y_near.append(send(landed, 1, "y_near"))
    last_parts = far_sums(1, [landed, y_near[1]])
    stored.append(store(1, 0, after(swap_flags, last_parts), own[2], z_lower, y_lower))
    others = collect(last_parts)
    mixed = call(
        functools.partial(finish_kernel, len(ours)),
        jax.ShapeDtypeStruct((height, width), tokens.dtype),
        [*ours, *others],
    )
    return (mixed, *(w[None] for w in stored))


def solution(mesh):
    in_specs = (
        P(("dp", "expert"), None),
        P(("dp", "expert"), None),
        P(("dp", "expert"), None),
        P("expert", None, None),
        P("expert", None, None),
        P("expert", None, None),
        P(),
        P(),
    )
    out_specs = (
        P(("dp", "expert"), None),
        P(("dp", "expert"), None, None),
        P(("dp", "expert"), None, None),
        P(("dp", "expert"), None, None),
    )
    return jax.shard_map(
        per_device, mesh=mesh, in_specs=in_specs, out_specs=out_specs, check_vma=False
    )
```

```python
import functools

import jax
import jax.numpy as jnp
from jax import lax
from jax.experimental import pallas as pl
from jax.experimental.pallas import tpu as pltpu
from jax.sharding import PartitionSpec as P

LANES = 128
VMEM_LIMIT = 20 * 2**20


def split_parts(values):
    parts = []
    for _ in range(3):
        part = lax.reduce_precision(values, exponent_bits=8, mantissa_bits=7)
        parts.append(part.astype(jnp.bfloat16))
        values = values - part
    return parts


def pack_gates(tokens, expert_ids, gate_probs, count):
    experts = jnp.arange(count, dtype=jnp.int32)
    chosen = expert_ids[:, None, :] == experts[None, :, None]
    weights = jnp.sum(jnp.where(chosen, gate_probs[:, None, :], 0.0), axis=2)
    parts = jnp.concatenate(split_parts(weights), axis=1)
    parts = jnp.pad(parts, ((0, 0), (0, -parts.shape[1] % LANES)))
    return jnp.concatenate([tokens, parts], axis=1)


def dot(a, b):
    return jnp.dot(a, b, preferred_element_type=jnp.float32)


def token_weight(tail, expert, count):
    lane = lax.broadcasted_iota(jnp.int32, tail.shape, 1)
    mine = (lane % count == expert) & (lane < 3 * count)
    return jnp.sum(jnp.where(mine, tail.astype(jnp.float32), 0.0), axis=1, keepdims=True)


def activate(gate, up):
    return (gate / (1.0 + jnp.exp(-gate)) * up).astype(jnp.bfloat16)


def rounded(value):
    return value.astype(jnp.bfloat16).astype(jnp.float32)


def near_kernel(count, placement, *refs):
    rows, weights, outs, x = refs[:2], (refs[2:5], refs[5:8]), refs[8:10], refs[10]
    height, width = rows[0].shape[0], x.shape[1]
    me = lax.axis_index("expert")
    for i in range(2):
        x[i * height : (i + 1) * height, :] = rows[i][:, :width]
    totals = [0.0, 0.0]
    for flip, (g, u, d) in enumerate(weights):
        hidden = activate(dot(x[...], g[...]), dot(x[...], u[...]))
        value = rounded(dot(hidden, d[...]))
        for i in range(2):
            weight = token_weight(rows[i][:, width:], placement[me ^ flip], count)
            totals[i] = totals[i] + value[i * height : (i + 1) * height, :] * weight
    for i in range(2):
        outs[i][...] = totals[i]


def hidden_kernel(blocks, width, *refs):
    rows, own, other, out, x = refs[:blocks], refs[blocks], refs[blocks + 1], refs[blocks + 2], refs[blocks + 3]
    height = rows[0].shape[0]
    half = lax.axis_index("dp") % 2
    depth = own.shape[0] // 2
    at = pl.multiple_of(half * depth, depth)
    off = pl.multiple_of(depth - at, depth)
    for first in range(0, blocks, 2):
        for i in range(2):
            x[i * height : (i + 1) * height, :] = rows[first + i][:, :width]
        xa, xb = x[:, pl.ds(at, depth)], x[:, pl.ds(off, depth)]
        gate = dot(xa, own[:depth, :]) + dot(xb, other[:depth, :])
        up = dot(xa, own[depth:, :]) + dot(xb, other[depth:, :])
        out[first * height : (first + 2) * height, :] = activate(gate, up)


def down_kernel(count, flips, blocks, half_flip, placement, *refs):
    number = len(blocks)
    rows, refs = refs[:number], refs[number:]
    experts, refs = refs[: 2 * len(flips)], refs[2 * len(flips) :]
    base, outs = refs[:number], refs[number:]
    height, part = outs[0].shape
    width = 2 * part
    me = lax.axis_index("expert")
    far = lax.axis_size("expert") // 2
    half = (lax.axis_index("dp") + half_flip) % 2
    columns = pl.ds(pl.multiple_of(half * part, part), part)
    for first in range(0, number, 2):
        pair = range(first, first + 2)
        totals = {i: base[i][...] if base[i].shape[1] == part else base[i][:, columns] for i in pair}
        for flip, hidden, down in zip(flips, experts[::2], experts[1::2]):
            span = slice(blocks[first] * height, (blocks[first] + 2) * height)
            value = rounded(dot(hidden[span, :], down[...]))
            for i in pair:
                weight = token_weight(rows[i][:, width:], placement[me ^ far ^ flip], count)
                at = (i - first) * height
                totals[i] = totals[i] + value[at : at + height, :] * weight
        for i in pair:
            outs[i][...] = totals[i].astype(outs[i].dtype)


def finish_kernel(ours, *refs):
    out = refs[-1]
    for flip, parts in ((0, refs[:ours]), (1, refs[ours:-1])):
        width = parts[0].shape[1]
        half = (lax.axis_index("dp") + flip) % 2
        total = parts[0][...]
        for part in parts[1:]:
            total = total + part[...].astype(jnp.float32)
        out[:, pl.ds(pl.multiple_of(half * width, width), width)] = total.astype(out.dtype)


def call(kernel, out_shape, args, scratch=(), scalars=0):
    vmem = pl.BlockSpec(memory_space=pltpu.VMEM)
    smem = pl.BlockSpec(memory_space=pltpu.SMEM)
    return pl.pallas_call(
        kernel,
        out_shape=out_shape,
        in_specs=[smem] * scalars + [vmem] * (len(args) - scalars),
        out_specs=jax.tree.map(lambda _: vmem, out_shape),
        scratch_shapes=list(scratch),
        compiler_params=pltpu.CompilerParams(vmem_limit_bytes=VMEM_LIMIT),
        cost_estimate=pl.CostEstimate(flops=0, bytes_accessed=0, transcendentals=0),
    )(*args)


def run_copies(copies, sems):
    copies = [pltpu.make_async_copy(a, b, sems.at[i]) for i, (a, b) in enumerate(copies)]
    for copy in copies:
        copy.start()
    for copy in copies:
        copy.wait()


def part_of(ref, axis, half, size):
    span = pl.ds(pl.multiple_of(half * size, size), size)
    return ref.at[span, :] if axis == 0 else ref.at[:, span]


def store_kernel(axis, first, flags, own, came, other, out, sems):
    half = lax.axis_index("dp") % 2
    size = out.shape[axis] // 2
    taken = flags[lax.axis_index("expert")] == 1

    @pl.when(taken)
    def _():
        if axis == 0:
            parts = [ref.at[pl.ds(first, size), :] for ref in (came, other)]
        else:
            parts = [came, other]
        run_copies(
            [
                (parts[0], part_of(out, axis, half, size)),
                (parts[1], part_of(out, axis, 1 - half, size)),
            ],
            sems,
        )

    @pl.when(jnp.logical_not(taken))
    def _():
        run_copies([(own, out)], sems)


def store(axis, first, flags, own, came, other):
    vmem = pl.BlockSpec(memory_space=pltpu.VMEM)
    return pl.pallas_call(
        functools.partial(store_kernel, axis, first),
        out_shape=jax.ShapeDtypeStruct(own.shape, own.dtype),
        in_specs=[pl.BlockSpec(memory_space=pltpu.SMEM)] + [vmem] * 3,
        out_specs=pl.BlockSpec(memory_space=pl.ANY),
        scratch_shapes=[pltpu.SemaphoreType.DMA((2,))],
        compiler_params=pltpu.CompilerParams(vmem_limit_bytes=8 * 2**20),
        cost_estimate=pl.CostEstimate(flops=0, bytes_accessed=0, transcendentals=0),
    )(flags, own, came, other)


def after(value, *others):
    return lax.optimization_barrier((value, *others))[0]


def per_device(tokens, expert_ids, gate_probs, w_gate, w_up, w_down, placement, swap_flags):
    count = lax.axis_size("expert")
    couple = lax.axis_index("dp") % 2
    half_axis = count // 2
    height, width = tokens.shape
    own = (w_gate[0], w_up[0], w_down[0])
    ff = own[0].shape[1]
    trades = [(d, d ^ 1) for d in range(lax.axis_size("dp"))]

    def send(value, bit, name):
        with jax.named_scope(name):
            return lax.ppermute(value, "expert", [(d, d ^ bit) for d in range(count)])

    def trade(value):
        with jax.named_scope("trade"):
            return lax.ppermute(value, "dp", trades)

    depth, part = own[0].shape[0] // 2, width // 2

    def half_of(first, second):
        return jnp.where(couple == 0, first, second)

    upper = half_of(
        jnp.concatenate([own[0][:depth], own[1][:depth]], axis=0),
        jnp.concatenate([own[0][depth:], own[1][depth:]], axis=0),
    )
    lower = half_of(own[2][:, :part], own[2][:, part:])

    bits = []
    bit = half_axis // 2
    while bit > 1:
        bits.append(bit)
        bit //= 2
    blocks = {0: pack_gates(tokens, expert_ids, gate_probs, count)}
    masks = {0: 0}
    for stage, bit in enumerate(bits):
        for i in sorted(blocks):
            blocks[i | 1 << stage] = send(blocks[i], bit, "tokens")
            masks[i | 1 << stage] = masks[i] ^ bit
    rows = [blocks[i] for i in range(len(blocks))]

    z_upper = send(upper, half_axis, "swap")
    z_lower = send(after(lower, z_upper, *rows), half_axis, "swap")
    y_upper = trade(after(z_upper, *rows))
    near = [send(after(w, lower), 1, "near") for w in own]

    firsts = list(reversed(range(0, len(rows), 2)))
    scratch = [pltpu.VMEM((2 * height, width), jnp.bfloat16)]
    base = {}
    for first in firsts:
        base[first] = call(
            functools.partial(near_kernel, count),
            [jax.ShapeDtypeStruct((height, width), jnp.float32)] * 2,
            [placement, *rows[first : first + 2], *own, *near],
            scratch,
            scalars=1,
        )

    arrived = after(z_lower, base)
    y_lower = trade(arrived)
    z_near = [send(z_upper, 1, "z_near"), send(arrived, 1, "z_near")]
    y_near = [send(after(y_upper, arrived), 1, "y_near")]
    hidden = [
        call(
            functools.partial(hidden_kernel, len(rows), width),
            jax.ShapeDtypeStruct((len(rows) * height, ff), jnp.bfloat16),
            [*rows, own_part, other_part],
            scratch,
        )
        for own_part, other_part in ((z_upper, y_upper), (z_near[0], y_near[0]))
    ]

    def far_sums(flips, downs, half_flip, blocks, sums, last):
        kinds = [jnp.bfloat16 if last and i > 0 else jnp.float32 for i in blocks]
        experts = [x for flip, down in zip(flips, downs) for x in (hidden[flip], down)]
        out = call(
            functools.partial(down_kernel, count, flips, blocks, half_flip),
            [jax.ShapeDtypeStruct((height, part), kind) for kind in kinds],
            [placement, *(rows[i] for i in blocks), *experts, *(sums[i] for i in blocks)],
            scalars=1,
        )
        return dict(zip(blocks, out))

    def collect(parts):
        return [parts[0]] + [send(parts[i], masks[i], "sums") for i in reversed(range(1, len(parts)))]

    near_sums = [x for first in reversed(firsts) for x in base[first]]
    parts = {}
    for first in firsts:
        parts |= far_sums((0, 1), [arrived, z_near[1]], 0, (first, first + 1), near_sums, True)
    flags = after(swap_flags, parts)
    stored = [
        store(0, 0, flags, own[0], z_upper, y_upper),
        store(0, depth, flags, own[1], z_upper, y_upper),
    ]
    ours = collect(parts)
    landed = after(y_lower, stored, ours[1:-1])
    y_near.append(send(landed, 1, "y_near"))
    everyone = tuple(range(len(rows)))
    last_sums = far_sums((0,), [landed], 1, everyone, near_sums, False)
    last_parts = {}
    for first in firsts:
        last_parts |= far_sums((1,), [y_near[1]], 1, (first, first + 1), last_sums, True)
    stored.append(store(1, 0, after(swap_flags, last_parts), own[2], z_lower, y_lower))
    others = collect(last_parts)
    mixed = call(
        functools.partial(finish_kernel, len(ours)),
        jax.ShapeDtypeStruct((height, width), tokens.dtype),
        [*ours, *others],
    )
    return (mixed, *(w[None] for w in stored))


def solution(mesh):
    in_specs = (
        P(("dp", "expert"), None),
        P(("dp", "expert"), None),
        P(("dp", "expert"), None),
        P("expert", None, None),
        P("expert", None, None),
        P("expert", None, None),
        P(),
        P(),
    )
    out_specs = (
        P(("dp", "expert"), None),
        P(("dp", "expert"), None, None),
        P(("dp", "expert"), None, None),
        P(("dp", "expert"), None, None),
    )
    return jax.shard_map(
        per_device, mesh=mesh, in_specs=in_specs, out_specs=out_specs, check_vma=False
    )
```

```python
import functools

import jax
import jax.numpy as jnp
from jax import lax
from jax.experimental import pallas as pl
from jax.experimental.pallas import tpu as pltpu
from jax.sharding import PartitionSpec as P

LANES = 128
VMEM_LIMIT = 20 * 2**20


def split_parts(values):
    parts = []
    for _ in range(3):
        part = lax.reduce_precision(values, exponent_bits=8, mantissa_bits=7)
        parts.append(part.astype(jnp.bfloat16))
        values = values - part
    return parts


def pack_gates(tokens, expert_ids, gate_probs, count):
    experts = jnp.arange(count, dtype=jnp.int32)
    chosen = expert_ids[:, None, :] == experts[None, :, None]
    weights = jnp.sum(jnp.where(chosen, gate_probs[:, None, :], 0.0), axis=2)
    parts = jnp.concatenate(split_parts(weights), axis=1)
    parts = jnp.pad(parts, ((0, 0), (0, -parts.shape[1] % LANES)))
    return jnp.concatenate([tokens, parts], axis=1)


def dot(a, b):
    return jnp.dot(a, b, preferred_element_type=jnp.float32)


def token_weight(tail, expert, count):
    lane = lax.broadcasted_iota(jnp.int32, tail.shape, 1)
    mine = (lane % count == expert) & (lane < 3 * count)
    return jnp.sum(jnp.where(mine, tail.astype(jnp.float32), 0.0), axis=1, keepdims=True)


def activate(gate, up):
    return (gate / (1.0 + jnp.exp(-gate)) * up).astype(jnp.bfloat16)


def rounded(value):
    return value.astype(jnp.bfloat16).astype(jnp.float32)


def near_kernel(count, placement, *refs):
    rows, weights, outs, x = refs[:2], (refs[2:5], refs[5:8]), refs[8:10], refs[10]
    height, width = rows[0].shape[0], x.shape[1]
    me = lax.axis_index("expert")
    for i in range(2):
        x[i * height : (i + 1) * height, :] = rows[i][:, :width]
    totals = [0.0, 0.0]
    for flip, (g, u, d) in enumerate(weights):
        hidden = activate(dot(x[...], g[...]), dot(x[...], u[...]))
        value = rounded(dot(hidden, d[...]))
        for i in range(2):
            weight = token_weight(rows[i][:, width:], placement[me ^ flip], count)
            totals[i] = totals[i] + value[i * height : (i + 1) * height, :] * weight
    for i in range(2):
        outs[i][...] = totals[i]


def hidden_kernel(blocks, width, *refs):
    rows, own, other, out, x = refs[:blocks], refs[blocks], refs[blocks + 1], refs[blocks + 2], refs[blocks + 3]
    height = rows[0].shape[0]
    half = lax.axis_index("dp") % 2
    depth = own.shape[0] // 2
    at = pl.multiple_of(half * depth, depth)
    off = pl.multiple_of(depth - at, depth)
    for first in range(0, blocks, 2):
        for i in range(2):
            x[i * height : (i + 1) * height, :] = rows[first + i][:, :width]
        xa, xb = x[:, pl.ds(at, depth)], x[:, pl.ds(off, depth)]
        gate = dot(xa, own[:depth, :]) + dot(xb, other[:depth, :])
        up = dot(xa, own[depth:, :]) + dot(xb, other[depth:, :])
        out[first * height : (first + 2) * height, :] = activate(gate, up)


def down_kernel(count, flips, blocks, half_flip, placement, *refs):
    number = len(blocks)
    rows, refs = refs[:number], refs[number:]
    experts, refs = refs[: 2 * len(flips)], refs[2 * len(flips) :]
    base, outs = refs[:number], refs[number:]
    height, part = outs[0].shape
    width = 2 * part
    me = lax.axis_index("expert")
    far = lax.axis_size("expert") // 2
    half = (lax.axis_index("dp") + half_flip) % 2
    columns = pl.ds(pl.multiple_of(half * part, part), part)
    for first in range(0, number, 2):
        pair = range(first, first + 2)
        totals = {i: base[i][...] if base[i].shape[1] == part else base[i][:, columns] for i in pair}
        for flip, hidden, down in zip(flips, experts[::2], experts[1::2]):
            span = slice(blocks[first] * height, (blocks[first] + 2) * height)
            value = rounded(dot(hidden[span, :], down[...]))
            for i in pair:
                weight = token_weight(rows[i][:, width:], placement[me ^ far ^ flip], count)
                at = (i - first) * height
                totals[i] = totals[i] + value[at : at + height, :] * weight
        for i in pair:
            outs[i][...] = totals[i].astype(outs[i].dtype)


def finish_kernel(ours, *refs):
    out = refs[-1]
    for flip, parts in ((0, refs[:ours]), (1, refs[ours:-1])):
        width = parts[0].shape[1]
        half = (lax.axis_index("dp") + flip) % 2
        total = parts[0][...]
        for part in parts[1:]:
            total = total + part[...].astype(jnp.float32)
        out[:, pl.ds(pl.multiple_of(half * width, width), width)] = total.astype(out.dtype)


def call(kernel, out_shape, args, scratch=(), scalars=0):
    vmem = pl.BlockSpec(memory_space=pltpu.VMEM)
    smem = pl.BlockSpec(memory_space=pltpu.SMEM)
    return pl.pallas_call(
        kernel,
        out_shape=out_shape,
        in_specs=[smem] * scalars + [vmem] * (len(args) - scalars),
        out_specs=jax.tree.map(lambda _: vmem, out_shape),
        scratch_shapes=list(scratch),
        compiler_params=pltpu.CompilerParams(vmem_limit_bytes=VMEM_LIMIT),
        cost_estimate=pl.CostEstimate(flops=0, bytes_accessed=0, transcendentals=0),
    )(*args)


def run_copies(copies, sems):
    copies = [pltpu.make_async_copy(a, b, sems.at[i]) for i, (a, b) in enumerate(copies)]
    for copy in copies:
        copy.start()
    for copy in copies:
        copy.wait()


def part_of(ref, axis, half, size):
    span = pl.ds(pl.multiple_of(half * size, size), size)
    return ref.at[span, :] if axis == 0 else ref.at[:, span]


def upper_kernel(gate, up, out, sems):
    half = lax.axis_index("dp") % 2
    depth = out.shape[0] // 2
    run_copies(
        [
            (part_of(gate, 0, half, depth), out.at[pl.ds(0, depth), :]),
            (part_of(up, 0, half, depth), out.at[pl.ds(depth, depth), :]),
        ],
        sems,
    )


def take_upper(gate, up):
    hbm = pl.BlockSpec(memory_space=pl.ANY)
    return pl.pallas_call(
        upper_kernel,
        out_shape=jax.ShapeDtypeStruct(gate.shape, gate.dtype),
        in_specs=[hbm] * 2,
        out_specs=pl.BlockSpec(memory_space=pltpu.VMEM),
        scratch_shapes=[pltpu.SemaphoreType.DMA((2,))],
        compiler_params=pltpu.CompilerParams(vmem_limit_bytes=58 * 2**20),
        cost_estimate=pl.CostEstimate(flops=0, bytes_accessed=0, transcendentals=0),
    )(gate, up)


def store_kernel(axis, first, flags, own, came, other, out, sems):
    half = lax.axis_index("dp") % 2
    size = out.shape[axis] // 2
    taken = flags[lax.axis_index("expert")] == 1

    @pl.when(taken)
    def _():
        if axis == 0:
            parts = [ref.at[pl.ds(first, size), :] for ref in (came, other)]
        else:
            parts = [came, other]
        run_copies(
            [
                (parts[0], part_of(out, axis, half, size)),
                (parts[1], part_of(out, axis, 1 - half, size)),
            ],
            sems,
        )

    @pl.when(jnp.logical_not(taken))
    def _():
        run_copies([(own, out)], sems)


def store(axis, first, flags, own, came, other):
    vmem = pl.BlockSpec(memory_space=pltpu.VMEM)
    return pl.pallas_call(
        functools.partial(store_kernel, axis, first),
        out_shape=jax.ShapeDtypeStruct(own.shape, own.dtype),
        in_specs=[pl.BlockSpec(memory_space=pltpu.SMEM)] + [vmem] * 3,
        out_specs=pl.BlockSpec(memory_space=pl.ANY),
        scratch_shapes=[pltpu.SemaphoreType.DMA((2,))],
        compiler_params=pltpu.CompilerParams(vmem_limit_bytes=8 * 2**20),
        cost_estimate=pl.CostEstimate(flops=0, bytes_accessed=0, transcendentals=0),
    )(flags, own, came, other)


def after(value, *others):
    return lax.optimization_barrier((value, *others))[0]


def per_device(tokens, expert_ids, gate_probs, w_gate, w_up, w_down, placement, swap_flags):
    count = lax.axis_size("expert")
    couple = lax.axis_index("dp") % 2
    half_axis = count // 2
    height, width = tokens.shape
    own = (w_gate[0], w_up[0], w_down[0])
    ff = own[0].shape[1]
    trades = [(d, d ^ 1) for d in range(lax.axis_size("dp"))]

    def send(value, bit, name):
        with jax.named_scope(name):
            return lax.ppermute(value, "expert", [(d, d ^ bit) for d in range(count)])

    def trade(value):
        with jax.named_scope("trade"):
            return lax.ppermute(value, "dp", trades)

    depth, part = own[0].shape[0] // 2, width // 2

    def half_of(first, second):
        return jnp.where(couple == 0, first, second)

    upper = take_upper(own[0], own[1])
    lower = half_of(own[2][:, :part], own[2][:, part:])

    bits = []
    bit = half_axis // 2
    while bit > 1:
        bits.append(bit)
        bit //= 2
    blocks = {0: pack_gates(tokens, expert_ids, gate_probs, count)}
    masks = {0: 0}
    for stage, bit in enumerate(bits):
        for i in sorted(blocks):
            blocks[i | 1 << stage] = send(blocks[i], bit, "tokens")
            masks[i | 1 << stage] = masks[i] ^ bit
    rows = [blocks[i] for i in range(len(blocks))]

    z_upper = send(upper, half_axis, "swap")
    z_lower = send(after(lower, z_upper, *rows), half_axis, "swap")
    y_upper = trade(after(z_upper, *rows))
    near = [send(after(w, lower), 1, "near") for w in own]

    firsts = list(reversed(range(0, len(rows), 2)))
    scratch = [pltpu.VMEM((2 * height, width), jnp.bfloat16)]
    base = {}
    for first in firsts:
        base[first] = call(
            functools.partial(near_kernel, count),
            [jax.ShapeDtypeStruct((height, width), jnp.float32)] * 2,
            [placement, *rows[first : first + 2], *own, *near],
            scratch,
            scalars=1,
        )

    arrived = after(z_lower, base)
    y_lower = trade(arrived)
    z_near = [send(z_upper, 1, "z_near"), send(arrived, 1, "z_near")]
    y_near = [send(after(y_upper, arrived), 1, "y_near")]
    hidden = [
        call(
            functools.partial(hidden_kernel, len(rows), width),
            jax.ShapeDtypeStruct((len(rows) * height, ff), jnp.bfloat16),
            [*rows, own_part, other_part],
            scratch,
        )
        for own_part, other_part in ((z_upper, y_upper), (z_near[0], y_near[0]))
    ]

    def far_sums(flips, downs, half_flip, blocks, sums, last):
        kinds = [jnp.bfloat16 if last and i > 0 else jnp.float32 for i in blocks]
        experts = [x for flip, down in zip(flips, downs) for x in (hidden[flip], down)]
        out = call(
            functools.partial(down_kernel, count, flips, blocks, half_flip),
            [jax.ShapeDtypeStruct((height, part), kind) for kind in kinds],
            [placement, *(rows[i] for i in blocks), *experts, *(sums[i] for i in blocks)],
            scalars=1,
        )
        return dict(zip(blocks, out))

    def collect(parts):
        return [parts[0]] + [send(parts[i], masks[i], "sums") for i in reversed(range(1, len(parts)))]

    near_sums = [x for first in reversed(firsts) for x in base[first]]
    parts = {}
    for first in firsts:
        parts |= far_sums((0, 1), [arrived, z_near[1]], 0, (first, first + 1), near_sums, True)
    flags = after(swap_flags, parts)
    stored = [
        store(0, 0, flags, own[0], z_upper, y_upper),
        store(0, depth, flags, own[1], z_upper, y_upper),
    ]
    ours = collect(parts)
    landed = after(y_lower, stored, ours[1:-1])
    y_near.append(send(landed, 1, "y_near"))
    everyone = tuple(range(len(rows)))
    last_sums = far_sums((0,), [landed], 1, everyone, near_sums, False)
    last_parts = {}
    for first in firsts:
        last_parts |= far_sums((1,), [y_near[1]], 1, (first, first + 1), last_sums, True)
    stored.append(store(1, 0, after(swap_flags, last_parts), own[2], z_lower, y_lower))
    others = collect(last_parts)
    mixed = call(
        functools.partial(finish_kernel, len(ours)),
        jax.ShapeDtypeStruct((height, width), tokens.dtype),
        [*ours, *others],
    )
    return (mixed, *(w[None] for w in stored))


def solution(mesh):
    in_specs = (
        P(("dp", "expert"), None),
        P(("dp", "expert"), None),
        P(("dp", "expert"), None),
        P("expert", None, None),
        P("expert", None, None),
        P("expert", None, None),
        P(),
        P(),
    )
    out_specs = (
        P(("dp", "expert"), None),
        P(("dp", "expert"), None, None),
        P(("dp", "expert"), None, None),
        P(("dp", "expert"), None, None),
    )
    return jax.shard_map(
        per_device, mesh=mesh, in_specs=in_specs, out_specs=out_specs, check_vma=False
    )
```

```python
import functools

import jax
import jax.numpy as jnp
from jax import lax
from jax.experimental import pallas as pl
from jax.experimental.pallas import tpu as pltpu
from jax.sharding import PartitionSpec as P

LANES = 128
VMEM_LIMIT = 20 * 2**20


def split_parts(values):
    parts = []
    for _ in range(3):
        part = lax.reduce_precision(values, exponent_bits=8, mantissa_bits=7)
        parts.append(part.astype(jnp.bfloat16))
        values = values - part
    return parts


def pack_gates(tokens, expert_ids, gate_probs, count):
    experts = jnp.arange(count, dtype=jnp.int32)
    chosen = expert_ids[:, None, :] == experts[None, :, None]
    weights = jnp.sum(jnp.where(chosen, gate_probs[:, None, :], 0.0), axis=2)
    parts = jnp.concatenate(split_parts(weights), axis=1)
    parts = jnp.pad(parts, ((0, 0), (0, -parts.shape[1] % LANES)))
    return jnp.concatenate([tokens, parts], axis=1)


def dot(a, b):
    return jnp.dot(a, b, preferred_element_type=jnp.float32)


def token_weight(tail, expert, count):
    lane = lax.broadcasted_iota(jnp.int32, tail.shape, 1)
    mine = (lane % count == expert) & (lane < 3 * count)
    return jnp.sum(jnp.where(mine, tail.astype(jnp.float32), 0.0), axis=1, keepdims=True)


def activate(gate, up):
    return (gate / (1.0 + jnp.exp(-gate)) * up).astype(jnp.bfloat16)


def rounded(value):
    return value.astype(jnp.bfloat16).astype(jnp.float32)


def near_kernel(count, placement, *refs):
    rows, weights, outs, x = refs[:2], (refs[2:5], refs[5:8]), refs[8:10], refs[10]
    height, width = rows[0].shape[0], x.shape[1]
    me = lax.axis_index("expert")
    for i in range(2):
        x[i * height : (i + 1) * height, :] = rows[i][:, :width]
    totals = [0.0, 0.0]
    for flip, (g, u, d) in enumerate(weights):
        hidden = activate(dot(x[...], g[...]), dot(x[...], u[...]))
        value = rounded(dot(hidden, d[...]))
        for i in range(2):
            weight = token_weight(rows[i][:, width:], placement[me ^ flip], count)
            totals[i] = totals[i] + value[i * height : (i + 1) * height, :] * weight
    for i in range(2):
        outs[i][...] = totals[i]


def hidden_kernel(blocks, width, *refs):
    rows, own, other, out, x = refs[:blocks], refs[blocks], refs[blocks + 1], refs[blocks + 2], refs[blocks + 3]
    height = rows[0].shape[0]
    half = lax.axis_index("dp") % 2
    depth = own.shape[0] // 2
    at = pl.multiple_of(half * depth, depth)
    off = pl.multiple_of(depth - at, depth)
    for first in range(0, blocks, 2):
        for i in range(2):
            x[i * height : (i + 1) * height, :] = rows[first + i][:, :width]
        xa, xb = x[:, pl.ds(at, depth)], x[:, pl.ds(off, depth)]
        gate = dot(xa, own[:depth, :]) + dot(xb, other[:depth, :])
        up = dot(xa, own[depth:, :]) + dot(xb, other[depth:, :])
        out[first * height : (first + 2) * height, :] = activate(gate, up)


def down_kernel(count, flips, places, half_flip, placement, *refs):
    number = count // 4
    rows, refs = refs[:number], refs[number:]
    experts, refs = refs[: 2 * len(flips)], refs[2 * len(flips) :]
    base, outs = refs[:number], refs[number:]
    height, part = outs[0].shape[-2:]
    width = 2 * part
    me = lax.axis_index("expert")
    far = lax.axis_size("expert") // 2
    half = (lax.axis_index("dp") + half_flip) % 2
    columns = pl.ds(pl.multiple_of(half * part, part), part)
    for first in range(0, number, 2):
        pair = range(first, first + 2)
        totals = {i: base[i][...] if base[i].shape[1] == part else base[i][:, columns] for i in pair}
        for flip, hidden, down in zip(flips, experts[::2], experts[1::2]):
            value = rounded(dot(hidden[first * height : (first + 2) * height, :], down[...]))
            for i in pair:
                weight = token_weight(rows[i][:, width:], placement[me ^ far ^ flip], count)
                at = (i - first) * height
                totals[i] = totals[i] + value[at : at + height, :] * weight
        for i in pair:
            if places is None:
                outs[i][...] = totals[i]
            else:
                owner = (me // 2) % number ^ places[i]
                outs[0][owner] = totals[i].astype(outs[0].dtype)


def finish_kernel(ours, others, out):
    for flip, parts in ((0, ours), (1, others)):
        width = parts.shape[2]
        half = (lax.axis_index("dp") + flip) % 2
        total = parts[0].astype(jnp.float32)
        for i in range(1, parts.shape[0]):
            total = total + parts[i].astype(jnp.float32)
        out[:, pl.ds(pl.multiple_of(half * width, width), width)] = total.astype(out.dtype)


def call(kernel, out_shape, args, scratch=(), scalars=0):
    vmem = pl.BlockSpec(memory_space=pltpu.VMEM)
    smem = pl.BlockSpec(memory_space=pltpu.SMEM)
    return pl.pallas_call(
        kernel,
        out_shape=out_shape,
        in_specs=[smem] * scalars + [vmem] * (len(args) - scalars),
        out_specs=jax.tree.map(lambda _: vmem, out_shape),
        scratch_shapes=list(scratch),
        compiler_params=pltpu.CompilerParams(vmem_limit_bytes=VMEM_LIMIT),
        cost_estimate=pl.CostEstimate(flops=0, bytes_accessed=0, transcendentals=0),
    )(*args)


def run_copies(copies, sems):
    copies = [pltpu.make_async_copy(a, b, sems.at[i]) for i, (a, b) in enumerate(copies)]
    for copy in copies:
        copy.start()
    for copy in copies:
        copy.wait()


def part_of(ref, axis, half, size):
    span = pl.ds(pl.multiple_of(half * size, size), size)
    return ref.at[span, :] if axis == 0 else ref.at[:, span]


def store_kernel(axis, first, flags, own, came, other, out, sems):
    half = lax.axis_index("dp") % 2
    size = out.shape[axis] // 2
    taken = flags[lax.axis_index("expert")] == 1

    @pl.when(taken)
    def _():
        if axis == 0:
            parts = [ref.at[pl.ds(first, size), :] for ref in (came, other)]
        else:
            parts = [came, other]
        run_copies(
            [
                (parts[0], part_of(out, axis, half, size)),
                (parts[1], part_of(out, axis, 1 - half, size)),
            ],
            sems,
        )

    @pl.when(jnp.logical_not(taken))
    def _():
        run_copies([(own, out)], sems)


def store(axis, first, flags, own, came, other):
    vmem = pl.BlockSpec(memory_space=pltpu.VMEM)
    return pl.pallas_call(
        functools.partial(store_kernel, axis, first),
        out_shape=jax.ShapeDtypeStruct(own.shape, own.dtype),
        in_specs=[pl.BlockSpec(memory_space=pltpu.SMEM)] + [vmem] * 3,
        out_specs=pl.BlockSpec(memory_space=pl.ANY),
        scratch_shapes=[pltpu.SemaphoreType.DMA((2,))],
        compiler_params=pltpu.CompilerParams(vmem_limit_bytes=8 * 2**20),
        cost_estimate=pl.CostEstimate(flops=0, bytes_accessed=0, transcendentals=0),
    )(flags, own, came, other)


def after(value, *others):
    return lax.optimization_barrier((value, *others))[0]


def per_device(tokens, expert_ids, gate_probs, w_gate, w_up, w_down, placement, swap_flags):
    count = lax.axis_size("expert")
    couple = lax.axis_index("dp") % 2
    half_axis = count // 2
    height, width = tokens.shape
    own = (w_gate[0], w_up[0], w_down[0])
    ff = own[0].shape[1]
    trades = [(d, d ^ 1) for d in range(lax.axis_size("dp"))]

    def send(value, bit, name):
        with jax.named_scope(name):
            return lax.ppermute(value, "expert", [(d, d ^ bit) for d in range(count)])

    def trade(value):
        with jax.named_scope("trade"):
            return lax.ppermute(value, "dp", trades)

    depth, part = own[0].shape[0] // 2, width // 2

    def half_of(first, second):
        return jnp.where(couple == 0, first, second)

    upper = half_of(
        jnp.concatenate([own[0][:depth], own[1][:depth]], axis=0),
        jnp.concatenate([own[0][depth:], own[1][depth:]], axis=0),
    )
    lower = half_of(own[2][:, :part], own[2][:, part:])

    bits = []
    bit = half_axis // 2
    while bit > 1:
        bits.append(bit)
        bit //= 2
    blocks = {0: pack_gates(tokens, expert_ids, gate_probs, count)}
    masks = {0: 0}
    for stage, bit in enumerate(bits):
        for i in sorted(blocks):
            blocks[i | 1 << stage] = send(blocks[i], bit, "tokens")
            masks[i | 1 << stage] = masks[i] ^ bit
    rows = [blocks[i] for i in range(len(blocks))]

    z_upper = send(upper, half_axis, "swap")
    z_lower = send(after(lower, z_upper, *rows), half_axis, "swap")
    y_upper = trade(after(z_upper, *rows))
    near = [send(after(w, lower), 1, "near") for w in own]

    firsts = list(reversed(range(0, len(rows), 2)))
    scratch = [pltpu.VMEM((2 * height, width), jnp.bfloat16)]
    base = {}
    for first in firsts:
        base[first] = call(
            functools.partial(near_kernel, count),
            [jax.ShapeDtypeStruct((height, width), jnp.float32)] * 2,
            [placement, *rows[first : first + 2], *own, *near],
            scratch,
            scalars=1,
        )

    arrived = after(z_lower, base)
    y_lower = trade(arrived)
    z_near = [send(z_upper, 1, "z_near"), send(arrived, 1, "z_near")]
    y_near = [send(after(y_upper, arrived), 1, "y_near")]
    hidden = [
        call(
            functools.partial(hidden_kernel, len(rows), width),
            jax.ShapeDtypeStruct((len(rows) * height, ff), jnp.bfloat16),
            [*rows, own_part, other_part],
            scratch,
        )
        for own_part, other_part in ((z_upper, y_upper), (z_near[0], y_near[0]))
    ]

    near_sums = [x for first in reversed(firsts) for x in base[first]]
    places = tuple(masks[i] // 2 for i in range(len(rows)))

    def far_sums(flips, downs, half_flip, sums, last):
        experts = [x for flip, down in zip(flips, downs) for x in (hidden[flip], down)]
        if last:
            shapes = [jax.ShapeDtypeStruct((len(rows), height, part), jnp.bfloat16)]
        else:
            shapes = [jax.ShapeDtypeStruct((height, part), jnp.float32)] * len(rows)
        return call(
            functools.partial(down_kernel, count, flips, places if last else None, half_flip),
            shapes,
            [placement, *rows, *experts, *sums],
            scalars=1,
        )

    members = [range(d, d + half_axis, 2) for d in (0, 1, half_axis, half_axis + 1)]

    def collect(parts):
        with jax.named_scope("sums"):
            return lax.all_to_all(
                parts, "expert", 0, 0, axis_index_groups=[list(m) for m in members], tiled=True
            )

    (parts,) = far_sums((0, 1), [arrived, z_near[1]], 0, near_sums, True)
    flags = after(swap_flags, parts)
    stored = [
        store(0, 0, flags, own[0], z_upper, y_upper),
        store(0, depth, flags, own[1], z_upper, y_upper),
    ]
    ours = collect(parts)
    landed = after(y_lower, stored, ours)
    y_near.append(send(landed, 1, "y_near"))
    last_sums = far_sums((0,), [landed], 1, near_sums, False)
    (last_parts,) = far_sums((1,), [y_near[1]], 1, last_sums, True)
    stored.append(store(1, 0, after(swap_flags, last_parts), own[2], z_lower, y_lower))
    mixed = call(
        finish_kernel,
        jax.ShapeDtypeStruct((height, width), tokens.dtype),
        [ours, collect(last_parts)],
    )
    return (mixed, *(w[None] for w in stored))


def solution(mesh):
    in_specs = (
        P(("dp", "expert"), None),
        P(("dp", "expert"), None),
        P(("dp", "expert"), None),
        P("expert", None, None),
        P("expert", None, None),
        P("expert", None, None),
        P(),
        P(),
    )
    out_specs = (
        P(("dp", "expert"), None),
        P(("dp", "expert"), None, None),
        P(("dp", "expert"), None, None),
        P(("dp", "expert"), None, None),
    )
    return jax.shard_map(
        per_device, mesh=mesh, in_specs=in_specs, out_specs=out_specs, check_vma=False
    )
```

```python
import functools

import jax
import jax.numpy as jnp
from jax import lax
from jax.experimental import pallas as pl
from jax.experimental.pallas import tpu as pltpu
from jax.sharding import PartitionSpec as P

LANES = 128
VMEM_LIMIT = 20 * 2**20


def split_parts(values):
    parts = []
    for _ in range(3):
        part = lax.reduce_precision(values, exponent_bits=8, mantissa_bits=7)
        parts.append(part.astype(jnp.bfloat16))
        values = values - part
    return parts


def pack_gates(tokens, expert_ids, gate_probs, count):
    experts = jnp.arange(count, dtype=jnp.int32)
    chosen = expert_ids[:, None, :] == experts[None, :, None]
    weights = jnp.sum(jnp.where(chosen, gate_probs[:, None, :], 0.0), axis=2)
    parts = jnp.concatenate(split_parts(weights), axis=1)
    parts = jnp.pad(parts, ((0, 0), (0, -parts.shape[1] % LANES)))
    return jnp.concatenate([tokens, parts], axis=1)


def dot(a, b):
    return jnp.dot(a, b, preferred_element_type=jnp.float32)


def token_weight(tail, expert, count):
    lane = lax.broadcasted_iota(jnp.int32, tail.shape, 1)
    mine = (lane % count == expert) & (lane < 3 * count)
    return jnp.sum(jnp.where(mine, tail.astype(jnp.float32), 0.0), axis=1, keepdims=True)


def activate(gate, up):
    return (gate / (1.0 + jnp.exp(-gate)) * up).astype(jnp.bfloat16)


def rounded(value):
    return value.astype(jnp.bfloat16).astype(jnp.float32)


def near_kernel(count, placement, *refs):
    rows, weights, outs, x = refs[:2], (refs[2:5], refs[5:8]), refs[8:10], refs[10]
    height, width = rows[0].shape[0], x.shape[1]
    me = lax.axis_index("expert")
    for i in range(2):
        x[i * height : (i + 1) * height, :] = rows[i][:, :width]
    totals = [0.0, 0.0]
    for flip, (g, u, d) in enumerate(weights):
        hidden = activate(dot(x[...], g[...]), dot(x[...], u[...]))
        value = rounded(dot(hidden, d[...]))
        for i in range(2):
            weight = token_weight(rows[i][:, width:], placement[me ^ flip], count)
            totals[i] = totals[i] + value[i * height : (i + 1) * height, :] * weight
    for i in range(2):
        outs[i][...] = totals[i]


def hidden_kernel(blocks, width, *refs):
    rows, (ga, ua, gb, ub), out, x = refs[:blocks], refs[blocks : blocks + 4], refs[blocks + 4], refs[blocks + 5]
    height = rows[0].shape[0]
    half = lax.axis_index("dp") % 2
    depth = ga.shape[0]
    at = pl.multiple_of(half * depth, depth)
    off = pl.multiple_of(depth - at, depth)
    for first in range(0, blocks, 2):
        for i in range(2):
            x[i * height : (i + 1) * height, :] = rows[first + i][:, :width]
        xa, xb = x[:, pl.ds(at, depth)], x[:, pl.ds(off, depth)]
        gate = dot(xa, ga[...]) + dot(xb, gb[...])
        up = dot(xa, ua[...]) + dot(xb, ub[...])
        out[first * height : (first + 2) * height, :] = activate(gate, up)


def down_kernel(count, flips, blocks, half_flip, placement, *refs):
    number = len(blocks)
    rows, refs = refs[:number], refs[number:]
    experts, refs = refs[: 2 * len(flips)], refs[2 * len(flips) :]
    base, outs = refs[:number], refs[number:]
    height, part = outs[0].shape
    width = 2 * part
    me = lax.axis_index("expert")
    far = lax.axis_size("expert") // 2
    half = (lax.axis_index("dp") + half_flip) % 2
    columns = pl.ds(pl.multiple_of(half * part, part), part)
    for first in range(0, number, 2):
        pair = range(first, first + 2)
        totals = {i: base[i][...] if base[i].shape[1] == part else base[i][:, columns] for i in pair}
        for flip, hidden, down in zip(flips, experts[::2], experts[1::2]):
            span = slice(blocks[first] * height, (blocks[first] + 2) * height)
            value = rounded(dot(hidden[span, :], down[...]))
            for i in pair:
                weight = token_weight(rows[i][:, width:], placement[me ^ far ^ flip], count)
                at = (i - first) * height
                totals[i] = totals[i] + value[at : at + height, :] * weight
        for i in pair:
            outs[i][...] = totals[i].astype(outs[i].dtype)


def finish_kernel(ours, *refs):
    out = refs[-1]
    for flip, parts in ((0, refs[:ours]), (1, refs[ours:-1])):
        width = parts[0].shape[1]
        half = (lax.axis_index("dp") + flip) % 2
        total = parts[0][...]
        for part in parts[1:]:
            total = total + part[...].astype(jnp.float32)
        out[:, pl.ds(pl.multiple_of(half * width, width), width)] = total.astype(out.dtype)


def call(kernel, out_shape, args, scratch=(), scalars=0):
    vmem = pl.BlockSpec(memory_space=pltpu.VMEM)
    smem = pl.BlockSpec(memory_space=pltpu.SMEM)
    return pl.pallas_call(
        kernel,
        out_shape=out_shape,
        in_specs=[smem] * scalars + [vmem] * (len(args) - scalars),
        out_specs=jax.tree.map(lambda _: vmem, out_shape),
        scratch_shapes=list(scratch),
        compiler_params=pltpu.CompilerParams(vmem_limit_bytes=VMEM_LIMIT),
        cost_estimate=pl.CostEstimate(flops=0, bytes_accessed=0, transcendentals=0),
    )(*args)


def run_copies(copies, sems):
    copies = [pltpu.make_async_copy(a, b, sems.at[i]) for i, (a, b) in enumerate(copies)]
    for copy in copies:
        copy.start()
    for copy in copies:
        copy.wait()


def part_of(ref, axis, half, size):
    span = pl.ds(pl.multiple_of(half * size, size), size)
    return ref.at[span, :] if axis == 0 else ref.at[:, span]


def store_kernel(axis, first, flags, own, came, other, out, sems):
    half = lax.axis_index("dp") % 2
    size = out.shape[axis] // 2
    taken = flags[lax.axis_index("expert")] == 1

    @pl.when(taken)
    def _():
        if axis == 0:
            parts = [ref.at[pl.ds(first, size), :] for ref in (came, other)]
        else:
            parts = [came, other]
        run_copies(
            [
                (parts[0], part_of(out, axis, half, size)),
                (parts[1], part_of(out, axis, 1 - half, size)),
            ],
            sems,
        )

    @pl.when(jnp.logical_not(taken))
    def _():
        run_copies([(own, out)], sems)


def store(axis, first, flags, own, came, other):
    vmem = pl.BlockSpec(memory_space=pltpu.VMEM)
    return pl.pallas_call(
        functools.partial(store_kernel, axis, first),
        out_shape=jax.ShapeDtypeStruct(own.shape, own.dtype),
        in_specs=[pl.BlockSpec(memory_space=pltpu.SMEM)] + [vmem] * 3,
        out_specs=pl.BlockSpec(memory_space=pl.ANY),
        scratch_shapes=[pltpu.SemaphoreType.DMA((2,))],
        compiler_params=pltpu.CompilerParams(vmem_limit_bytes=8 * 2**20),
        cost_estimate=pl.CostEstimate(flops=0, bytes_accessed=0, transcendentals=0),
    )(flags, own, came, other)


def after(value, *others):
    return lax.optimization_barrier((value, *others))[0]


def per_device(tokens, expert_ids, gate_probs, w_gate, w_up, w_down, placement, swap_flags):
    count = lax.axis_size("expert")
    couple = lax.axis_index("dp") % 2
    half_axis = count // 2
    height, width = tokens.shape
    own = (w_gate[0], w_up[0], w_down[0])
    ff = own[0].shape[1]
    trades = [(d, d ^ 1) for d in range(lax.axis_size("dp"))]

    def send(value, bit, name):
        with jax.named_scope(name):
            return lax.ppermute(value, "expert", [(d, d ^ bit) for d in range(count)])

    def trade(value):
        with jax.named_scope("trade"):
            return lax.ppermute(value, "dp", trades)

    depth, part = own[0].shape[0] // 2, width // 2

    def half_of(first, second):
        return jnp.where(couple == 0, first, second)

    upper = [half_of(w[:depth], w[depth:]) for w in own[:2]]
    lower = half_of(own[2][:, :part], own[2][:, part:])

    bits = []
    bit = half_axis // 2
    while bit > 1:
        bits.append(bit)
        bit //= 2
    blocks = {0: pack_gates(tokens, expert_ids, gate_probs, count)}
    masks = {0: 0}
    z_upper = [send(w, half_axis, "swap") for w in upper]
    for stage, bit in enumerate(bits):
        for i in sorted(blocks):
            last = (i | 1 << stage) + 1 == 1 << len(bits)
            block = after(blocks[i], z_upper[0]) if last else blocks[i]
            blocks[i | 1 << stage] = send(block, bit, "tokens")
            masks[i | 1 << stage] = masks[i] ^ bit
    rows = [blocks[i] for i in range(len(blocks))]

    y_upper = [trade(z_upper[0])]
    y_upper.append(trade(after(z_upper[1], y_upper[0])))
    near = [send(after(w, z_upper[0], lower, upper[1], *rows[1:-1]), 1, "near") for w in own]
    z_lower = send(after(lower, z_upper[1]), half_axis, "swap")

    firsts = list(reversed(range(0, len(rows), 2)))
    scratch = [pltpu.VMEM((2 * height, width), jnp.bfloat16)]
    base = {}
    for first in firsts:
        base[first] = call(
            functools.partial(near_kernel, count),
            [jax.ShapeDtypeStruct((height, width), jnp.float32)] * 2,
            [placement, *rows[first : first + 2], *own, *near],
            scratch,
            scalars=1,
        )

    arrived = after(z_lower, base)
    y_lower = trade(arrived)
    z_near = [send(w, 1, "z_near") for w in (*z_upper, arrived)]
    y_near = [send(y_upper[0], 1, "y_near"), send(after(y_upper[1], arrived), 1, "y_near")]
    hidden = [
        call(
            functools.partial(hidden_kernel, len(rows), width),
            jax.ShapeDtypeStruct((len(rows) * height, ff), jnp.bfloat16),
            [*rows, *own_part, *other_part],
            scratch,
        )
        for own_part, other_part in ((z_upper, y_upper), (z_near[:2], y_near[:2]))
    ]

    def far_sums(flips, downs, half_flip, blocks, sums, last):
        kinds = [jnp.bfloat16 if last and i > 0 else jnp.float32 for i in blocks]
        experts = [x for flip, down in zip(flips, downs) for x in (hidden[flip], down)]
        out = call(
            functools.partial(down_kernel, count, flips, blocks, half_flip),
            [jax.ShapeDtypeStruct((height, part), kind) for kind in kinds],
            [placement, *(rows[i] for i in blocks), *experts, *(sums[i] for i in blocks)],
            scalars=1,
        )
        return dict(zip(blocks, out))

    def collect(parts):
        return [parts[0]] + [send(parts[i], masks[i], "sums") for i in reversed(range(1, len(parts)))]

    near_sums = [x for first in reversed(firsts) for x in base[first]]
    parts = {}
    for first in firsts:
        parts |= far_sums((0, 1), [arrived, z_near[2]], 0, (first, first + 1), near_sums, True)
    flags = after(swap_flags, parts)
    stored = [
        store(0, 0, flags, own[0], z_upper[0], y_upper[0]),
        store(0, 0, flags, own[1], z_upper[1], y_upper[1]),
    ]
    ours = collect(parts)
    landed = after(y_lower, stored, ours[1:-1])
    y_near.append(send(landed, 1, "y_near"))
    everyone = tuple(range(len(rows)))
    last_sums = far_sums((0,), [landed], 1, everyone, near_sums, False)
    last_parts = {}
    for first in firsts:
        last_parts |= far_sums((1,), [y_near[2]], 1, (first, first + 1), last_sums, True)
    stored.append(store(1, 0, after(swap_flags, last_parts), own[2], z_lower, y_lower))
    others = collect(last_parts)
    mixed = call(
        functools.partial(finish_kernel, len(ours)),
        jax.ShapeDtypeStruct((height, width), tokens.dtype),
        [*ours, *others],
    )
    return (mixed, *(w[None] for w in stored))


def solution(mesh):
    in_specs = (
        P(("dp", "expert"), None),
        P(("dp", "expert"), None),
        P(("dp", "expert"), None),
        P("expert", None, None),
        P("expert", None, None),
        P("expert", None, None),
        P(),
        P(),
    )
    out_specs = (
        P(("dp", "expert"), None),
        P(("dp", "expert"), None, None),
        P(("dp", "expert"), None, None),
        P(("dp", "expert"), None, None),
    )
    return jax.shard_map(
        per_device, mesh=mesh, in_specs=in_specs, out_specs=out_specs, check_vma=False
    )
```

```python
import functools

import jax
import jax.numpy as jnp
from jax import lax
from jax.experimental import pallas as pl
from jax.experimental.pallas import tpu as pltpu
from jax.sharding import PartitionSpec as P

LANES = 128
VMEM_LIMIT = 20 * 2**20


def split_parts(values):
    parts = []
    for _ in range(3):
        part = lax.reduce_precision(values, exponent_bits=8, mantissa_bits=7)
        parts.append(part.astype(jnp.bfloat16))
        values = values - part
    return parts


def pack_gates(tokens, expert_ids, gate_probs, count):
    experts = jnp.arange(count, dtype=jnp.int32)
    chosen = expert_ids[:, None, :] == experts[None, :, None]
    weights = jnp.sum(jnp.where(chosen, gate_probs[:, None, :], 0.0), axis=2)
    parts = jnp.concatenate(split_parts(weights), axis=1)
    parts = jnp.pad(parts, ((0, 0), (0, -parts.shape[1] % LANES)))
    return jnp.concatenate([tokens, parts], axis=1)


def dot(a, b):
    return jnp.dot(a, b, preferred_element_type=jnp.float32)


def token_weight(tail, expert, count):
    lane = lax.broadcasted_iota(jnp.int32, tail.shape, 1)
    mine = (lane % count == expert) & (lane < 3 * count)
    return jnp.sum(jnp.where(mine, tail.astype(jnp.float32), 0.0), axis=1, keepdims=True)


def activate(gate, up):
    return (gate / (1.0 + jnp.exp(-gate)) * up).astype(jnp.bfloat16)


def rounded(value):
    return value.astype(jnp.bfloat16).astype(jnp.float32)


def near_kernel(count, placement, *refs):
    rows, weights, outs, x = refs[:2], (refs[2:5], refs[5:8]), refs[8:10], refs[10]
    height, width = rows[0].shape[0], x.shape[1]
    me = lax.axis_index("expert")
    for i in range(2):
        x[i * height : (i + 1) * height, :] = rows[i][:, :width]
    totals = [0.0, 0.0]
    for flip, (g, u, d) in enumerate(weights):
        hidden = activate(dot(x[...], g[...]), dot(x[...], u[...]))
        value = rounded(dot(hidden, d[...]))
        for i in range(2):
            weight = token_weight(rows[i][:, width:], placement[me ^ flip], count)
            totals[i] = totals[i] + value[i * height : (i + 1) * height, :] * weight
    for i in range(2):
        outs[i][...] = totals[i]


def hidden_kernel(blocks, width, *refs):
    rows, own, other, out, x = refs[:blocks], refs[blocks], refs[blocks + 1], refs[blocks + 2], refs[blocks + 3]
    height = rows[0].shape[0]
    half = lax.axis_index("dp") % 2
    depth = own.shape[0] // 2
    at = pl.multiple_of(half * depth, depth)
    off = pl.multiple_of(depth - at, depth)
    for first in range(0, blocks, 2):
        for i in range(2):
            x[i * height : (i + 1) * height, :] = rows[first + i][:, :width]
        xa, xb = x[:, pl.ds(at, depth)], x[:, pl.ds(off, depth)]
        gate = dot(xa, own[:depth, :]) + dot(xb, other[:depth, :])
        up = dot(xa, own[depth:, :]) + dot(xb, other[depth:, :])
        out[first * height : (first + 2) * height, :] = activate(gate, up)


def down_kernel(count, flips, blocks, half_flip, placement, *refs):
    number = len(blocks)
    rows, refs = refs[:number], refs[number:]
    experts, refs = refs[: 2 * len(flips)], refs[2 * len(flips) :]
    base, outs = refs[:number], refs[number:]
    height, part = outs[0].shape
    width = 2 * part
    me = lax.axis_index("expert")
    far = lax.axis_size("expert") // 2
    half = (lax.axis_index("dp") + half_flip) % 2
    columns = pl.ds(pl.multiple_of(half * part, part), part)
    for first in range(0, number, 2):
        pair = range(first, first + 2)
        totals = {i: base[i][...] if base[i].shape[1] == part else base[i][:, columns] for i in pair}
        for flip, hidden, down in zip(flips, experts[::2], experts[1::2]):
            span = slice(blocks[first] * height, (blocks[first] + 2) * height)
            value = rounded(dot(hidden[span, :], down[...]))
            for i in pair:
                weight = token_weight(rows[i][:, width:], placement[me ^ far ^ flip], count)
                at = (i - first) * height
                totals[i] = totals[i] + value[at : at + height, :] * weight
        for i in pair:
            outs[i][...] = totals[i].astype(outs[i].dtype)


def finish_kernel(ours, *refs):
    out = refs[-1]
    for flip, parts in ((0, refs[:ours]), (1, refs[ours:-1])):
        width = parts[0].shape[1]
        half = (lax.axis_index("dp") + flip) % 2
        total = parts[0][...]
        for part in parts[1:]:
            total = total + part[...].astype(jnp.float32)
        out[:, pl.ds(pl.multiple_of(half * width, width), width)] = total.astype(out.dtype)


def call(kernel, out_shape, args, scratch=(), scalars=0):
    vmem = pl.BlockSpec(memory_space=pltpu.VMEM)
    smem = pl.BlockSpec(memory_space=pltpu.SMEM)
    return pl.pallas_call(
        kernel,
        out_shape=out_shape,
        in_specs=[smem] * scalars + [vmem] * (len(args) - scalars),
        out_specs=jax.tree.map(lambda _: vmem, out_shape),
        scratch_shapes=list(scratch),
        compiler_params=pltpu.CompilerParams(vmem_limit_bytes=VMEM_LIMIT),
        cost_estimate=pl.CostEstimate(flops=0, bytes_accessed=0, transcendentals=0),
    )(*args)


def run_copies(copies, sems):
    copies = [pltpu.make_async_copy(a, b, sems.at[i]) for i, (a, b) in enumerate(copies)]
    for copy in copies:
        copy.start()
    for copy in copies:
        copy.wait()


def part_of(ref, axis, half, size):
    span = pl.ds(pl.multiple_of(half * size, size), size)
    return ref.at[span, :] if axis == 0 else ref.at[:, span]


def store_kernel(axis, first, flags, own, came, other, out, sems):
    half = lax.axis_index("dp") % 2
    size = out.shape[axis] // 2
    taken = flags[lax.axis_index("expert")] == 1

    @pl.when(taken)
    def _():
        if axis == 0:
            parts = [ref.at[pl.ds(first, size), :] for ref in (came, other)]
        else:
            parts = [came, other]
        run_copies(
            [
                (parts[0], part_of(out, axis, half, size)),
                (parts[1], part_of(out, axis, 1 - half, size)),
            ],
            sems,
        )

    @pl.when(jnp.logical_not(taken))
    def _():
        run_copies([(own, out)], sems)


def store(axis, first, flags, own, came, other):
    vmem = pl.BlockSpec(memory_space=pltpu.VMEM)
    return pl.pallas_call(
        functools.partial(store_kernel, axis, first),
        out_shape=jax.ShapeDtypeStruct(own.shape, own.dtype),
        in_specs=[pl.BlockSpec(memory_space=pltpu.SMEM)] + [vmem] * 3,
        out_specs=pl.BlockSpec(memory_space=pl.ANY),
        scratch_shapes=[pltpu.SemaphoreType.DMA((2,))],
        compiler_params=pltpu.CompilerParams(vmem_limit_bytes=8 * 2**20),
        cost_estimate=pl.CostEstimate(flops=0, bytes_accessed=0, transcendentals=0),
    )(flags, own, came, other)


def after(value, *others):
    return lax.optimization_barrier((value, *others))[0]


def per_device(tokens, expert_ids, gate_probs, w_gate, w_up, w_down, placement, swap_flags):
    count = lax.axis_size("expert")
    couple = lax.axis_index("dp") % 2
    half_axis = count // 2
    height, width = tokens.shape
    own = (w_gate[0], w_up[0], w_down[0])
    ff = own[0].shape[1]
    trades = [(d, d ^ 1) for d in range(lax.axis_size("dp"))]

    def send(value, bit, name):
        with jax.named_scope(name):
            return lax.ppermute(value, "expert", [(d, d ^ bit) for d in range(count)])

    def trade(value):
        with jax.named_scope("trade"):
            return lax.ppermute(value, "dp", trades)

    depth, part = own[0].shape[0] // 2, width // 2

    def half_of(first, second):
        return jnp.where(couple == 0, first, second)

    upper = half_of(
        jnp.concatenate([own[0][:depth], own[1][:depth]], axis=0),
        jnp.concatenate([own[0][depth:], own[1][depth:]], axis=0),
    )
    lower = half_of(own[2][:, :part], own[2][:, part:])

    bits = []
    bit = half_axis // 2
    while bit > 1:
        bits.append(bit)
        bit //= 2
    blocks = {0: pack_gates(tokens, expert_ids, gate_probs, count)}
    masks = {0: 0}
    for stage, bit in enumerate(bits):
        for i in sorted(blocks):
            blocks[i | 1 << stage] = send(blocks[i], bit, "tokens")
            masks[i | 1 << stage] = masks[i] ^ bit
    rows = [blocks[i] for i in range(len(blocks))]

    z_upper = send(upper, half_axis, "swap")
    z_lower = send(after(lower, z_upper, *rows), half_axis, "swap")
    y_upper = trade(after(z_upper, *rows))
    near = [send(after(w, lower), 1, "near") for w in own]

    firsts = list(reversed(range(0, len(rows), 2)))
    scratch = [pltpu.VMEM((2 * height, width), jnp.bfloat16)]
    base = {}
    for first in firsts:
        base[first] = call(
            functools.partial(near_kernel, count),
            [jax.ShapeDtypeStruct((height, width), jnp.float32)] * 2,
            [placement, *rows[first : first + 2], *own, *near],
            scratch,
            scalars=1,
        )

    arrived = after(z_lower, base)
    y_lower = trade(arrived)
    z_near = [send(z_upper, 1, "z_near"), send(arrived, 1, "z_near")]
    y_near = [send(after(y_upper, arrived), 1, "y_near")]
    hidden = [
        call(
            functools.partial(hidden_kernel, len(rows), width),
            jax.ShapeDtypeStruct((len(rows) * height, ff), jnp.bfloat16),
            [*rows, own_part, other_part],
            scratch,
        )
        for own_part, other_part in ((z_upper, y_upper), (z_near[0], y_near[0]))
    ]

    def far_sums(flips, downs, half_flip, blocks, sums, last):
        kinds = [jnp.bfloat16 if last and i > 0 else jnp.float32 for i in blocks]
        experts = [x for flip, down in zip(flips, downs) for x in (hidden[flip], down)]
        out = call(
            functools.partial(down_kernel, count, flips, blocks, half_flip),
            [jax.ShapeDtypeStruct((height, part), kind) for kind in kinds],
            [placement, *(rows[i] for i in blocks), *experts, *(sums[i] for i in blocks)],
            scalars=1,
        )
        return dict(zip(blocks, out))

    def collect(parts):
        return [parts[0]] + [send(parts[i], masks[i], "sums") for i in reversed(range(1, len(parts)))]

    near_sums = [x for first in reversed(firsts) for x in base[first]]
    parts = {}
    for first in firsts:
        parts |= far_sums((0, 1), [arrived, z_near[1]], 0, (first, first + 1), near_sums, True)
    flags = after(swap_flags, parts)
    stored = [
        store(0, 0, flags, own[0], z_upper, y_upper),
        store(0, depth, flags, own[1], z_upper, y_upper),
    ]
    ours = collect(parts)
    landed = after(y_lower, stored, ours[1 : len(ours) // 2])
    y_near.append(send(landed, 1, "y_near"))
    everyone = tuple(range(len(rows)))
    last_sums = far_sums((0,), [landed], 1, everyone, near_sums, False)
    last_parts = {}
    for first in firsts:
        last_parts |= far_sums((1,), [y_near[1]], 1, (first, first + 1), last_sums, True)
    stored.append(store(1, 0, after(swap_flags, last_parts), own[2], z_lower, y_lower))
    others = collect(last_parts)
    mixed = call(
        functools.partial(finish_kernel, len(ours)),
        jax.ShapeDtypeStruct((height, width), tokens.dtype),
        [*ours, *others],
    )
    return (mixed, *(w[None] for w in stored))


def solution(mesh):
    in_specs = (
        P(("dp", "expert"), None),
        P(("dp", "expert"), None),
        P(("dp", "expert"), None),
        P("expert", None, None),
        P("expert", None, None),
        P("expert", None, None),
        P(),
        P(),
    )
    out_specs = (
        P(("dp", "expert"), None),
        P(("dp", "expert"), None, None),
        P(("dp", "expert"), None, None),
        P(("dp", "expert"), None, None),
    )
    return jax.shard_map(
        per_device, mesh=mesh, in_specs=in_specs, out_specs=out_specs, check_vma=False
    )
```

```python
import functools

import jax
import jax.numpy as jnp
from jax import lax
from jax.experimental import pallas as pl
from jax.experimental.pallas import tpu as pltpu
from jax.sharding import PartitionSpec as P

LANES = 128
VMEM_LIMIT = 20 * 2**20


def split_parts(values):
    parts = []
    for _ in range(3):
        part = lax.reduce_precision(values, exponent_bits=8, mantissa_bits=7)
        parts.append(part.astype(jnp.bfloat16))
        values = values - part
    return parts


def pack_gates(tokens, expert_ids, gate_probs, count):
    experts = jnp.arange(count, dtype=jnp.int32)
    chosen = expert_ids[:, None, :] == experts[None, :, None]
    weights = jnp.sum(jnp.where(chosen, gate_probs[:, None, :], 0.0), axis=2)
    parts = jnp.concatenate(split_parts(weights), axis=1)
    parts = jnp.pad(parts, ((0, 0), (0, -parts.shape[1] % LANES)))
    return jnp.concatenate([tokens, parts], axis=1)


def dot(a, b):
    return jnp.dot(a, b, preferred_element_type=jnp.float32)


def token_weight(tail, expert, count):
    lane = lax.broadcasted_iota(jnp.int32, tail.shape, 1)
    mine = (lane % count == expert) & (lane < 3 * count)
    return jnp.sum(jnp.where(mine, tail.astype(jnp.float32), 0.0), axis=1, keepdims=True)


def activate(gate, up):
    return (gate / (1.0 + jnp.exp(-gate)) * up).astype(jnp.bfloat16)


def rounded(value):
    return value.astype(jnp.bfloat16).astype(jnp.float32)


def near_kernel(count, placement, *refs):
    rows, weights, outs, x = refs[:2], (refs[2:5], refs[5:8]), refs[8:10], refs[10]
    height, width = rows[0].shape[0], x.shape[1]
    me = lax.axis_index("expert")
    for i in range(2):
        x[i * height : (i + 1) * height, :] = rows[i][:, :width]
    totals = [0.0, 0.0]
    for flip, (g, u, d) in enumerate(weights):
        hidden = activate(dot(x[...], g[...]), dot(x[...], u[...]))
        value = rounded(dot(hidden, d[...]))
        for i in range(2):
            weight = token_weight(rows[i][:, width:], placement[me ^ flip], count)
            totals[i] = totals[i] + value[i * height : (i + 1) * height, :] * weight
    for i in range(2):
        outs[i][...] = totals[i]


def hidden_kernel(blocks, width, *refs):
    rows, own, other, out, x = refs[:blocks], refs[blocks], refs[blocks + 1], refs[blocks + 2], refs[blocks + 3]
    height = rows[0].shape[0]
    half = lax.axis_index("dp") % 2
    depth = own.shape[0] // 2
    at = pl.multiple_of(half * depth, depth)
    off = pl.multiple_of(depth - at, depth)
    for first in range(0, blocks, 2):
        for i in range(2):
            x[i * height : (i + 1) * height, :] = rows[first + i][:, :width]
        xa, xb = x[:, pl.ds(at, depth)], x[:, pl.ds(off, depth)]
        gate = dot(xa, own[:depth, :]) + dot(xb, other[:depth, :])
        up = dot(xa, own[depth:, :]) + dot(xb, other[depth:, :])
        out[first * height : (first + 2) * height, :] = activate(gate, up)


def down_kernel(count, flips, blocks, half_flip, placement, *refs):
    number = len(blocks)
    rows, refs = refs[:number], refs[number:]
    experts, refs = refs[: 2 * len(flips)], refs[2 * len(flips) :]
    base, outs = refs[:number], refs[number:]
    height, part = outs[0].shape
    width = 2 * part
    me = lax.axis_index("expert")
    far = lax.axis_size("expert") // 2
    half = (lax.axis_index("dp") + half_flip) % 2
    columns = pl.ds(pl.multiple_of(half * part, part), part)
    for first in range(0, number, 2):
        pair = range(first, first + 2)
        totals = {i: base[i][...] if base[i].shape[1] == part else base[i][:, columns] for i in pair}
        for flip, hidden, down in zip(flips, experts[::2], experts[1::2]):
            span = slice(blocks[first] * height, (blocks[first] + 2) * height)
            value = rounded(dot(hidden[span, :], down[...]))
            for i in pair:
                weight = token_weight(rows[i][:, width:], placement[me ^ far ^ flip], count)
                at = (i - first) * height
                totals[i] = totals[i] + value[at : at + height, :] * weight
        for i in pair:
            outs[i][...] = totals[i].astype(outs[i].dtype)


def finish_kernel(ours, *refs):
    out = refs[-1]
    for flip, parts in ((0, refs[:ours]), (1, refs[ours:-1])):
        width = parts[0].shape[1]
        half = (lax.axis_index("dp") + flip) % 2
        total = parts[0][...]
        for part in parts[1:]:
            total = total + part[...].astype(jnp.float32)
        out[:, pl.ds(pl.multiple_of(half * width, width), width)] = total.astype(out.dtype)


def call(kernel, out_shape, args, scratch=(), scalars=0):
    vmem = pl.BlockSpec(memory_space=pltpu.VMEM)
    smem = pl.BlockSpec(memory_space=pltpu.SMEM)
    return pl.pallas_call(
        kernel,
        out_shape=out_shape,
        in_specs=[smem] * scalars + [vmem] * (len(args) - scalars),
        out_specs=jax.tree.map(lambda _: vmem, out_shape),
        scratch_shapes=list(scratch),
        compiler_params=pltpu.CompilerParams(vmem_limit_bytes=VMEM_LIMIT),
        cost_estimate=pl.CostEstimate(flops=0, bytes_accessed=0, transcendentals=0),
    )(*args)


def run_copies(copies, sems):
    copies = [pltpu.make_async_copy(a, b, sems.at[i]) for i, (a, b) in enumerate(copies)]
    for copy in copies:
        copy.start()
    for copy in copies:
        copy.wait()


def part_of(ref, axis, half, size):
    span = pl.ds(pl.multiple_of(half * size, size), size)
    return ref.at[span, :] if axis == 0 else ref.at[:, span]


def store_kernel(axis, first, flags, own, came, other, out, sems):
    half = lax.axis_index("dp") % 2
    size = out.shape[axis] // 2
    taken = flags[lax.axis_index("expert")] == 1

    @pl.when(taken)
    def _():
        if axis == 0:
            parts = [ref.at[pl.ds(first, size), :] for ref in (came, other)]
        else:
            parts = [came, other]
        run_copies(
            [
                (parts[0], part_of(out, axis, half, size)),
                (parts[1], part_of(out, axis, 1 - half, size)),
            ],
            sems,
        )

    @pl.when(jnp.logical_not(taken))
    def _():
        run_copies([(own, out)], sems)


def store(axis, first, flags, own, came, other):
    vmem = pl.BlockSpec(memory_space=pltpu.VMEM)
    return pl.pallas_call(
        functools.partial(store_kernel, axis, first),
        out_shape=jax.ShapeDtypeStruct(own.shape, own.dtype),
        in_specs=[pl.BlockSpec(memory_space=pltpu.SMEM)] + [vmem] * 3,
        out_specs=pl.BlockSpec(memory_space=pl.ANY),
        scratch_shapes=[pltpu.SemaphoreType.DMA((2,))],
        compiler_params=pltpu.CompilerParams(vmem_limit_bytes=8 * 2**20),
        cost_estimate=pl.CostEstimate(flops=0, bytes_accessed=0, transcendentals=0),
    )(flags, own, came, other)


def after(value, *others):
    return lax.optimization_barrier((value, *others))[0]


def per_device(tokens, expert_ids, gate_probs, w_gate, w_up, w_down, placement, swap_flags):
    count = lax.axis_size("expert")
    couple = lax.axis_index("dp") % 2
    half_axis = count // 2
    height, width = tokens.shape
    own = (w_gate[0], w_up[0], w_down[0])
    ff = own[0].shape[1]
    trades = [(d, d ^ 1) for d in range(lax.axis_size("dp"))]

    def send(value, bit, name):
        with jax.named_scope(name):
            return lax.ppermute(value, "expert", [(d, d ^ bit) for d in range(count)])

    def trade(value):
        with jax.named_scope("trade"):
            return lax.ppermute(value, "dp", trades)

    depth, part = own[0].shape[0] // 2, width // 2

    def half_of(first, second):
        return jnp.where(couple == 0, first, second)

    upper = half_of(
        jnp.concatenate([own[0][:depth], own[1][:depth]], axis=0),
        jnp.concatenate([own[0][depth:], own[1][depth:]], axis=0),
    )
    lower = half_of(own[2][:, :part], own[2][:, part:])

    bits = []
    bit = half_axis // 2
    while bit > 1:
        bits.append(bit)
        bit //= 2
    blocks = {0: pack_gates(tokens, expert_ids, gate_probs, count)}
    masks = {0: 0}
    for stage, bit in enumerate(bits):
        for i in sorted(blocks):
            blocks[i | 1 << stage] = send(blocks[i], bit, "tokens")
            masks[i | 1 << stage] = masks[i] ^ bit
    rows = [blocks[i] for i in range(len(blocks))]

    z_upper = send(upper, half_axis, "swap")
    z_lower = send(after(lower, z_upper, *rows), half_axis, "swap")
    y_upper = trade(after(z_upper, *rows))
    near = [send(after(w, lower), 1, "near") for w in own]

    firsts = list(reversed(range(0, len(rows), 2)))
    scratch = [pltpu.VMEM((2 * height, width), jnp.bfloat16)]
    base = {}
    for first in firsts:
        base[first] = call(
            functools.partial(near_kernel, count),
            [jax.ShapeDtypeStruct((height, width), jnp.float32)] * 2,
            [placement, *rows[first : first + 2], *own, *near],
            scratch,
            scalars=1,
        )

    def hidden_units(*halves):
        return call(
            functools.partial(hidden_kernel, len(rows), width),
            jax.ShapeDtypeStruct((len(rows) * height, ff), jnp.bfloat16),
            [*rows, *halves],
            scratch,
        )

    hidden = [hidden_units(z_upper, y_upper)]
    arrived = after(z_lower, base, hidden[0])
    y_lower = trade(arrived)
    z_near = [send(z_upper, 1, "z_near"), send(arrived, 1, "z_near")]
    y_near = [send(after(y_upper, arrived), 1, "y_near")]
    hidden.append(hidden_units(z_near[0], y_near[0]))

    def far_sums(flips, downs, half_flip, blocks, sums, last):
        kinds = [jnp.bfloat16 if last and i > 0 else jnp.float32 for i in blocks]
        experts = [x for flip, down in zip(flips, downs) for x in (hidden[flip], down)]
        out = call(
            functools.partial(down_kernel, count, flips, blocks, half_flip),
            [jax.ShapeDtypeStruct((height, part), kind) for kind in kinds],
            [placement, *(rows[i] for i in blocks), *experts, *(sums[i] for i in blocks)],
            scalars=1,
        )
        return dict(zip(blocks, out))

    def collect(parts):
        return [parts[0]] + [send(parts[i], masks[i], "sums") for i in reversed(range(1, len(parts)))]

    near_sums = [x for first in reversed(firsts) for x in base[first]]
    parts = {}
    for first in firsts:
        parts |= far_sums((0, 1), [arrived, z_near[1]], 0, (first, first + 1), near_sums, True)
    flags = after(swap_flags, parts)
    stored = [
        store(0, 0, flags, own[0], z_upper, y_upper),
        store(0, depth, flags, own[1], z_upper, y_upper),
    ]
    ours = collect(parts)
    landed = after(y_lower, stored, ours[1:-1])
    y_near.append(send(landed, 1, "y_near"))
    everyone = tuple(range(len(rows)))
    last_sums = far_sums((0,), [landed], 1, everyone, near_sums, False)
    last_parts = {}
    for first in firsts:
        last_parts |= far_sums((1,), [y_near[1]], 1, (first, first + 1), last_sums, True)
    stored.append(store(1, 0, after(swap_flags, last_parts), own[2], z_lower, y_lower))
    others = collect(last_parts)
    mixed = call(
        functools.partial(finish_kernel, len(ours)),
        jax.ShapeDtypeStruct((height, width), tokens.dtype),
        [*ours, *others],
    )
    return (mixed, *(w[None] for w in stored))


def solution(mesh):
    in_specs = (
        P(("dp", "expert"), None),
        P(("dp", "expert"), None),
        P(("dp", "expert"), None),
        P("expert", None, None),
        P("expert", None, None),
        P("expert", None, None),
        P(),
        P(),
    )
    out_specs = (
        P(("dp", "expert"), None),
        P(("dp", "expert"), None, None),
        P(("dp", "expert"), None, None),
        P(("dp", "expert"), None, None),
    )
    return jax.shard_map(
        per_device, mesh=mesh, in_specs=in_specs, out_specs=out_specs, check_vma=False
    )
```

```python
import functools

import jax
import jax.numpy as jnp
from jax import lax
from jax.experimental import pallas as pl
from jax.experimental.pallas import tpu as pltpu
from jax.sharding import PartitionSpec as P

LANES = 128
VMEM_LIMIT = 20 * 2**20


def split_parts(values):
    parts = []
    for _ in range(3):
        part = lax.reduce_precision(values, exponent_bits=8, mantissa_bits=7)
        parts.append(part.astype(jnp.bfloat16))
        values = values - part
    return parts


def pack_gates(tokens, expert_ids, gate_probs, count):
    experts = jnp.arange(count, dtype=jnp.int32)
    chosen = expert_ids[:, None, :] == experts[None, :, None]
    weights = jnp.sum(jnp.where(chosen, gate_probs[:, None, :], 0.0), axis=2)
    parts = jnp.concatenate(split_parts(weights), axis=1)
    parts = jnp.pad(parts, ((0, 0), (0, -parts.shape[1] % LANES)))
    return jnp.concatenate([tokens, parts], axis=1)


def dot(a, b):
    return jnp.dot(a, b, preferred_element_type=jnp.float32)


def token_weight(tail, expert, count):
    lane = lax.broadcasted_iota(jnp.int32, tail.shape, 1)
    mine = (lane % count == expert) & (lane < 3 * count)
    return jnp.sum(jnp.where(mine, tail.astype(jnp.float32), 0.0), axis=1, keepdims=True)


def activate(gate, up):
    return (gate / (1.0 + jnp.exp(-gate)) * up).astype(jnp.bfloat16)


def rounded(value):
    return value.astype(jnp.bfloat16).astype(jnp.float32)


def near_kernel(count, placement, *refs):
    rows, weights, outs, x = refs[:2], (refs[2:5], refs[5:8]), refs[8:10], refs[10]
    height, width = rows[0].shape[0], x.shape[1]
    me = lax.axis_index("expert")
    for i in range(2):
        x[i * height : (i + 1) * height, :] = rows[i][:, :width]
    totals = [0.0, 0.0]
    for flip, (g, u, d) in enumerate(weights):
        hidden = activate(dot(x[...], g[...]), dot(x[...], u[...]))
        value = rounded(dot(hidden, d[...]))
        for i in range(2):
            weight = token_weight(rows[i][:, width:], placement[me ^ flip], count)
            totals[i] = totals[i] + value[i * height : (i + 1) * height, :] * weight
    for i in range(2):
        outs[i][...] = totals[i]


def hidden_kernel(blocks, width, *refs):
    rows, mats, out, x = refs[:blocks], refs[blocks : blocks + 4], refs[blocks + 4], refs[blocks + 5]
    came_gate, came_up, traded_gate, traded_up = mats
    height = rows[0].shape[0]
    half = lax.axis_index("dp") % 2

    def run(g, u):
        for first in range(0, blocks, 2):
            for i in range(2):
                x[i * height : (i + 1) * height, :] = rows[first + i][:, :width]
            units = activate(dot(x[...], g[...]), dot(x[...], u[...]))
            out[first * height : (first + 2) * height, :] = units

    pl.when(half == 0)(lambda: run(came_gate, traded_up))
    pl.when(half == 1)(lambda: run(traded_gate, came_up))


def down_kernel(count, flips, blocks, half_flip, placement, *refs):
    number = len(blocks)
    rows, refs = refs[:number], refs[number:]
    experts, refs = refs[: 2 * len(flips)], refs[2 * len(flips) :]
    base, outs = refs[:number], refs[number:]
    height, part = outs[0].shape
    width = 2 * part
    me = lax.axis_index("expert")
    far = lax.axis_size("expert") // 2
    half = (lax.axis_index("dp") + half_flip) % 2
    columns = pl.ds(pl.multiple_of(half * part, part), part)
    for first in range(0, number, 2):
        pair = range(first, first + 2)
        totals = {i: base[i][...] if base[i].shape[1] == part else base[i][:, columns] for i in pair}
        for flip, hidden, down in zip(flips, experts[::2], experts[1::2]):
            span = slice(blocks[first] * height, (blocks[first] + 2) * height)
            value = rounded(dot(hidden[span, :], down[...]))
            for i in pair:
                weight = token_weight(rows[i][:, width:], placement[me ^ far ^ flip], count)
                at = (i - first) * height
                totals[i] = totals[i] + value[at : at + height, :] * weight
        for i in pair:
            outs[i][...] = totals[i].astype(outs[i].dtype)


def finish_kernel(ours, *refs):
    out = refs[-1]
    for flip, parts in ((0, refs[:ours]), (1, refs[ours:-1])):
        width = parts[0].shape[1]
        half = (lax.axis_index("dp") + flip) % 2
        total = parts[0][...]
        for part in parts[1:]:
            total = total + part[...].astype(jnp.float32)
        out[:, pl.ds(pl.multiple_of(half * width, width), width)] = total.astype(out.dtype)


def call(kernel, out_shape, args, scratch=(), scalars=0):
    vmem = pl.BlockSpec(memory_space=pltpu.VMEM)
    smem = pl.BlockSpec(memory_space=pltpu.SMEM)
    return pl.pallas_call(
        kernel,
        out_shape=out_shape,
        in_specs=[smem] * scalars + [vmem] * (len(args) - scalars),
        out_specs=jax.tree.map(lambda _: vmem, out_shape),
        scratch_shapes=list(scratch),
        compiler_params=pltpu.CompilerParams(vmem_limit_bytes=VMEM_LIMIT),
        cost_estimate=pl.CostEstimate(flops=0, bytes_accessed=0, transcendentals=0),
    )(*args)


def run_copies(copies, sems):
    copies = [pltpu.make_async_copy(a, b, sems.at[i]) for i, (a, b) in enumerate(copies)]
    for copy in copies:
        copy.start()
    for copy in copies:
        copy.wait()


def part_of(ref, axis, half, size):
    span = pl.ds(pl.multiple_of(half * size, size), size)
    return ref.at[span, :] if axis == 0 else ref.at[:, span]


def store_kernel(turn, flags, own, came, other, out, sems):
    half = lax.axis_index("dp") % 2
    taken = flags[lax.axis_index("expert")] == 1

    @pl.when(taken)
    def _():
        if turn is None:
            size = came.shape[1]
            run_copies(
                [
                    (came, part_of(out, 1, half, size)),
                    (other, part_of(out, 1, 1 - half, size)),
                ],
                sems,
            )
        else:
            pl.when(half == turn)(lambda: run_copies([(came, out)], sems))
            pl.when(half != turn)(lambda: run_copies([(other, out)], sems))

    @pl.when(jnp.logical_not(taken))
    def _():
        run_copies([(own, out)], sems)


def store(turn, flags, own, came, other):
    vmem = pl.BlockSpec(memory_space=pltpu.VMEM)
    return pl.pallas_call(
        functools.partial(store_kernel, turn),
        out_shape=jax.ShapeDtypeStruct(own.shape, own.dtype),
        in_specs=[pl.BlockSpec(memory_space=pltpu.SMEM)] + [vmem] * 3,
        out_specs=pl.BlockSpec(memory_space=pl.ANY),
        scratch_shapes=[pltpu.SemaphoreType.DMA((2,))],
        compiler_params=pltpu.CompilerParams(vmem_limit_bytes=8 * 2**20),
        cost_estimate=pl.CostEstimate(flops=0, bytes_accessed=0, transcendentals=0),
    )(flags, own, came, other)


def after(value, *others):
    return lax.optimization_barrier((value, *others))[0]


def per_device(tokens, expert_ids, gate_probs, w_gate, w_up, w_down, placement, swap_flags):
    count = lax.axis_size("expert")
    couple = lax.axis_index("dp") % 2
    half_axis = count // 2
    height, width = tokens.shape
    own = (w_gate[0], w_up[0], w_down[0])
    ff = own[0].shape[1]
    trades = [(d, d ^ 1) for d in range(lax.axis_size("dp"))]

    def send(value, bit, name):
        with jax.named_scope(name):
            return lax.ppermute(value, "expert", [(d, d ^ bit) for d in range(count)])

    def send_in(value, bit, turn, name):
        pairs = [
            (d * count + e, d * count + (e ^ bit))
            for d in range(turn, lax.axis_size("dp"), 2)
            for e in range(count)
        ]
        with jax.named_scope(name):
            return lax.ppermute(value, ("dp", "expert"), pairs)

    def hand_over(value, turn):
        with jax.named_scope("trade"):
            return lax.ppermute(value, "dp", trades[turn::2])

    def trade(value):
        with jax.named_scope("trade"):
            return lax.ppermute(value, "dp", trades)

    part = width // 2

    def half_of(first, second):
        return jnp.where(couple == 0, first, second)

    lower = half_of(own[2][:, :part], own[2][:, part:])

    bits = []
    bit = half_axis // 2
    while bit > 1:
        bits.append(bit)
        bit //= 2
    blocks = {0: pack_gates(tokens, expert_ids, gate_probs, count)}
    masks = {0: 0}
    for stage, bit in enumerate(bits):
        for i in sorted(blocks):
            blocks[i | 1 << stage] = send(blocks[i], bit, "tokens")
            masks[i | 1 << stage] = masks[i] ^ bit
    rows = [blocks[i] for i in range(len(blocks))]

    z_upper = [send_in(own[turn], half_axis, turn, "swap") for turn in (0, 1)]
    z_lower = send(after(lower, z_upper, *rows), half_axis, "swap")
    y_upper = [hand_over(after(z_upper[turn], *rows), turn) for turn in (0, 1)]
    near = [send(after(w, lower), 1, "near") for w in own]

    firsts = list(reversed(range(0, len(rows), 2)))
    scratch = [pltpu.VMEM((2 * height, width), jnp.bfloat16)]
    base = {}
    for first in firsts:
        base[first] = call(
            functools.partial(near_kernel, count),
            [jax.ShapeDtypeStruct((height, width), jnp.float32)] * 2,
            [placement, *rows[first : first + 2], *own, *near],
            scratch,
            scalars=1,
        )

    def hidden_units(*halves):
        return call(
            functools.partial(hidden_kernel, len(rows), width),
            jax.ShapeDtypeStruct((len(rows) * height, ff), jnp.bfloat16),
            [*rows, *halves],
            scratch,
        )

    hidden = [hidden_units(*z_upper, *y_upper)]
    arrived = after(z_lower, base, hidden[0])
    y_lower = trade(arrived)
    z_across = [send_in(z_upper[turn], 1, turn, "z_near") for turn in (0, 1)]
    y_across = [send_in(after(y_upper[turn], arrived), 1, 1 - turn, "y_near") for turn in (0, 1)]
    z_near, y_near = [send(arrived, 1, "z_near")], []
    hidden.append(hidden_units(*z_across, *y_across))

    def far_sums(flips, downs, half_flip, blocks, sums, last):
        kinds = [jnp.bfloat16 if last and i > 0 else jnp.float32 for i in blocks]
        experts = [x for flip, down in zip(flips, downs) for x in (hidden[flip], down)]
        out = call(
            functools.partial(down_kernel, count, flips, blocks, half_flip),
            [jax.ShapeDtypeStruct((height, part), kind) for kind in kinds],
            [placement, *(rows[i] for i in blocks), *experts, *(sums[i] for i in blocks)],
            scalars=1,
        )
        return dict(zip(blocks, out))

    def collect(parts):
        return [parts[0]] + [send(parts[i], masks[i], "sums") for i in reversed(range(1, len(parts)))]

    near_sums = [x for first in reversed(firsts) for x in base[first]]
    parts = {}
    for first in firsts:
        parts |= far_sums((0, 1), [arrived, z_near[0]], 0, (first, first + 1), near_sums, True)
    flags = after(swap_flags, parts)
    stored = [
        store(0, flags, own[0], z_upper[0], y_upper[0]),
        store(1, flags, own[1], z_upper[1], y_upper[1]),
    ]
    ours = collect(parts)
    landed = after(y_lower, stored, ours[1:-1])
    y_near.append(send(landed, 1, "y_near"))
    everyone = tuple(range(len(rows)))
    last_sums = far_sums((0,), [landed], 1, everyone, near_sums, False)
    last_parts = {}
    for first in firsts:
        last_parts |= far_sums((1,), [y_near[0]], 1, (first, first + 1), last_sums, True)
    stored.append(store(None, after(swap_flags, last_parts), own[2], z_lower, y_lower))
    others = collect(last_parts)
    mixed = call(
        functools.partial(finish_kernel, len(ours)),
        jax.ShapeDtypeStruct((height, width), tokens.dtype),
        [*ours, *others],
    )
    return (mixed, *(w[None] for w in stored))


def solution(mesh):
    in_specs = (
        P(("dp", "expert"), None),
        P(("dp", "expert"), None),
        P(("dp", "expert"), None),
        P("expert", None, None),
        P("expert", None, None),
        P("expert", None, None),
        P(),
        P(),
    )
    out_specs = (
        P(("dp", "expert"), None),
        P(("dp", "expert"), None, None),
        P(("dp", "expert"), None, None),
        P(("dp", "expert"), None, None),
    )
    return jax.shard_map(
        per_device, mesh=mesh, in_specs=in_specs, out_specs=out_specs, check_vma=False
    )
```

```python
import functools

import jax
import jax.numpy as jnp
from jax import lax
from jax.experimental import pallas as pl
from jax.experimental.pallas import tpu as pltpu
from jax.sharding import PartitionSpec as P

LANES = 128
VMEM_LIMIT = 20 * 2**20


def split_parts(values):
    parts = []
    for _ in range(3):
        part = lax.reduce_precision(values, exponent_bits=8, mantissa_bits=7)
        parts.append(part.astype(jnp.bfloat16))
        values = values - part
    return parts


def pack_gates(tokens, expert_ids, gate_probs, count):
    experts = jnp.arange(count, dtype=jnp.int32)
    chosen = expert_ids[:, None, :] == experts[None, :, None]
    weights = jnp.sum(jnp.where(chosen, gate_probs[:, None, :], 0.0), axis=2)
    parts = jnp.concatenate(split_parts(weights), axis=1)
    parts = jnp.pad(parts, ((0, 0), (0, -parts.shape[1] % LANES)))
    return jnp.concatenate([tokens, parts], axis=1)


def dot(a, b):
    return jnp.dot(a, b, preferred_element_type=jnp.float32)


def token_weight(tail, expert, count):
    lane = lax.broadcasted_iota(jnp.int32, tail.shape, 1)
    mine = (lane % count == expert) & (lane < 3 * count)
    return jnp.sum(jnp.where(mine, tail.astype(jnp.float32), 0.0), axis=1, keepdims=True)


def activate(gate, up):
    return (gate / (1.0 + jnp.exp(-gate)) * up).astype(jnp.bfloat16)


def rounded(value):
    return value.astype(jnp.bfloat16).astype(jnp.float32)


def near_kernel(count, placement, *refs):
    rows, weights, outs, x = refs[:2], (refs[2:5], refs[5:8]), refs[8:10], refs[10]
    height, width = rows[0].shape[0], x.shape[1]
    me = lax.axis_index("expert")
    for i in range(2):
        x[i * height : (i + 1) * height, :] = rows[i][:, :width]
    totals = [0.0, 0.0]
    for flip, (g, u, d) in enumerate(weights):
        hidden = activate(dot(x[...], g[...]), dot(x[...], u[...]))
        value = rounded(dot(hidden, d[...]))
        for i in range(2):
            weight = token_weight(rows[i][:, width:], placement[me ^ flip], count)
            totals[i] = totals[i] + value[i * height : (i + 1) * height, :] * weight
    for i in range(2):
        outs[i][...] = totals[i]


def hidden_kernel(blocks, width, *refs):
    rows, own, other, out, x = refs[:blocks], refs[blocks], refs[blocks + 1], refs[blocks + 2], refs[blocks + 3]
    height = rows[0].shape[0]
    half = lax.axis_index("dp") % 2
    depth = own.shape[0] // 2
    at = pl.multiple_of(half * depth, depth)
    off = pl.multiple_of(depth - at, depth)
    for first in range(0, blocks, 2):
        for i in range(2):
            x[i * height : (i + 1) * height, :] = rows[first + i][:, :width]
        xa, xb = x[:, pl.ds(at, depth)], x[:, pl.ds(off, depth)]
        gate = dot(xa, own[:depth, :]) + dot(xb, other[:depth, :])
        up = dot(xa, own[depth:, :]) + dot(xb, other[depth:, :])
        out[first * height : (first + 2) * height, :] = activate(gate, up)


def down_kernel(count, flips, blocks, half_flip, placement, *refs):
    number = len(blocks)
    rows, refs = refs[:number], refs[number:]
    experts, refs = refs[: 2 * len(flips)], refs[2 * len(flips) :]
    base, outs = refs[:number], refs[number:]
    height, part = outs[0].shape
    width = 2 * part
    me = lax.axis_index("expert")
    far = lax.axis_size("expert") // 2
    half = (lax.axis_index("dp") + half_flip) % 2
    columns = pl.ds(pl.multiple_of(half * part, part), part)
    for first in range(0, number, 2):
        pair = range(first, first + 2)
        totals = {i: base[i][...] if base[i].shape[1] == part else base[i][:, columns] for i in pair}
        for flip, hidden, down in zip(flips, experts[::2], experts[1::2]):
            span = slice(blocks[first] * height, (blocks[first] + 2) * height)
            value = rounded(dot(hidden[span, :], down[...]))
            for i in pair:
                weight = token_weight(rows[i][:, width:], placement[me ^ far ^ flip], count)
                at = (i - first) * height
                totals[i] = totals[i] + value[at : at + height, :] * weight
        for i in pair:
            outs[i][...] = totals[i].astype(outs[i].dtype)


def finish_kernel(ours, *refs):
    out = refs[-1]
    for flip, parts in ((0, refs[:ours]), (1, refs[ours:-1])):
        width = parts[0].shape[1]
        half = (lax.axis_index("dp") + flip) % 2
        total = parts[0][...]
        for part in parts[1:]:
            total = total + part[...].astype(jnp.float32)
        out[:, pl.ds(pl.multiple_of(half * width, width), width)] = total.astype(out.dtype)


def call(kernel, out_shape, args, scratch=(), scalars=0):
    vmem = pl.BlockSpec(memory_space=pltpu.VMEM)
    smem = pl.BlockSpec(memory_space=pltpu.SMEM)
    return pl.pallas_call(
        kernel,
        out_shape=out_shape,
        in_specs=[smem] * scalars + [vmem] * (len(args) - scalars),
        out_specs=jax.tree.map(lambda _: vmem, out_shape),
        scratch_shapes=list(scratch),
        compiler_params=pltpu.CompilerParams(vmem_limit_bytes=VMEM_LIMIT),
        cost_estimate=pl.CostEstimate(flops=0, bytes_accessed=0, transcendentals=0),
    )(*args)


def run_copies(copies, sems):
    copies = [pltpu.make_async_copy(a, b, sems.at[i]) for i, (a, b) in enumerate(copies)]
    for copy in copies:
        copy.start()
    for copy in copies:
        copy.wait()


def part_of(ref, axis, half, size):
    span = pl.ds(pl.multiple_of(half * size, size), size)
    return ref.at[span, :] if axis == 0 else ref.at[:, span]


def store_kernel(axis, first, flags, own, came, other, out, sems):
    half = lax.axis_index("dp") % 2
    size = out.shape[axis] // 2
    taken = flags[lax.axis_index("expert")] == 1

    @pl.when(taken)
    def _():
        if axis == 0:
            parts = [ref.at[pl.ds(first, size), :] for ref in (came, other)]
        else:
            parts = [came, other]
        run_copies(
            [
                (parts[0], part_of(out, axis, half, size)),
                (parts[1], part_of(out, axis, 1 - half, size)),
            ],
            sems,
        )

    @pl.when(jnp.logical_not(taken))
    def _():
        run_copies([(own, out)], sems)


def store(axis, first, flags, own, came, other):
    vmem = pl.BlockSpec(memory_space=pltpu.VMEM)
    return pl.pallas_call(
        functools.partial(store_kernel, axis, first),
        out_shape=jax.ShapeDtypeStruct(own.shape, own.dtype),
        in_specs=[pl.BlockSpec(memory_space=pltpu.SMEM)] + [vmem] * 3,
        out_specs=pl.BlockSpec(memory_space=pl.ANY),
        scratch_shapes=[pltpu.SemaphoreType.DMA((2,))],
        compiler_params=pltpu.CompilerParams(vmem_limit_bytes=8 * 2**20),
        cost_estimate=pl.CostEstimate(flops=0, bytes_accessed=0, transcendentals=0),
    )(flags, own, came, other)


def after(value, *others):
    return lax.optimization_barrier((value, *others))[0]


def per_device(tokens, expert_ids, gate_probs, w_gate, w_up, w_down, placement, swap_flags):
    count = lax.axis_size("expert")
    couple = lax.axis_index("dp") % 2
    half_axis = count // 2
    height, width = tokens.shape
    own = (w_gate[0], w_up[0], w_down[0])
    ff = own[0].shape[1]
    trades = [(d, d ^ 1) for d in range(lax.axis_size("dp"))]

    def send(value, bit, name):
        with jax.named_scope(name):
            return lax.ppermute(value, "expert", [(d, d ^ bit) for d in range(count)])

    def trade(value):
        with jax.named_scope("trade"):
            return lax.ppermute(value, "dp", trades)

    depth, part = own[0].shape[0] // 2, width // 2

    def half_of(first, second):
        return jnp.where(couple == 0, first, second)

    upper = half_of(
        jnp.concatenate([own[0][:depth], own[1][:depth]], axis=0),
        jnp.concatenate([own[0][depth:], own[1][depth:]], axis=0),
    )
    lower = half_of(own[2][:, :part], own[2][:, part:])

    bits = []
    bit = half_axis // 2
    while bit > 1:
        bits.append(bit)
        bit //= 2
    blocks = {0: pack_gates(tokens, expert_ids, gate_probs, count)}
    masks = {0: 0}
    for stage, bit in enumerate(bits):
        for i in sorted(blocks):
            blocks[i | 1 << stage] = send(blocks[i], bit, "tokens")
            masks[i | 1 << stage] = masks[i] ^ bit
    rows = [blocks[i] for i in range(len(blocks))]

    z_upper = send(upper, half_axis, "swap")
    z_lower = send(after(lower, z_upper, *rows), half_axis, "swap")
    y_upper = trade(after(z_upper, *rows))
    near = [send(after(w, lower), 1, "near") for w in own]

    firsts = list(reversed(range(0, len(rows), 2)))
    scratch = [pltpu.VMEM((2 * height, width), jnp.bfloat16)]
    base = {}
    for first in firsts:
        base[first] = call(
            functools.partial(near_kernel, count),
            [jax.ShapeDtypeStruct((height, width), jnp.float32)] * 2,
            [placement, *rows[first : first + 2], *own, *near],
            scratch,
            scalars=1,
        )

    def hidden_units(*halves):
        return call(
            functools.partial(hidden_kernel, len(rows), width),
            jax.ShapeDtypeStruct((len(rows) * height, ff), jnp.bfloat16),
            [*rows, *halves],
            scratch,
        )

    hidden = [hidden_units(z_upper, y_upper)]
    arrived = after(z_lower, base, hidden[0])
    y_lower = trade(arrived)
    z_near = [send(z_upper, 1, "z_near"), send(arrived, 1, "z_near")]
    y_near = [send(after(y_upper, arrived), 1, "y_near")]
    hidden.append(hidden_units(z_near[0], y_near[0]))

    def far_sums(flips, downs, half_flip, blocks, sums, last):
        kinds = [jnp.bfloat16 if last and i > 0 else jnp.float32 for i in blocks]
        experts = [x for flip, down in zip(flips, downs) for x in (hidden[flip], down)]
        out = call(
            functools.partial(down_kernel, count, flips, blocks, half_flip),
            [jax.ShapeDtypeStruct((height, part), kind) for kind in kinds],
            [placement, *(rows[i] for i in blocks), *experts, *(sums[i] for i in blocks)],
            scalars=1,
        )
        return dict(zip(blocks, out))

    def collect(parts):
        return [parts[0]] + [send(parts[i], masks[i], "sums") for i in reversed(range(1, len(parts)))]

    near_sums = [x for first in reversed(firsts) for x in base[first]]
    parts = {}
    for first in firsts:
        parts |= far_sums((0, 1), [arrived, z_near[1]], 0, (first, first + 1), near_sums, True)
    flags = after(swap_flags, parts)
    stored = [
        store(0, 0, flags, own[0], z_upper, y_upper),
        store(0, depth, flags, own[1], z_upper, y_upper),
    ]
    ours = collect(parts)
    landed = after(y_lower, stored, ours[1 : len(ours) // 2])
    y_near.append(send(landed, 1, "y_near"))
    everyone = tuple(range(len(rows)))
    last_sums = far_sums((0,), [landed], 1, everyone, near_sums, False)
    last_parts = {}
    for first in firsts:
        last_parts |= far_sums((1,), [y_near[1]], 1, (first, first + 1), last_sums, True)
    stored.append(store(1, 0, after(swap_flags, last_parts), own[2], z_lower, y_lower))
    others = collect(last_parts)
    mixed = call(
        functools.partial(finish_kernel, len(ours)),
        jax.ShapeDtypeStruct((height, width), tokens.dtype),
        [*ours, *others],
    )
    return (mixed, *(w[None] for w in stored))


def solution(mesh):
    in_specs = (
        P(("dp", "expert"), None),
        P(("dp", "expert"), None),
        P(("dp", "expert"), None),
        P("expert", None, None),
        P("expert", None, None),
        P("expert", None, None),
        P(),
        P(),
    )
    out_specs = (
        P(("dp", "expert"), None),
        P(("dp", "expert"), None, None),
        P(("dp", "expert"), None, None),
        P(("dp", "expert"), None, None),
    )
    return jax.shard_map(
        per_device, mesh=mesh, in_specs=in_specs, out_specs=out_specs, check_vma=False
    )
```

```python
import functools

import jax
import jax.numpy as jnp
from jax import lax
from jax.experimental import pallas as pl
from jax.experimental.pallas import tpu as pltpu
from jax.sharding import PartitionSpec as P

LANES = 128
VMEM_LIMIT = 20 * 2**20


def split_parts(values):
    parts = []
    for _ in range(3):
        part = lax.reduce_precision(values, exponent_bits=8, mantissa_bits=7)
        parts.append(part.astype(jnp.bfloat16))
        values = values - part
    return parts


def pack_gates(tokens, expert_ids, gate_probs, count):
    experts = jnp.arange(count, dtype=jnp.int32)
    chosen = expert_ids[:, None, :] == experts[None, :, None]
    weights = jnp.sum(jnp.where(chosen, gate_probs[:, None, :], 0.0), axis=2)
    parts = jnp.concatenate(split_parts(weights), axis=1)
    parts = jnp.pad(parts, ((0, 0), (0, -parts.shape[1] % LANES)))
    return jnp.concatenate([tokens, parts], axis=1)


def dot(a, b):
    return jnp.dot(a, b, preferred_element_type=jnp.float32)


def token_weight(tail, expert, count):
    lane = lax.broadcasted_iota(jnp.int32, tail.shape, 1)
    mine = (lane % count == expert) & (lane < 3 * count)
    return jnp.sum(jnp.where(mine, tail.astype(jnp.float32), 0.0), axis=1, keepdims=True)


def activate(gate, up):
    return (gate / (1.0 + jnp.exp(-gate)) * up).astype(jnp.bfloat16)


def rounded(value):
    return value.astype(jnp.bfloat16).astype(jnp.float32)


def near_kernel(count, placement, *refs):
    rows, weights, outs, x = refs[:2], (refs[2:5], refs[5:8]), refs[8:10], refs[10]
    height, width = rows[0].shape[0], x.shape[1]
    me = lax.axis_index("expert")
    for i in range(2):
        x[i * height : (i + 1) * height, :] = rows[i][:, :width]
    totals = [0.0, 0.0]
    for flip, (g, u, d) in enumerate(weights):
        hidden = activate(dot(x[...], g[...]), dot(x[...], u[...]))
        value = rounded(dot(hidden, d[...]))
        for i in range(2):
            weight = token_weight(rows[i][:, width:], placement[me ^ flip], count)
            totals[i] = totals[i] + value[i * height : (i + 1) * height, :] * weight
    for i in range(2):
        outs[i][...] = totals[i]


def hidden_kernel(blocks, width, *refs):
    rows, (own, other_gate, other_up), out, x = refs[:blocks], refs[blocks : blocks + 3], refs[-2], refs[-1]
    height = rows[0].shape[0]
    half = lax.axis_index("dp") % 2
    depth = own.shape[0] // 2
    at = pl.multiple_of(half * depth, depth)
    off = pl.multiple_of(depth - at, depth)
    for first in range(0, blocks, 2):
        for i in range(2):
            x[i * height : (i + 1) * height, :] = rows[first + i][:, :width]
        xa, xb = x[:, pl.ds(at, depth)], x[:, pl.ds(off, depth)]
        gate = dot(xa, own[:depth, :]) + dot(xb, other_gate[...])
        up = dot(xa, own[depth:, :]) + dot(xb, other_up[...])
        out[first * height : (first + 2) * height, :] = activate(gate, up)


def down_kernel(count, flips, blocks, half_flip, placement, *refs):
    number = len(blocks)
    rows, refs = refs[:number], refs[number:]
    experts, refs = refs[: 2 * len(flips)], refs[2 * len(flips) :]
    base, outs = refs[:number], refs[number:]
    height, part = outs[0].shape
    width = 2 * part
    me = lax.axis_index("expert")
    far = lax.axis_size("expert") // 2
    half = (lax.axis_index("dp") + half_flip) % 2
    columns = pl.ds(pl.multiple_of(half * part, part), part)
    for first in range(0, number, 2):
        pair = range(first, first + 2)
        totals = {i: base[i][...] if base[i].shape[1] == part else base[i][:, columns] for i in pair}
        for flip, hidden, down in zip(flips, experts[::2], experts[1::2]):
            span = slice(blocks[first] * height, (blocks[first] + 2) * height)
            value = rounded(dot(hidden[span, :], down[...]))
            for i in pair:
                weight = token_weight(rows[i][:, width:], placement[me ^ far ^ flip], count)
                at = (i - first) * height
                totals[i] = totals[i] + value[at : at + height, :] * weight
        for i in pair:
            outs[i][...] = totals[i].astype(outs[i].dtype)


def finish_kernel(ours, *refs):
    out = refs[-1]
    for flip, parts in ((0, refs[:ours]), (1, refs[ours:-1])):
        width = parts[0].shape[1]
        half = (lax.axis_index("dp") + flip) % 2
        total = parts[0][...]
        for part in parts[1:]:
            total = total + part[...].astype(jnp.float32)
        out[:, pl.ds(pl.multiple_of(half * width, width), width)] = total.astype(out.dtype)


def call(kernel, out_shape, args, scratch=(), scalars=0):
    vmem = pl.BlockSpec(memory_space=pltpu.VMEM)
    smem = pl.BlockSpec(memory_space=pltpu.SMEM)
    return pl.pallas_call(
        kernel,
        out_shape=out_shape,
        in_specs=[smem] * scalars + [vmem] * (len(args) - scalars),
        out_specs=jax.tree.map(lambda _: vmem, out_shape),
        scratch_shapes=list(scratch),
        compiler_params=pltpu.CompilerParams(vmem_limit_bytes=VMEM_LIMIT),
        cost_estimate=pl.CostEstimate(flops=0, bytes_accessed=0, transcendentals=0),
    )(*args)


def run_copies(copies, sems):
    copies = [pltpu.make_async_copy(a, b, sems.at[i]) for i, (a, b) in enumerate(copies)]
    for copy in copies:
        copy.start()
    for copy in copies:
        copy.wait()


def part_of(ref, axis, half, size):
    span = pl.ds(pl.multiple_of(half * size, size), size)
    return ref.at[span, :] if axis == 0 else ref.at[:, span]


def store_kernel(axis, first, flags, own, came, other, out, sems):
    half = lax.axis_index("dp") % 2
    size = out.shape[axis] // 2
    taken = flags[lax.axis_index("expert")] == 1

    @pl.when(taken)
    def _():
        if axis == 0:
            parts = [came.at[pl.ds(first, size), :], other]
        else:
            parts = [came, other]
        run_copies(
            [
                (parts[0], part_of(out, axis, half, size)),
                (parts[1], part_of(out, axis, 1 - half, size)),
            ],
            sems,
        )

    @pl.when(jnp.logical_not(taken))
    def _():
        run_copies([(own, out)], sems)


def store(axis, first, flags, own, came, other):
    vmem = pl.BlockSpec(memory_space=pltpu.VMEM)
    return pl.pallas_call(
        functools.partial(store_kernel, axis, first),
        out_shape=jax.ShapeDtypeStruct(own.shape, own.dtype),
        in_specs=[pl.BlockSpec(memory_space=pltpu.SMEM)] + [vmem] * 3,
        out_specs=pl.BlockSpec(memory_space=pl.ANY),
        scratch_shapes=[pltpu.SemaphoreType.DMA((2,))],
        compiler_params=pltpu.CompilerParams(vmem_limit_bytes=8 * 2**20),
        cost_estimate=pl.CostEstimate(flops=0, bytes_accessed=0, transcendentals=0),
    )(flags, own, came, other)


def after(value, *others):
    return lax.optimization_barrier((value, *others))[0]


def per_device(tokens, expert_ids, gate_probs, w_gate, w_up, w_down, placement, swap_flags):
    count = lax.axis_size("expert")
    couple = lax.axis_index("dp") % 2
    half_axis = count // 2
    height, width = tokens.shape
    own = (w_gate[0], w_up[0], w_down[0])
    ff = own[0].shape[1]
    trades = [(d, d ^ 1) for d in range(lax.axis_size("dp"))]

    def send(value, bit, name):
        with jax.named_scope(name):
            return lax.ppermute(value, "expert", [(d, d ^ bit) for d in range(count)])

    def trade(value):
        with jax.named_scope("trade"):
            return lax.ppermute(value, "dp", trades)

    depth, part = own[0].shape[0] // 2, width // 2

    def half_of(first, second):
        return jnp.where(couple == 0, first, second)

    upper = half_of(
        jnp.concatenate([own[0][:depth], own[1][:depth]], axis=0),
        jnp.concatenate([own[0][depth:], own[1][depth:]], axis=0),
    )
    lower = half_of(own[2][:, :part], own[2][:, part:])

    bits = []
    bit = half_axis // 2
    while bit > 1:
        bits.append(bit)
        bit //= 2
    blocks = {0: pack_gates(tokens, expert_ids, gate_probs, count)}
    masks = {0: 0}
    for stage, bit in enumerate(bits):
        for i in sorted(blocks):
            blocks[i | 1 << stage] = send(blocks[i], bit, "tokens")
            masks[i | 1 << stage] = masks[i] ^ bit
    rows = [blocks[i] for i in range(len(blocks))]

    z_upper = send(upper, half_axis, "swap")
    z_lower = send(after(lower, z_upper, *rows), half_axis, "swap")
    y_upper = [trade(after(w, *rows)) for w in (z_upper[:depth], z_upper[depth:])]
    near = [send(after(w, lower), 1, "near") for w in own]

    firsts = list(reversed(range(0, len(rows), 2)))
    scratch = [pltpu.VMEM((2 * height, width), jnp.bfloat16)]
    base = {}
    for first in firsts:
        base[first] = call(
            functools.partial(near_kernel, count),
            [jax.ShapeDtypeStruct((height, width), jnp.float32)] * 2,
            [placement, *rows[first : first + 2], *own, *near],
            scratch,
            scalars=1,
        )

    arrived = after(z_lower, base)
    y_lower = trade(arrived)
    z_near = [send(z_upper, 1, "z_near"), send(arrived, 1, "z_near")]
    y_near = [[send(after(w, arrived), 1, "y_near") for w in y_upper]]
    hidden = [
        call(
            functools.partial(hidden_kernel, len(rows), width),
            jax.ShapeDtypeStruct((len(rows) * height, ff), jnp.bfloat16),
            [*rows, own_part, *other_part],
            scratch,
        )
        for own_part, other_part in ((z_upper, y_upper), (z_near[0], y_near[0]))
    ]

    def far_sums(flips, downs, half_flip, blocks, sums, last):
        kinds = [jnp.bfloat16 if last and i > 0 else jnp.float32 for i in blocks]
        experts = [x for flip, down in zip(flips, downs) for x in (hidden[flip], down)]
        out = call(
            functools.partial(down_kernel, count, flips, blocks, half_flip),
            [jax.ShapeDtypeStruct((height, part), kind) for kind in kinds],
            [placement, *(rows[i] for i in blocks), *experts, *(sums[i] for i in blocks)],
            scalars=1,
        )
        return dict(zip(blocks, out))

    def collect(parts):
        return [parts[0]] + [send(parts[i], masks[i], "sums") for i in reversed(range(1, len(parts)))]

    near_sums = [x for first in reversed(firsts) for x in base[first]]
    parts = {}
    for first in firsts:
        parts |= far_sums((0, 1), [arrived, z_near[1]], 0, (first, first + 1), near_sums, True)
    flags = after(swap_flags, parts)
    stored = [
        store(0, 0, flags, own[0], z_upper, y_upper[0]),
        store(0, depth, flags, own[1], z_upper, y_upper[1]),
    ]
    ours = collect(parts)
    landed = after(y_lower, stored, ours[1:-1])
    y_near.append(send(landed, 1, "y_near"))
    everyone = tuple(range(len(rows)))
    last_sums = far_sums((0,), [landed], 1, everyone, near_sums, False)
    last_parts = {}
    for first in firsts:
        last_parts |= far_sums((1,), [y_near[1]], 1, (first, first + 1), last_sums, True)
    stored.append(store(1, 0, after(swap_flags, last_parts), own[2], z_lower, y_lower))
    others = collect(last_parts)
    mixed = call(
        functools.partial(finish_kernel, len(ours)),
        jax.ShapeDtypeStruct((height, width), tokens.dtype),
        [*ours, *others],
    )
    return (mixed, *(w[None] for w in stored))


def solution(mesh):
    in_specs = (
        P(("dp", "expert"), None),
        P(("dp", "expert"), None),
        P(("dp", "expert"), None),
        P("expert", None, None),
        P("expert", None, None),
        P("expert", None, None),
        P(),
        P(),
    )
    out_specs = (
        P(("dp", "expert"), None),
        P(("dp", "expert"), None, None),
        P(("dp", "expert"), None, None),
        P(("dp", "expert"), None, None),
    )
    return jax.shard_map(
        per_device, mesh=mesh, in_specs=in_specs, out_specs=out_specs, check_vma=False
    )
```

```python
import functools

import jax
import jax.numpy as jnp
from jax import lax
from jax.experimental import pallas as pl
from jax.experimental.pallas import tpu as pltpu
from jax.sharding import PartitionSpec as P

LANES = 128
VMEM_LIMIT = 20 * 2**20


def split_parts(values):
    parts = []
    for _ in range(3):
        part = lax.reduce_precision(values, exponent_bits=8, mantissa_bits=7)
        parts.append(part.astype(jnp.bfloat16))
        values = values - part
    return parts


def pack_gates(tokens, expert_ids, gate_probs, count):
    experts = jnp.arange(count, dtype=jnp.int32)
    chosen = expert_ids[:, None, :] == experts[None, :, None]
    weights = jnp.sum(jnp.where(chosen, gate_probs[:, None, :], 0.0), axis=2)
    parts = jnp.concatenate(split_parts(weights), axis=1)
    parts = jnp.pad(parts, ((0, 0), (0, -parts.shape[1] % LANES)))
    return jnp.concatenate([tokens, parts], axis=1)


def dot(a, b):
    return jnp.dot(a, b, preferred_element_type=jnp.float32)


def token_weight(tail, expert, count):
    lane = lax.broadcasted_iota(jnp.int32, tail.shape, 1)
    mine = (lane % count == expert) & (lane < 3 * count)
    return jnp.sum(jnp.where(mine, tail.astype(jnp.float32), 0.0), axis=1, keepdims=True)


def activate(gate, up):
    return (gate / (1.0 + jnp.exp(-gate)) * up).astype(jnp.bfloat16)


def rounded(value):
    return value.astype(jnp.bfloat16).astype(jnp.float32)


def near_kernel(count, placement, *refs):
    rows, weights, outs, x = refs[:2], (refs[2:5], refs[5:8]), refs[8:10], refs[10]
    height, width = rows[0].shape[0], x.shape[1]
    me = lax.axis_index("expert")
    for i in range(2):
        x[i * height : (i + 1) * height, :] = rows[i][:, :width]
    totals = [0.0, 0.0]
    for flip, (g, u, d) in enumerate(weights):
        hidden = activate(dot(x[...], g[...]), dot(x[...], u[...]))
        value = rounded(dot(hidden, d[...]))
        for i in range(2):
            weight = token_weight(rows[i][:, width:], placement[me ^ flip], count)
            totals[i] = totals[i] + value[i * height : (i + 1) * height, :] * weight
    for i in range(2):
        outs[i][...] = totals[i]


def hidden_kernel(blocks, width, *refs):
    rows, own, other, out, x = refs[:blocks], refs[blocks], refs[blocks + 1], refs[blocks + 2], refs[blocks + 3]
    height = rows[0].shape[0]
    half = lax.axis_index("dp") % 2
    depth = own.shape[0] // 2
    at = pl.multiple_of(half * depth, depth)
    off = pl.multiple_of(depth - at, depth)
    for first in range(0, blocks, 2):
        for i in range(2):
            x[i * height : (i + 1) * height, :] = rows[first + i][:, :width]
        xa, xb = x[:, pl.ds(at, depth)], x[:, pl.ds(off, depth)]
        gate = dot(xa, own[:depth, :]) + dot(xb, other[:depth, :])
        up = dot(xa, own[depth:, :]) + dot(xb, other[depth:, :])
        out[first * height : (first + 2) * height, :] = activate(gate, up)


def down_kernel(count, flips, blocks, half_flip, placement, *refs):
    number = len(blocks)
    rows, refs = refs[:number], refs[number:]
    experts, refs = refs[: 2 * len(flips)], refs[2 * len(flips) :]
    base, outs = refs[:number], refs[number:]
    height, part = outs[0].shape
    width = 2 * part
    me = lax.axis_index("expert")
    far = lax.axis_size("expert") // 2
    half = (lax.axis_index("dp") + half_flip) % 2
    columns = pl.ds(pl.multiple_of(half * part, part), part)
    for first in range(0, number, 2):
        pair = range(first, first + 2)
        totals = {i: base[i][...] if base[i].shape[1] == part else base[i][:, columns] for i in pair}
        for flip, hidden, down in zip(flips, experts[::2], experts[1::2]):
            spans = [slice(blocks[i] * height, (blocks[i] + 1) * height) for i in pair]
            units = jnp.concatenate([hidden[span, :] for span in spans], axis=0)
            value = rounded(dot(units, down[...]))
            for i in pair:
                weight = token_weight(rows[i][:, width:], placement[me ^ far ^ flip], count)
                at = (i - first) * height
                totals[i] = totals[i] + value[at : at + height, :] * weight
        for i in pair:
            outs[i][...] = totals[i].astype(outs[i].dtype)


def finish_kernel(ours, *refs):
    out = refs[-1]
    for flip, parts in ((0, refs[:ours]), (1, refs[ours:-1])):
        width = parts[0].shape[1]
        half = (lax.axis_index("dp") + flip) % 2
        total = parts[0][...]
        for part in parts[1:]:
            total = total + part[...].astype(jnp.float32)
        out[:, pl.ds(pl.multiple_of(half * width, width), width)] = total.astype(out.dtype)


def call(kernel, out_shape, args, scratch=(), scalars=0):
    vmem = pl.BlockSpec(memory_space=pltpu.VMEM)
    smem = pl.BlockSpec(memory_space=pltpu.SMEM)
    return pl.pallas_call(
        kernel,
        out_shape=out_shape,
        in_specs=[smem] * scalars + [vmem] * (len(args) - scalars),
        out_specs=jax.tree.map(lambda _: vmem, out_shape),
        scratch_shapes=list(scratch),
        compiler_params=pltpu.CompilerParams(vmem_limit_bytes=VMEM_LIMIT),
        cost_estimate=pl.CostEstimate(flops=0, bytes_accessed=0, transcendentals=0),
    )(*args)


def run_copies(copies, sems):
    copies = [pltpu.make_async_copy(a, b, sems.at[i]) for i, (a, b) in enumerate(copies)]
    for copy in copies:
        copy.start()
    for copy in copies:
        copy.wait()


def part_of(ref, axis, half, size):
    span = pl.ds(pl.multiple_of(half * size, size), size)
    return ref.at[span, :] if axis == 0 else ref.at[:, span]


def store_kernel(axis, first, flags, own, came, other, out, sems):
    half = lax.axis_index("dp") % 2
    size = out.shape[axis] // 2
    taken = flags[lax.axis_index("expert")] == 1

    @pl.when(taken)
    def _():
        if axis == 0:
            parts = [ref.at[pl.ds(first, size), :] for ref in (came, other)]
        else:
            parts = [came, other]
        run_copies(
            [
                (parts[0], part_of(out, axis, half, size)),
                (parts[1], part_of(out, axis, 1 - half, size)),
            ],
            sems,
        )

    @pl.when(jnp.logical_not(taken))
    def _():
        run_copies([(own, out)], sems)


def store(axis, first, flags, own, came, other):
    vmem = pl.BlockSpec(memory_space=pltpu.VMEM)
    return pl.pallas_call(
        functools.partial(store_kernel, axis, first),
        out_shape=jax.ShapeDtypeStruct(own.shape, own.dtype),
        in_specs=[pl.BlockSpec(memory_space=pltpu.SMEM)] + [vmem] * 3,
        out_specs=pl.BlockSpec(memory_space=pl.ANY),
        scratch_shapes=[pltpu.SemaphoreType.DMA((2,))],
        compiler_params=pltpu.CompilerParams(vmem_limit_bytes=8 * 2**20),
        cost_estimate=pl.CostEstimate(flops=0, bytes_accessed=0, transcendentals=0),
    )(flags, own, came, other)


def after(value, *others):
    return lax.optimization_barrier((value, *others))[0]


def per_device(tokens, expert_ids, gate_probs, w_gate, w_up, w_down, placement, swap_flags):
    count = lax.axis_size("expert")
    couple = lax.axis_index("dp") % 2
    half_axis = count // 2
    height, width = tokens.shape
    own = (w_gate[0], w_up[0], w_down[0])
    ff = own[0].shape[1]
    trades = [(d, d ^ 1) for d in range(lax.axis_size("dp"))]

    def send(value, bit, name):
        with jax.named_scope(name):
            return lax.ppermute(value, "expert", [(d, d ^ bit) for d in range(count)])

    def trade(value):
        with jax.named_scope("trade"):
            return lax.ppermute(value, "dp", trades)

    depth, part = own[0].shape[0] // 2, width // 2

    def half_of(first, second):
        return jnp.where(couple == 0, first, second)

    upper = half_of(
        jnp.concatenate([own[0][:depth], own[1][:depth]], axis=0),
        jnp.concatenate([own[0][depth:], own[1][depth:]], axis=0),
    )
    lower = half_of(own[2][:, :part], own[2][:, part:])

    bits = []
    bit = half_axis // 2
    while bit > 1:
        bits.append(bit)
        bit //= 2
    blocks = {0: pack_gates(tokens, expert_ids, gate_probs, count)}
    masks = {0: 0}
    for stage, bit in enumerate(bits):
        for i in sorted(blocks):
            blocks[i | 1 << stage] = send(blocks[i], bit, "tokens")
            masks[i | 1 << stage] = masks[i] ^ bit
    rows = [blocks[i] for i in range(len(blocks))]

    z_upper = send(upper, half_axis, "swap")
    z_lower = send(after(lower, z_upper, *rows), half_axis, "swap")
    y_upper = trade(after(z_upper, *rows))
    near = [send(after(w, lower), 1, "near") for w in own]

    firsts = list(reversed(range(0, len(rows), 2)))
    scratch = [pltpu.VMEM((2 * height, width), jnp.bfloat16)]
    base = {}
    for first in firsts:
        base[first] = call(
            functools.partial(near_kernel, count),
            [jax.ShapeDtypeStruct((height, width), jnp.float32)] * 2,
            [placement, *rows[first : first + 2], *own, *near],
            scratch,
            scalars=1,
        )

    arrived = after(z_lower, base)
    y_lower = trade(arrived)
    z_near = [send(z_upper, 1, "z_near"), send(arrived, 1, "z_near")]
    y_near = [send(after(y_upper, arrived), 1, "y_near")]
    hidden = [
        call(
            functools.partial(hidden_kernel, len(rows), width),
            jax.ShapeDtypeStruct((len(rows) * height, ff), jnp.bfloat16),
            [*rows, own_part, other_part],
            scratch,
        )
        for own_part, other_part in ((z_upper, y_upper), (z_near[0], y_near[0]))
    ]

    def far_sums(flips, downs, half_flip, blocks, sums, last):
        kinds = [jnp.bfloat16 if last and i > 0 else jnp.float32 for i in blocks]
        experts = [x for flip, down in zip(flips, downs) for x in (hidden[flip], down)]
        out = call(
            functools.partial(down_kernel, count, flips, blocks, half_flip),
            [jax.ShapeDtypeStruct((height, part), kind) for kind in kinds],
            [placement, *(rows[i] for i in blocks), *experts, *(sums[i] for i in blocks)],
            scalars=1,
        )
        return dict(zip(blocks, out))

    pairs = [(i, i + len(rows) // 2) for i in reversed(range(len(rows) // 2))]
    order = [i for pair in pairs for i in reversed(pair) if i > 0]

    def collect(parts):
        return [parts[0]] + [send(parts[i], masks[i], "sums") for i in order]

    near_sums = [x for first in reversed(firsts) for x in base[first]]
    parts = {}
    for pair in pairs:
        parts |= far_sums((0, 1), [arrived, z_near[1]], 0, pair, near_sums, True)
    flags = after(swap_flags, parts)
    stored = [
        store(0, 0, flags, own[0], z_upper, y_upper),
        store(0, depth, flags, own[1], z_upper, y_upper),
    ]
    ours = collect(parts)
    landed = after(y_lower, stored, ours[1:-1])
    y_near.append(send(landed, 1, "y_near"))
    everyone = tuple(range(len(rows)))
    last_sums = far_sums((0,), [landed], 1, everyone, near_sums, False)
    last_parts = {}
    for pair in pairs:
        last_parts |= far_sums((1,), [y_near[1]], 1, pair, last_sums, True)
    stored.append(store(1, 0, after(swap_flags, last_parts), own[2], z_lower, y_lower))
    others = collect(last_parts)
    mixed = call(
        functools.partial(finish_kernel, len(ours)),
        jax.ShapeDtypeStruct((height, width), tokens.dtype),
        [*ours, *others],
    )
    return (mixed, *(w[None] for w in stored))


def solution(mesh):
    in_specs = (
        P(("dp", "expert"), None),
        P(("dp", "expert"), None),
        P(("dp", "expert"), None),
        P("expert", None, None),
        P("expert", None, None),
        P("expert", None, None),
        P(),
        P(),
    )
    out_specs = (
        P(("dp", "expert"), None),
        P(("dp", "expert"), None, None),
        P(("dp", "expert"), None, None),
        P(("dp", "expert"), None, None),
    )
    return jax.shard_map(
        per_device, mesh=mesh, in_specs=in_specs, out_specs=out_specs, check_vma=False
    )
```

```python
import functools

import jax
import jax.numpy as jnp
from jax import lax
from jax.experimental import pallas as pl
from jax.experimental.pallas import tpu as pltpu
from jax.sharding import PartitionSpec as P

LANES = 128
VMEM_LIMIT = 20 * 2**20


def split_parts(values):
    parts = []
    for _ in range(3):
        part = lax.reduce_precision(values, exponent_bits=8, mantissa_bits=7)
        parts.append(part.astype(jnp.bfloat16))
        values = values - part
    return parts


def pack_gates(tokens, expert_ids, gate_probs, count):
    experts = jnp.arange(count, dtype=jnp.int32)
    chosen = expert_ids[:, None, :] == experts[None, :, None]
    weights = jnp.sum(jnp.where(chosen, gate_probs[:, None, :], 0.0), axis=2)
    parts = jnp.concatenate(split_parts(weights), axis=1)
    parts = jnp.pad(parts, ((0, 0), (0, -parts.shape[1] % LANES)))
    return jnp.concatenate([tokens, parts], axis=1)


def dot(a, b):
    return jnp.dot(a, b, preferred_element_type=jnp.float32)


def token_weight(tail, expert, count):
    lane = lax.broadcasted_iota(jnp.int32, tail.shape, 1)
    mine = (lane % count == expert) & (lane < 3 * count)
    return jnp.sum(jnp.where(mine, tail.astype(jnp.float32), 0.0), axis=1, keepdims=True)


def activate(gate, up):
    return (gate / (1.0 + jnp.exp(-gate)) * up).astype(jnp.bfloat16)


def rounded(value):
    return value.astype(jnp.bfloat16).astype(jnp.float32)


def near_kernel(count, placement, *refs):
    rows, weights, outs, x = refs[:2], (refs[2:5], refs[5:8]), refs[8:10], refs[10]
    height, width = rows[0].shape[0], x.shape[1]
    me = lax.axis_index("expert")
    for i in range(2):
        x[i * height : (i + 1) * height, :] = rows[i][:, :width]
    totals = [0.0, 0.0]
    for flip, (g, u, d) in enumerate(weights):
        hidden = activate(dot(x[...], g[...]), dot(x[...], u[...]))
        value = rounded(dot(hidden, d[...]))
        for i in range(2):
            weight = token_weight(rows[i][:, width:], placement[me ^ flip], count)
            totals[i] = totals[i] + value[i * height : (i + 1) * height, :] * weight
    for i in range(2):
        outs[i][...] = totals[i]


def hidden_kernel(blocks, width, *refs):
    rows, own, other, out, x = refs[:blocks], refs[blocks], refs[blocks + 1], refs[blocks + 2], refs[blocks + 3]
    height = rows[0].shape[0]
    half = lax.axis_index("dp") % 2
    depth = own.shape[0] // 2
    at = pl.multiple_of(half * depth, depth)
    off = pl.multiple_of(depth - at, depth)
    for first in range(0, blocks, 2):
        for i in range(2):
            x[i * height : (i + 1) * height, :] = rows[first + i][:, :width]
        xa, xb = x[:, pl.ds(at, depth)], x[:, pl.ds(off, depth)]
        gate = dot(xa, own[:depth, :]) + dot(xb, other[:depth, :])
        up = dot(xa, own[depth:, :]) + dot(xb, other[depth:, :])
        out[first * height : (first + 2) * height, :] = activate(gate, up)


def down_kernel(count, flips, blocks, half_flip, placement, *refs):
    number = len(blocks)
    rows, refs = refs[:number], refs[number:]
    experts, refs = refs[: 2 * len(flips)], refs[2 * len(flips) :]
    base, outs = refs[:number], refs[number:]
    height, part = outs[0].shape
    width = 2 * part
    me = lax.axis_index("expert")
    far = lax.axis_size("expert") // 2
    half = (lax.axis_index("dp") + half_flip) % 2
    columns = pl.ds(pl.multiple_of(half * part, part), part)
    for first in range(0, number, 2):
        pair = range(first, first + 2)
        totals = {i: base[i][...] if base[i].shape[1] == part else base[i][:, columns] for i in pair}
        for flip, hidden, down in zip(flips, experts[::2], experts[1::2]):
            spans = [slice(blocks[i] * height, (blocks[i] + 1) * height) for i in pair]
            units = jnp.concatenate([hidden[span, :] for span in spans], axis=0)
            value = rounded(dot(units, down[...]))
            for i in pair:
                weight = token_weight(rows[i][:, width:], placement[me ^ far ^ flip], count)
                at = (i - first) * height
                totals[i] = totals[i] + value[at : at + height, :] * weight
        for i in pair:
            outs[i][...] = totals[i].astype(outs[i].dtype)


def finish_kernel(ours, *refs):
    out = refs[-1]
    for flip, parts in ((0, refs[:ours]), (1, refs[ours:-1])):
        width = parts[0].shape[1]
        half = (lax.axis_index("dp") + flip) % 2
        total = parts[0][...]
        for part in parts[1:]:
            total = total + part[...].astype(jnp.float32)
        out[:, pl.ds(pl.multiple_of(half * width, width), width)] = total.astype(out.dtype)


def call(kernel, out_shape, args, scratch=(), scalars=0):
    vmem = pl.BlockSpec(memory_space=pltpu.VMEM)
    smem = pl.BlockSpec(memory_space=pltpu.SMEM)
    return pl.pallas_call(
        kernel,
        out_shape=out_shape,
        in_specs=[smem] * scalars + [vmem] * (len(args) - scalars),
        out_specs=jax.tree.map(lambda _: vmem, out_shape),
        scratch_shapes=list(scratch),
        compiler_params=pltpu.CompilerParams(vmem_limit_bytes=VMEM_LIMIT),
        cost_estimate=pl.CostEstimate(flops=0, bytes_accessed=0, transcendentals=0),
    )(*args)


def run_copies(copies, sems):
    copies = [pltpu.make_async_copy(a, b, sems.at[i]) for i, (a, b) in enumerate(copies)]
    for copy in copies:
        copy.start()
    for copy in copies:
        copy.wait()


def part_of(ref, axis, half, size):
    span = pl.ds(pl.multiple_of(half * size, size), size)
    return ref.at[span, :] if axis == 0 else ref.at[:, span]


def store_kernel(axis, first, flags, own, came, other, out, sems):
    half = lax.axis_index("dp") % 2
    size = out.shape[axis] // 2
    taken = flags[lax.axis_index("expert")] == 1

    @pl.when(taken)
    def _():
        if axis == 0:
            parts = [ref.at[pl.ds(first, size), :] for ref in (came, other)]
        else:
            parts = [came, other]
        run_copies(
            [
                (parts[0], part_of(out, axis, half, size)),
                (parts[1], part_of(out, axis, 1 - half, size)),
            ],
            sems,
        )

    @pl.when(jnp.logical_not(taken))
    def _():
        run_copies([(own, out)], sems)


def store(axis, first, flags, own, came, other):
    vmem = pl.BlockSpec(memory_space=pltpu.VMEM)
    return pl.pallas_call(
        functools.partial(store_kernel, axis, first),
        out_shape=jax.ShapeDtypeStruct(own.shape, own.dtype),
        in_specs=[pl.BlockSpec(memory_space=pltpu.SMEM)] + [vmem] * 3,
        out_specs=pl.BlockSpec(memory_space=pl.ANY),
        scratch_shapes=[pltpu.SemaphoreType.DMA((2,))],
        compiler_params=pltpu.CompilerParams(vmem_limit_bytes=8 * 2**20),
        cost_estimate=pl.CostEstimate(flops=0, bytes_accessed=0, transcendentals=0),
    )(flags, own, came, other)


def after(value, *others):
    return lax.optimization_barrier((value, *others))[0]


def per_device(tokens, expert_ids, gate_probs, w_gate, w_up, w_down, placement, swap_flags):
    count = lax.axis_size("expert")
    couple = lax.axis_index("dp") % 2
    half_axis = count // 2
    height, width = tokens.shape
    own = (w_gate[0], w_up[0], w_down[0])
    ff = own[0].shape[1]
    trades = [(d, d ^ 1) for d in range(lax.axis_size("dp"))]

    def send(value, bit, name):
        with jax.named_scope(name):
            return lax.ppermute(value, "expert", [(d, d ^ bit) for d in range(count)])

    def trade(value):
        with jax.named_scope("trade"):
            return lax.ppermute(value, "dp", trades)

    depth, part = own[0].shape[0] // 2, width // 2

    def half_of(first, second):
        return jnp.where(couple == 0, first, second)

    upper = half_of(
        jnp.concatenate([own[0][:depth], own[1][:depth]], axis=0),
        jnp.concatenate([own[0][depth:], own[1][depth:]], axis=0),
    )
    lower = half_of(own[2][:, :part], own[2][:, part:])

    bits = []
    bit = half_axis // 2
    while bit > 1:
        bits.append(bit)
        bit //= 2
    blocks = {0: pack_gates(tokens, expert_ids, gate_probs, count)}
    masks = {0: 0}
    for stage, bit in enumerate(bits):
        for i in sorted(blocks):
            blocks[i | 1 << stage] = send(blocks[i], bit, "tokens")
            masks[i | 1 << stage] = masks[i] ^ bit
    rows = [blocks[i] for i in range(len(blocks))]

    z_upper = send(upper, half_axis, "swap")
    z_lower = send(after(lower, z_upper, *rows), half_axis, "swap")
    y_upper = trade(after(z_upper, *rows))
    near = [send(after(w, lower), 1, "near") for w in own]

    firsts = list(reversed(range(0, len(rows), 2)))
    scratch = [pltpu.VMEM((2 * height, width), jnp.bfloat16)]
    base = {}
    for first in firsts:
        base[first] = call(
            functools.partial(near_kernel, count),
            [jax.ShapeDtypeStruct((height, width), jnp.float32)] * 2,
            [placement, *rows[first : first + 2], *own, *near],
            scratch,
            scalars=1,
        )

    def hidden_units(*halves):
        return call(
            functools.partial(hidden_kernel, len(rows), width),
            jax.ShapeDtypeStruct((len(rows) * height, ff), jnp.bfloat16),
            [*rows, *halves],
            scratch,
        )

    hidden = [hidden_units(z_upper, y_upper)]
    arrived = after(z_lower, base, hidden[0])
    y_lower = trade(arrived)
    z_near = [send(z_upper, 1, "z_near"), send(arrived, 1, "z_near")]
    y_near = [send(after(y_upper, arrived), 1, "y_near")]
    hidden.append(hidden_units(z_near[0], y_near[0]))

    def far_sums(flips, downs, half_flip, blocks, sums, last):
        kinds = [jnp.bfloat16 if last and i > 0 else jnp.float32 for i in blocks]
        experts = [x for flip, down in zip(flips, downs) for x in (hidden[flip], down)]
        out = call(
            functools.partial(down_kernel, count, flips, blocks, half_flip),
            [jax.ShapeDtypeStruct((height, part), kind) for kind in kinds],
            [placement, *(rows[i] for i in blocks), *experts, *(sums[i] for i in blocks)],
            scalars=1,
        )
        return dict(zip(blocks, out))

    pairs = [(i, i + len(rows) // 2) for i in reversed(range(len(rows) // 2))]
    order = [i for pair in pairs for i in reversed(pair) if i > 0]

    def collect(parts):
        return [parts[0]] + [send(parts[i], masks[i], "sums") for i in order]

    near_sums = [x for first in reversed(firsts) for x in base[first]]
    parts = {}
    for pair in pairs:
        parts |= far_sums((0, 1), [arrived, z_near[1]], 0, pair, near_sums, True)
    flags = after(swap_flags, parts)
    stored = [
        store(0, 0, flags, own[0], z_upper, y_upper),
        store(0, depth, flags, own[1], z_upper, y_upper),
    ]
    ours = collect(parts)
    landed = after(y_lower, stored, ours[1:-1])
    y_near.append(send(landed, 1, "y_near"))
    everyone = tuple(range(len(rows)))
    last_sums = far_sums((0,), [landed], 1, everyone, near_sums, False)
    last_parts = {}
    for pair in pairs:
        last_parts |= far_sums((1,), [y_near[1]], 1, pair, last_sums, True)
    stored.append(store(1, 0, after(swap_flags, last_parts), own[2], z_lower, y_lower))
    others = collect(last_parts)
    mixed = call(
        functools.partial(finish_kernel, len(ours)),
        jax.ShapeDtypeStruct((height, width), tokens.dtype),
        [*ours, *others],
    )
    return (mixed, *(w[None] for w in stored))


def solution(mesh):
    in_specs = (
        P(("dp", "expert"), None),
        P(("dp", "expert"), None),
        P(("dp", "expert"), None),
        P("expert", None, None),
        P("expert", None, None),
        P("expert", None, None),
        P(),
        P(),
    )
    out_specs = (
        P(("dp", "expert"), None),
        P(("dp", "expert"), None, None),
        P(("dp", "expert"), None, None),
        P(("dp", "expert"), None, None),
    )
    return jax.shard_map(
        per_device, mesh=mesh, in_specs=in_specs, out_specs=out_specs, check_vma=False
    )
```

```python
import functools

import jax
import jax.numpy as jnp
from jax import lax
from jax.experimental import pallas as pl
from jax.experimental.pallas import tpu as pltpu
from jax.sharding import PartitionSpec as P

LANES = 128
VMEM_LIMIT = 20 * 2**20


def split_parts(values):
    parts = []
    for _ in range(3):
        part = lax.reduce_precision(values, exponent_bits=8, mantissa_bits=7)
        parts.append(part.astype(jnp.bfloat16))
        values = values - part
    return parts


def pack_gates(tokens, expert_ids, gate_probs, count):
    experts = jnp.arange(count, dtype=jnp.int32)
    chosen = expert_ids[:, None, :] == experts[None, :, None]
    weights = jnp.sum(jnp.where(chosen, gate_probs[:, None, :], 0.0), axis=2)
    parts = jnp.concatenate(split_parts(weights), axis=1)
    parts = jnp.pad(parts, ((0, 0), (0, -parts.shape[1] % LANES)))
    return jnp.concatenate([tokens, parts], axis=1)


def dot(a, b):
    return jnp.dot(a, b, preferred_element_type=jnp.float32)


def token_weight(tail, expert, count):
    lane = lax.broadcasted_iota(jnp.int32, tail.shape, 1)
    mine = (lane % count == expert) & (lane < 3 * count)
    return jnp.sum(jnp.where(mine, tail.astype(jnp.float32), 0.0), axis=1, keepdims=True)


def activate(gate, up):
    return (gate / (1.0 + jnp.exp(-gate)) * up).astype(jnp.bfloat16)


def rounded(value):
    return value.astype(jnp.bfloat16).astype(jnp.float32)


def near_kernel(count, placement, *refs):
    rows, weights, outs, x = refs[:2], (refs[2:5], refs[5:8]), refs[8:10], refs[10]
    height, width = rows[0].shape[0], x.shape[1]
    me = lax.axis_index("expert")
    for i in range(2):
        x[i * height : (i + 1) * height, :] = rows[i][:, :width]
    totals = [0.0, 0.0]
    for flip, (g, u, d) in enumerate(weights):
        hidden = activate(dot(x[...], g[...]), dot(x[...], u[...]))
        value = rounded(dot(hidden, d[...]))
        for i in range(2):
            weight = token_weight(rows[i][:, width:], placement[me ^ flip], count)
            totals[i] = totals[i] + value[i * height : (i + 1) * height, :] * weight
    for i in range(2):
        outs[i][...] = totals[i]


def hidden_kernel(blocks, width, *refs):
    rows, own, other, out, x = refs[:blocks], refs[blocks], refs[blocks + 1], refs[blocks + 2], refs[blocks + 3]
    height = rows[0].shape[0]
    half = lax.axis_index("dp") % 2
    depth = own.shape[0] // 2
    at = pl.multiple_of(half * depth, depth)
    off = pl.multiple_of(depth - at, depth)
    for first in range(0, blocks, 2):
        for i in range(2):
            x[i * height : (i + 1) * height, :] = rows[first + i][:, :width]
        xa, xb = x[:, pl.ds(at, depth)], x[:, pl.ds(off, depth)]
        gate = dot(xa, own[:depth, :]) + dot(xb, other[:depth, :])
        up = dot(xa, own[depth:, :]) + dot(xb, other[depth:, :])
        out[first * height : (first + 2) * height, :] = activate(gate, up)


def down_kernel(count, flips, blocks, half_flip, placement, *refs):
    number = len(blocks)
    rows, refs = refs[:number], refs[number:]
    experts, refs = refs[: 2 * len(flips)], refs[2 * len(flips) :]
    base, outs = refs[:number], refs[number:]
    height, part = outs[0].shape
    width = 2 * part
    me = lax.axis_index("expert")
    far = lax.axis_size("expert") // 2
    half = (lax.axis_index("dp") + half_flip) % 2
    columns = pl.ds(pl.multiple_of(half * part, part), part)
    for first in range(0, number, 2):
        pair = range(first, first + 2)
        totals = {i: base[i][...] if base[i].shape[1] == part else base[i][:, columns] for i in pair}
        for flip, hidden, down in zip(flips, experts[::2], experts[1::2]):
            spans = [slice(blocks[i] * height, (blocks[i] + 1) * height) for i in pair]
            units = jnp.concatenate([hidden[span, :] for span in spans], axis=0)
            value = rounded(dot(units, down[...]))
            for i in pair:
                weight = token_weight(rows[i][:, width:], placement[me ^ far ^ flip], count)
                at = (i - first) * height
                totals[i] = totals[i] + value[at : at + height, :] * weight
        for i in pair:
            outs[i][...] = totals[i].astype(outs[i].dtype)


def finish_kernel(ours, *refs):
    out = refs[-1]
    for flip, parts in ((0, refs[:ours]), (1, refs[ours:-1])):
        width = parts[0].shape[1]
        half = (lax.axis_index("dp") + flip) % 2
        total = parts[0][...]
        for part in parts[1:]:
            total = total + part[...].astype(jnp.float32)
        out[:, pl.ds(pl.multiple_of(half * width, width), width)] = total.astype(out.dtype)


def call(kernel, out_shape, args, scratch=(), scalars=0):
    vmem = pl.BlockSpec(memory_space=pltpu.VMEM)
    smem = pl.BlockSpec(memory_space=pltpu.SMEM)
    return pl.pallas_call(
        kernel,
        out_shape=out_shape,
        in_specs=[smem] * scalars + [vmem] * (len(args) - scalars),
        out_specs=jax.tree.map(lambda _: vmem, out_shape),
        scratch_shapes=list(scratch),
        compiler_params=pltpu.CompilerParams(vmem_limit_bytes=VMEM_LIMIT),
        cost_estimate=pl.CostEstimate(flops=0, bytes_accessed=0, transcendentals=0),
    )(*args)


def run_copies(copies, sems):
    copies = [pltpu.make_async_copy(a, b, sems.at[i]) for i, (a, b) in enumerate(copies)]
    for copy in copies:
        copy.start()
    for copy in copies:
        copy.wait()


def part_of(ref, axis, half, size):
    span = pl.ds(pl.multiple_of(half * size, size), size)
    return ref.at[span, :] if axis == 0 else ref.at[:, span]


def store_kernel(axis, first, flags, own, came, other, out, sems):
    half = lax.axis_index("dp") % 2
    size = out.shape[axis] // 2
    taken = flags[lax.axis_index("expert")] == 1

    @pl.when(taken)
    def _():
        if axis == 0:
            parts = [ref.at[pl.ds(first, size), :] for ref in (came, other)]
        else:
            parts = [came, other]
        run_copies(
            [
                (parts[0], part_of(out, axis, half, size)),
                (parts[1], part_of(out, axis, 1 - half, size)),
            ],
            sems,
        )

    @pl.when(jnp.logical_not(taken))
    def _():
        run_copies([(own, out)], sems)


def store(axis, first, flags, own, came, other):
    vmem = pl.BlockSpec(memory_space=pltpu.VMEM)
    return pl.pallas_call(
        functools.partial(store_kernel, axis, first),
        out_shape=jax.ShapeDtypeStruct(own.shape, own.dtype),
        in_specs=[pl.BlockSpec(memory_space=pltpu.SMEM)] + [vmem] * 3,
        out_specs=pl.BlockSpec(memory_space=pl.ANY),
        scratch_shapes=[pltpu.SemaphoreType.DMA((2,))],
        compiler_params=pltpu.CompilerParams(vmem_limit_bytes=8 * 2**20),
        cost_estimate=pl.CostEstimate(flops=0, bytes_accessed=0, transcendentals=0),
    )(flags, own, came, other)


def after(value, *others):
    return lax.optimization_barrier((value, *others))[0]


def per_device(tokens, expert_ids, gate_probs, w_gate, w_up, w_down, placement, swap_flags):
    count = lax.axis_size("expert")
    couple = lax.axis_index("dp") % 2
    half_axis = count // 2
    height, width = tokens.shape
    own = (w_gate[0], w_up[0], w_down[0])
    ff = own[0].shape[1]
    trades = [(d, d ^ 1) for d in range(lax.axis_size("dp"))]

    def send(value, bit, name):
        with jax.named_scope(name):
            return lax.ppermute(value, "expert", [(d, d ^ bit) for d in range(count)])

    def trade(value):
        with jax.named_scope("trade"):
            return lax.ppermute(value, "dp", trades)

    depth, part = own[0].shape[0] // 2, width // 2

    def half_of(first, second):
        return jnp.where(couple == 0, first, second)

    upper = half_of(
        jnp.concatenate([own[0][:depth], own[1][:depth]], axis=0),
        jnp.concatenate([own[0][depth:], own[1][depth:]], axis=0),
    )
    lower = half_of(own[2][:, :part], own[2][:, part:])

    bits = []
    bit = half_axis // 2
    while bit > 1:
        bits.append(bit)
        bit //= 2
    blocks = {0: pack_gates(tokens, expert_ids, gate_probs, count)}
    masks = {0: 0}
    for stage, bit in enumerate(bits):
        for i in sorted(blocks):
            blocks[i | 1 << stage] = send(blocks[i], bit, "tokens")
            masks[i | 1 << stage] = masks[i] ^ bit
    rows = [blocks[i] for i in range(len(blocks))]

    z_upper = send(upper, half_axis, "swap")
    z_lower = send(after(lower, z_upper, *rows), half_axis, "swap")
    y_upper = trade(after(z_upper, *rows))
    near = [send(after(w, lower), 1, "near") for w in own]

    firsts = list(reversed(range(0, len(rows), 2)))
    scratch = [pltpu.VMEM((2 * height, width), jnp.bfloat16)]
    base = {}
    for first in firsts:
        base[first] = call(
            functools.partial(near_kernel, count),
            [jax.ShapeDtypeStruct((height, width), jnp.float32)] * 2,
            [placement, *rows[first : first + 2], *own, *near],
            scratch,
            scalars=1,
        )

    arrived = after(z_lower, base)
    y_lower = trade(arrived)
    z_near = [send(z_upper, 1, "z_near"), send(arrived, 1, "z_near")]
    y_near = [send(after(y_upper, arrived), 1, "y_near")]
    hidden = [
        call(
            functools.partial(hidden_kernel, len(rows), width),
            jax.ShapeDtypeStruct((len(rows) * height, ff), jnp.bfloat16),
            [*rows, own_part, other_part],
            scratch,
        )
        for own_part, other_part in ((z_upper, y_upper), (z_near[0], y_near[0]))
    ]

    def far_sums(flips, downs, half_flip, blocks, sums, last):
        kinds = [jnp.bfloat16 if last and i > 0 else jnp.float32 for i in blocks]
        experts = [x for flip, down in zip(flips, downs) for x in (hidden[flip], down)]
        out = call(
            functools.partial(down_kernel, count, flips, blocks, half_flip),
            [jax.ShapeDtypeStruct((height, part), kind) for kind in kinds],
            [placement, *(rows[i] for i in blocks), *experts, *(sums[i] for i in blocks)],
            scalars=1,
        )
        return dict(zip(blocks, out))

    pairs = [(i, i + len(rows) // 2) for i in reversed(range(len(rows) // 2))]
    order = [i for pair in pairs for i in reversed(pair) if i > 0]

    def collect(parts):
        return [parts[0]] + [send(parts[i], masks[i], "sums") for i in order]

    near_sums = [x for first in reversed(firsts) for x in base[first]]
    parts = {}
    for pair in pairs:
        parts |= far_sums((0, 1), [arrived, z_near[1]], 0, pair, near_sums, True)
    flags = after(swap_flags, parts)
    stored = [
        store(0, 0, flags, own[0], z_upper, y_upper),
        store(0, depth, flags, own[1], z_upper, y_upper),
    ]
    ours = collect(parts)
    landed = after(y_lower, stored, ours[1 : len(ours) // 2])
    y_near.append(send(landed, 1, "y_near"))
    everyone = tuple(range(len(rows)))
    last_sums = far_sums((0,), [landed], 1, everyone, near_sums, False)
    last_parts = {}
    for pair in pairs:
        last_parts |= far_sums((1,), [y_near[1]], 1, pair, last_sums, True)
    stored.append(store(1, 0, after(swap_flags, last_parts), own[2], z_lower, y_lower))
    others = collect(last_parts)
    mixed = call(
        functools.partial(finish_kernel, len(ours)),
        jax.ShapeDtypeStruct((height, width), tokens.dtype),
        [*ours, *others],
    )
    return (mixed, *(w[None] for w in stored))


def solution(mesh):
    in_specs = (
        P(("dp", "expert"), None),
        P(("dp", "expert"), None),
        P(("dp", "expert"), None),
        P("expert", None, None),
        P("expert", None, None),
        P("expert", None, None),
        P(),
        P(),
    )
    out_specs = (
        P(("dp", "expert"), None),
        P(("dp", "expert"), None, None),
        P(("dp", "expert"), None, None),
        P(("dp", "expert"), None, None),
    )
    return jax.shard_map(
        per_device, mesh=mesh, in_specs=in_specs, out_specs=out_specs, check_vma=False
    )
```
